128 devices in a mesh: wide: 16 (over x, y_hi, core), narrow: 8 (over z, y_lo).
Axes of the slice: x: 4, y: 4 (y_hi: 2, y_lo: 2; y = y_hi * 2 + y_lo), z: 4, core: 2. Of those that a mesh axis runs over, the one named last changes fastest.
Arguments:
- tokens: bfloat16 [65536, 768], P(('wide', 'narrow')), may hold values from -6 to 6
- seq_lengths: int32 [128, 2], P(('wide', 'narrow')), may hold values from 1 to 384, 512 in all within a row
- key_mask: int32 [65536], P(('wide', 'narrow')), may hold values 0 or 1
- routes: int32 [65536, 2], P(('wide', 'narrow')), may hold values from 0 to 15, all different within a row
- cotangent: bfloat16 [65536, 768], P(('wide', 'narrow')), may hold values from -6 to 6
- qkv_weight: float32 [768, 2304], P(('wide', 'narrow')), may hold values from -0.21875 to 0.21875
- out_weight: float32 [768, 768], P(('wide', 'narrow')), may hold values from -0.875 to 0.875
- router_weight: float32 [768, 16], P(('wide', 'narrow')), may hold values from -0.15625 to 0.15625
- norm_gains: float32 [2, 768], P(None, ('wide', 'narrow')), may hold values from 0.5 to 1.5
- norm_biases: float32 [2, 768], P(None, ('wide', 'narrow')), may hold values from -1.8 to 1.8
- up_train: float32 [8, 768, 3072], P('narrow', 'wide'), may hold values from -0.21875 to 0.21875
- down_train: float32 [8, 3072, 768], P('narrow', 'wide'), may hold values from -0.109375 to 0.109375
- up_frozen: bfloat16 [8, 768, 3072], P('narrow', 'wide'), may hold values from -0.21875 to 0.21875
- down_frozen: bfloat16 [8, 3072, 768], P('narrow', 'wide'), may hold values from -0.109375 to 0.109375
Outputs:
- block_out: bfloat16 [65536, 768], P(('wide', 'narrow'))
- input_grad: float32 [65536, 768], P(('wide', 'narrow'))
- grad_qkv: float32 [768, 2304], P(('wide', 'narrow'))
- grad_out: float32 [768, 768], P(('wide', 'narrow'))
- grad_router: float32 [768, 16], P(('wide', 'narrow'))
- grad_gains: float32 [2, 768], P(None, ('wide', 'narrow'))
- grad_biases: float32 [2, 768], P(None, ('wide', 'narrow'))
- grad_up: float32 [8, 768, 3072], P('narrow', 'wide')
- grad_down: float32 [8, 3072, 768], P('narrow', 'wide')
The draws below stay inside these ranges and needn't reach their ends.
Inputs may be any that keep to these rules, and one draw needn't show every extreme that they name: `seq_lengths`: the 2 lengths of a row add up to 512; no length exceeds 384. `routes`: the 2 experts of a token differ.
All inputs are finite; a program needn't handle non-finite values. No bound on the sum of `key_mask` on one device may be relied on, other than what follows from the above.
Results may differ from the reference program's by a relative error of at most 0.015.
Values may be sent and summed in bfloat16 or wider, within the bound.
No kernel may reach another device: no remote copies, remote signals or barrier semaphores. Data moves between devices by JAX's collectives and lax.ppermute only.
A program may use at most 256 MiB of HBM per device.

```python
import math
import jax
import jax.numpy as jnp
import numpy as np
from jax import lax

D = 768
HEAD = 64
FF = 3072
TOP = 2
SEQS = 2
ROW = 512
LONGEST = 384
ROWS = 128
TOKENS = 65536
TRAINED = 8
EXPERTS = 16
CAPACITY = 96


def with_ends(values, key, low, top_value):
    longest = values.shape.index(max(values.shape))
    spots = []
    for shift in (0, 1):
        where = [jax.random.randint(jax.random.fold_in(key, axis), (), 0, length) for axis, length in enumerate(values.shape)]
        where[longest] = (where[longest] + shift) % values.shape[longest]
        spots.append(tuple(where))
    return values.at[spots[0]].set(low).at[spots[1]].set(top_value)


def level_of(stream_key, extent, split, low, top_value):
    gain, own = 1.0, jax.random.fold_in(stream_key, 6)
    for axis_at, parts in split:
        draws = jnp.exp(jax.random.uniform(jax.random.fold_in(own, axis_at), (parts,), jnp.float32, low / len(split), top_value / len(split)))
        gain = gain * jnp.repeat(draws, extent[axis_at] // parts).reshape([-1 if axis == axis_at else 1 for axis in range(len(extent))])
    return gain


def picks_of(stream_key, rows, amount, top, lift):
    sequence = jax.random.permutation(jax.random.fold_in(stream_key, 1), amount)
    favour = sequence
    for power in range(3):
        favour = favour * favour // amount
    favour = favour * lift // amount
    tickets = jax.random.randint(jax.random.fold_in(stream_key, 2), (rows, amount), 0, 4096) + favour
    sure = jax.random.permutation(jax.random.fold_in(stream_key, 3), rows)[jnp.arange(amount) % rows]
    tickets = jnp.where(jnp.arange(rows)[:, None] == sure[None, :], 1 << 14, tickets)
    priority = tickets * amount + jnp.arange(amount)
    return lax.top_k(priority.astype(jnp.int32), top)[1].astype(jnp.int32)


def length_profile(amount, total, reach, skew):
    weights = [(1 << 20) // math.isqrt(standing ** skew) + 1 for standing in range(2, amount + 1)]
    rest, counts = total - reach - (amount - 1), [1] * (amount - 1)
    while rest > 0:
        free = [i for i in range(amount - 1) if counts[i] < reach]
        mass, remaining = sum([weights[i] for i in free]), rest
        for i in free:
            addition = min(reach - counts[i], max(1, remaining * weights[i] // mass), rest)
            counts[i] = counts[i] + addition
            rest = rest - addition
    return np.array([reach] + counts)


def uneven(key, amount, total, bound, skew):
    if amount == 2:
        one = jax.random.randint(key, (), max(1, total - bound), min(bound, total - 1) + 1)
        return jnp.stack([one, total - one])
    lengths = jnp.asarray(length_profile(amount, total, bound, skew), jnp.int32)
    twos = (amount - 1) // 2
    giver, sink = lengths[1:1 + 2 * twos:2], lengths[2:2 + 2 * twos:2]
    slack = jnp.minimum(giver - 1, bound - sink)
    passed = jax.random.randint(jax.random.fold_in(key, 1), (twos,), 0, 1 << 20) % (slack + 1)
    lengths = lengths.at[1:1 + 2 * twos:2].set(giver - passed).at[2:2 + 2 * twos:2].set(sink + passed)
    return lengths[jax.random.permutation(jax.random.fold_in(key, 2), amount)]


def normal_values(rng, dims, deviation, bound, split=(), held_as=jnp.bfloat16):
    values = jax.random.normal(rng, dims, jnp.float32) * deviation
    if len(split) > 0:
        values = level_of(rng, dims, split, -0.22, 0.18) * values
    return jnp.clip(values, min=-bound, max=bound).astype(held_as)


def setup_inputs(seed: int = 0) -> dict:
    seeds = jax.random.split(jax.random.key(seed), 15)
    tokens = normal_values(seeds[0], (TOKENS, D), 1.0, 6.0, ((0, 128),))
    seq_lengths = jax.vmap(lambda own: uneven(own, SEQS, ROW, LONGEST, 1))(jax.random.split(seeds[1], ROWS)).reshape((ROWS, SEQS)).astype(jnp.int32)
    key_mask = with_ends((jax.random.randint(seeds[2], (TOKENS,), 0, 8) < 7).astype(jnp.int32), jax.random.fold_in(seeds[2], 1), 0, 1)
    routes = picks_of(seeds[3], TOKENS, EXPERTS, TOP, 1024)
    cotangent = normal_values(seeds[4], (TOKENS, D), 1.0, 6.0, ((0, 128),))
    qkv_weight = normal_values(seeds[5], (D, 3 * D), D ** -0.5, 0.21875, ((0, 128),), jnp.float32)
    out_weight = normal_values(seeds[6], (D, D), (D // 16) ** -0.5, 0.875, ((0, 128),), jnp.float32)
    router_weight = normal_values(seeds[7], (D, EXPERTS), (2 * D) ** -0.5, 0.15625, ((0, 128),), jnp.float32)
    norm_gains = jnp.clip(1.0 + 0.1 * jax.random.normal(seeds[8], (2, D), jnp.float32), 0.5, 1.5)
    norm_biases = normal_values(seeds[9], (2, D), 0.3, 1.8, ((1, 128),), jnp.float32)
    up_train = normal_values(seeds[10], (TRAINED, D, FF), D ** -0.5, 0.21875, ((0, 8), (1, 16)), jnp.float32)
    down_train = normal_values(seeds[11], (TRAINED, FF, D), FF ** -0.5, 0.109375, ((0, 8), (1, 16)), jnp.float32)
    up_frozen = normal_values(seeds[12], (TRAINED, D, FF), D ** -0.5, 0.21875, ((0, 8), (1, 16)))
    down_frozen = normal_values(seeds[13], (TRAINED, FF, D), FF ** -0.5, 0.109375, ((0, 8), (1, 16)))
    return {"tokens": tokens, "seq_lengths": seq_lengths, "key_mask": key_mask, "routes": routes, "cotangent": cotangent, "qkv_weight": qkv_weight, "out_weight": out_weight, "router_weight": router_weight, "norm_gains": norm_gains, "norm_biases": norm_biases, "up_train": up_train, "down_train": down_train, "up_frozen": up_frozen, "down_frozen": down_frozen}


exact_mode = lax.Precision.HIGHEST

@jax.custom_vjp
def low(v):
    return lax.optimization_barrier(v.astype(jnp.bfloat16)).astype(jnp.float32)

@jax.custom_vjp
def low_back(v):
    return v

def low_keep(v):
    return (low(v), None)

def low_pass(kept, grad):
    return (grad,)

def back_keep(v):
    return (v, None)

def back_low(kept, grad):
    return (low(grad),)
low.defvjp(low_keep, low_pass)
low_back.defvjp(back_keep, back_low)

def layer_norm(values, gain_row, bias_row):
    average = lax.optimization_barrier(jnp.mean(values, -1, keepdims=True))
    centered = values - average
    variance = lax.optimization_barrier(jnp.mean(centered * centered, -1, keepdims=True))
    return centered * lax.rsqrt(variance + 1e-05) * gain_row + bias_row

def visible(lengths_row, mask_row, count):
    places = lax.iota(jnp.int32, count)
    seq_ends = jnp.cumsum(lengths_row)
    segment = lax.optimization_barrier(jnp.sum((places[:, None] >= seq_ends[None, :]).astype(jnp.int32), 1))
    same_seq = segment[:, None] == segment[None, :]
    causal = places[None, :] <= places[:, None]
    open_key = (mask_row[None, :] == 1) | (places[:, None] == places[None, :])
    return same_seq & causal & open_key

def reference(tokens, seq_lengths, key_mask, routes, cotangent, qkv_weight, out_weight, router_weight, norm_gains, norm_biases, up_train, down_train, up_frozen, down_frozen):
    rows_in = tokens.astype(jnp.float32).reshape(ROWS, ROW, D)
    mask_rows = key_mask.reshape(ROWS, ROW)
    route_rows = routes.reshape(ROWS, ROW, TOP)
    head_count = D // HEAD

    def forward(rows_x, w_qkv, w_out, w_router, gains, biases, up_mine, down_mine):
        w_qkv = low(w_qkv)
        w_out = low(w_out)
        w_router = low(w_router)
        gains = low(gains)
        biases = low(biases)
        up_all = jnp.concatenate((low(up_mine), up_frozen.astype(jnp.float32)), 0)
        down_all = jnp.concatenate((low(down_mine), down_frozen.astype(jnp.float32)), 0)

        def one_row(packed):
            values, lengths_row, mask_row, routes_row = packed
            allowed = visible(lengths_row, mask_row, ROW)
            h_one = low(layer_norm(values, gains[0], biases[0]))
            qkv_all = low(low_back(jnp.dot(h_one, w_qkv, precision=exact_mode)))
            q_part = qkv_all[:, :D].reshape(ROW, head_count, HEAD)
            k_part = qkv_all[:, D:2 * D].reshape(ROW, head_count, HEAD)
            v_part = qkv_all[:, 2 * D:].reshape(ROW, head_count, HEAD)
            scores = low_back(jnp.einsum('qhd,khd->hqk', q_part, k_part, precision=exact_mode) * 0.125)
            scores = jnp.where(allowed[None], scores, -1e+30)
            attn_probs = jax.nn.softmax(scores, -1)
            attn_out = jnp.einsum('hqk,khd->qhd', low(attn_probs), v_part, precision=exact_mode).reshape(ROW, D)
            attn_out = low(low_back(attn_out))
            x_mid = values + low_back(jnp.dot(attn_out, w_out, precision=exact_mode))
            h_two = low(layer_norm(x_mid, gains[1], biases[1]))
            logits = jnp.dot(h_two, w_router, precision=exact_mode)
            chosen = jnp.take_along_axis(logits, routes_row, 1)
            gate_vals = jax.nn.softmax(chosen, -1)
            flat_ids = routes_row.reshape(-1)
            flat_hot = (flat_ids[:, None] == lax.iota(jnp.int32, EXPERTS)[None, :]).astype(jnp.int32)
            slot_pos = lax.optimization_barrier(jnp.sum((jnp.cumsum(flat_hot, 0) - flat_hot) * flat_hot, 1))
            is_kept = slot_pos < CAPACITY
            slot_id = jnp.where(is_kept, flat_ids * CAPACITY + slot_pos, EXPERTS * CAPACITY).astype(jnp.int32)
            pair_rows = jnp.repeat(h_two, TOP, axis=0)
            slot_rows = jnp.zeros((EXPERTS * CAPACITY, D), jnp.float32).at[slot_id].add(pair_rows, mode='drop')
            slot_rows = low_back(slot_rows).reshape(EXPERTS, CAPACITY, D)
            up_vals = low_back(jnp.einsum('ecd,edf->ecf', slot_rows, up_all, precision=exact_mode))
            activated = low(jax.nn.gelu(up_vals, approximate=True))
            expert_out = low(low_back(jnp.einsum('ecf,efd->ecd', activated, down_all, precision=exact_mode)))
            expert_out = expert_out.reshape(EXPERTS * CAPACITY, D)
            pick_index = jnp.minimum(slot_id, EXPERTS * CAPACITY - 1)
            pair_vals = jnp.where(is_kept[:, None], expert_out[pick_index], 0.0).reshape(ROW, TOP, D)
            return x_mid + lax.optimization_barrier(jnp.sum(gate_vals[:, :, None] * pair_vals, 1))
        return lax.map(jax.checkpoint(one_row), (rows_x, seq_lengths, mask_rows, route_rows))
    outputs, pullback = jax.vjp(forward, rows_in, qkv_weight, out_weight, router_weight, norm_gains, norm_biases, up_train, down_train)
    gradients = pullback(cotangent.astype(jnp.float32).reshape(ROWS, ROW, D))
    block_out = outputs.reshape(TOKENS, D).astype(jnp.bfloat16)
    input_grad = gradients[0].reshape(TOKENS, D)
    return (block_out, input_grad, gradients[1], gradients[2], gradients[3], gradients[4], gradients[5], gradients[6], gradients[7])
```

```python
import jax
import jax.numpy as jnp
from jax import lax
from jax.sharding import Mesh
from jax.sharding import PartitionSpec as P

HEAD = 64
TOP = 2
SIZES = (4, 2, 2, 4, 2)
NAMES = ("x", "yh", "c", "z", "yl")
WIDE = ("x", "yh", "c")
NARROW = ("z", "yl")
BF = jnp.bfloat16
F32 = jnp.float32


def shift(value, axis, by):
    count = lax.axis_size(axis)
    return lax.ppermute(value, axis, [(i, (i + by) % count) for i in range(count)])


def ordered(mine, other, index):
    first = jnp.where(index == 0, mine, other)
    second = jnp.where(index == 0, other, mine)
    return first, second


def gather_dense(block):
    width = block.shape[1]
    spread = jnp.broadcast_to(block[None], (8, 8, width))
    near = lax.all_to_all(spread, NARROW, split_axis=0, concat_axis=0, tiled=True)
    rows = near[:, :6].reshape(48, width)
    x, yh, c = (lax.axis_index(name) for name in WIDE)
    both = jnp.stack(ordered(rows, shift(rows, "yh", 1), yh))
    full = jnp.zeros((4, 2, 2, 48, width), BF)
    for step in range(4):
        part = both if step == 0 else shift(both, "x", step)
        pair = jnp.stack(ordered(part, shift(part, "c", 1), c), 1)
        full = lax.dynamic_update_slice(full, pair[None], ((x - step) % 4, 0, 0, 0, 0))
    return full.reshape(768, width)


def scatter_dense(grad):
    width = grad.shape[1]
    x, yh, c = (lax.axis_index(name) for name in WIDE)
    parts = grad.reshape(8, 2, 48, width)
    keep = lax.dynamic_index_in_dim(parts, c, 1, False)
    away = lax.dynamic_index_in_dim(parts, 1 - c, 1, False)
    held = (keep.astype(F32) + shift(away, "c", 1).astype(F32)).astype(BF).reshape(4, 2, 48, width)
    total = lax.dynamic_index_in_dim(held, x, 0, False).astype(F32)
    for step in (1, 3, 2):
        piece = lax.dynamic_index_in_dim(held, (x + step) % 4, 0, False)
        total = total + shift(piece, "x", step).astype(F32)
    away = lax.dynamic_index_in_dim(total, 1 - yh, 0, False).astype(BF)
    total = lax.dynamic_index_in_dim(total, yh, 0, False) + shift(away, "yh", 1).astype(F32)
    pieces = total.astype(BF).reshape(8, 6, width)
    pieces = jnp.pad(pieces, ((0, 0), (0, 2), (0, 0)))
    near = lax.all_to_all(pieces, NARROW, split_axis=0, concat_axis=0, tiled=True)
    return jnp.sum(near.astype(F32), 0)[:6]


def layer_norm(values, gain_row, bias_row):
    average = jnp.mean(values, -1, keepdims=True)
    centered = values - average
    variance = jnp.mean(centered * centered, -1, keepdims=True)
    return centered * lax.rsqrt(variance + 1e-05) * gain_row + bias_row


def smooth_act(pre_act):
    return jax.nn.gelu(pre_act, approximate=True)


def visible(lengths_row, mask_row, count):
    places = lax.iota(jnp.int32, count)
    seq_ends = jnp.cumsum(lengths_row)
    segment = jnp.sum((places[:, None] >= seq_ends[None, :]).astype(jnp.int32), 1)
    same_seq = segment[:, None] == segment[None, :]
    causal = places[None, :] <= places[:, None]
    open_key = (mask_row[None, :] == 1) | (places[:, None] == places[None, :])
    return same_seq & causal & open_key


def masked_scores(q_part, k_part, allowed):
    scores = jnp.einsum("qhd,khd->hqk", q_part, k_part, preferred_element_type=F32) * 0.125
    return jnp.where(allowed[None], scores, -1e30)


def with_tail(rows, values):
    high = values.astype(BF)
    low = (values - high.astype(F32)).astype(BF)
    line = jnp.concatenate((jnp.pad(high, ((0, 0), (0, 32))), jnp.pad(low, ((0, 0), (0, 32)))), 1)
    tail = jnp.pad(line[:, None, :], ((0, 0), (0, 15), (0, 512)))
    return jnp.concatenate((rows, tail), 1)


def split_tail(sent):
    line = sent[:, 96].astype(F32)
    return sent[:, :96], line[:, :96] + line[:, 128:224]


def exchange(rows):
    return lax.all_to_all(rows, ("c", "z", "yl"), split_axis=0, concat_axis=0, tiled=True)


def shards(
    tokens,
    seq_lengths,
    key_mask,
    routes,
    cotangent,
    qkv_weight,
    out_weight,
    router_weight,
    norm_gains,
    norm_biases,
    up_train,
    down_train,
    up_frozen,
    down_frozen,
):
    row_count, width = tokens.shape
    head_count = width // HEAD
    experts = 16
    capacity = 96
    slot_count = experts * capacity
    core = lax.axis_index("c")

    small = jnp.concatenate((router_weight, norm_gains.T, norm_biases.T), 1).astype(BF)
    block = jnp.concatenate(
        (qkv_weight.astype(BF), out_weight.astype(BF), jnp.pad(small, ((0, 0), (0, 108)))), 1
    )
    dense = gather_dense(jnp.pad(block, ((0, 2), (0, 0))))
    w_qkv, w_out, rest = dense[:, :2304], dense[:, 2304:3072], dense[:, 3072:]
    w_router = rest[:, :16]
    gains = rest[:, 16:18].astype(F32).T
    biases = rest[:, 18:20].astype(F32).T

    up_t, down_t = up_train[0].astype(BF), down_train[0].astype(BF)
    up_f, down_f = up_frozen[0], down_frozen[0]
    up_other = shift(jnp.where(core == 0, up_f, up_t), "c", 1)
    down_other = shift(jnp.where(core == 0, down_f, down_t), "c", 1)
    up_two = jnp.concatenate(ordered(jnp.where(core == 0, up_t, up_f), up_other, core), 0)
    down_two = jnp.concatenate(ordered(jnp.where(core == 0, down_t, down_f), down_other, core), 0)
    w_up = lax.all_gather(up_two, ("x", "yh"), tiled=True)
    w_down = lax.all_gather(down_two, ("x", "yh"), tiled=True)

    route_hot = routes[:, :, None] == lax.iota(jnp.int32, experts)[None, None, :]
    token_hot = jnp.any(route_hot, 1).astype(BF)
    places = lax.iota(jnp.int32, row_count)
    before = (places[None, :] < places[:, None]).astype(BF)
    earlier = jnp.dot(before, token_hot, preferred_element_type=F32)
    slot_pos = jnp.sum(jnp.where(route_hot, earlier[:, None, :], 0.0), -1).astype(jnp.int32)
    slot_id = jnp.where(slot_pos < capacity, routes * capacity + slot_pos, slot_count)
    slots = lax.iota(jnp.int32, slot_count)
    hot_first = slots[:, None] == slot_id[None, :, 0]
    hot_second = slots[:, None] == slot_id[None, :, 1]
    dispatch = (hot_first | hot_second).astype(BF)
    g_slots = jnp.dot(dispatch, cotangent, preferred_element_type=F32).astype(BF)
    g_rows = exchange(g_slots.reshape(experts, capacity, width)).reshape(slot_count, width)

    allowed = visible(seq_lengths[0], key_mask, row_count)
    x_in = tokens.astype(F32)
    h_one = layer_norm(x_in, gains[0], biases[0]).astype(BF)
    qkv_all = jnp.dot(h_one, w_qkv, preferred_element_type=F32).astype(BF)
    q_part = qkv_all[:, :width].reshape(row_count, head_count, HEAD)
    k_part = qkv_all[:, width : 2 * width].reshape(row_count, head_count, HEAD)
    v_part = qkv_all[:, 2 * width :].reshape(row_count, head_count, HEAD)
    scores = masked_scores(q_part, k_part, allowed)
    row_peak = jnp.max(scores, -1, keepdims=True)
    exp_scores = jnp.exp(scores - row_peak)
    row_total = jnp.sum(exp_scores, -1, keepdims=True)
    log_total = row_peak + jnp.log(row_total)
    attn_probs = (exp_scores / row_total).astype(BF)
    attn_out = (
        jnp.einsum("hqk,khd->qhd", attn_probs, v_part, preferred_element_type=F32)
        .reshape(row_count, width)
        .astype(BF)
    )
    x_mid = x_in + jnp.dot(attn_out, w_out, preferred_element_type=F32)
    h_two = layer_norm(x_mid, gains[1], biases[1]).astype(BF)
    logits = jnp.dot(h_two, w_router, preferred_element_type=F32)
    chosen = jnp.sum(jnp.where(route_hot, logits[:, None, :], 0.0), -1)
    gate_vals = jax.nn.softmax(chosen, -1)
    gate_slot = jnp.sum(
        jnp.where(hot_first, gate_vals[None, :, 0], 0.0)
        + jnp.where(hot_second, gate_vals[None, :, 1], 0.0),
        1,
    )
    h_slots = jnp.dot(dispatch, h_two, preferred_element_type=F32).astype(BF)
    sent = with_tail(h_slots.reshape(experts, capacity, width), gate_slot.reshape(experts, capacity))
    rows, gate_rows = split_tail(exchange(sent))
    rows = rows.reshape(slot_count, width)
    gate_rows = gate_rows.reshape(slot_count, 1)

    up_vals = jnp.dot(rows, w_up, preferred_element_type=F32)
    act_vals, gelu_pull = jax.vjp(smooth_act, up_vals)
    activated = act_vals.astype(BF)
    expert_out = jnp.dot(activated, w_down, preferred_element_type=F32).astype(BF)
    d_out = (gate_rows * g_rows.astype(F32)).astype(BF)
    d_gate_rows = jnp.sum(expert_out.astype(F32) * g_rows.astype(F32), -1)
    d_acts = jnp.einsum("rd,fd->rf", d_out, w_down, preferred_element_type=F32)
    d_up = gelu_pull(d_acts)[0].astype(BF)
    d_rows = jnp.einsum("rf,df->rd", d_up, w_up, preferred_element_type=F32).astype(BF)
    d_sent = with_tail(
        d_rows.reshape(experts, capacity, width), d_gate_rows.reshape(experts, capacity)
    )
    d_back, d_gate_slot = split_tail(exchange(d_sent))
    returned = exchange(expert_out.reshape(experts, capacity, width)).reshape(slot_count, width)
    grad_down_t = jnp.einsum("rf,rd->fd", activated, d_out, preferred_element_type=F32).astype(BF)
    grad_up_t = jnp.einsum("rd,rf->df", rows, d_up, preferred_element_type=F32).astype(BF)

    def expert_grad(grad):
        parts = grad.reshape(8, 2, grad.shape[0] // 16, grad.shape[1])
        got = lax.ppermute(parts[:, 1], "c", [(0, 1)])
        mine = jnp.where(core == 0, parts[:, 0], got).reshape(-1, grad.shape[1])
        return lax.psum_scatter(mine, ("x", "yh"), scatter_dimension=0, tiled=True).astype(F32)[None]

    grad_up = expert_grad(grad_up_t)
    grad_down = expert_grad(grad_down_t)

    pick = (slot_id[:, :, None] == slots[None, None, :]).astype(BF)
    back_first = jnp.dot(pick[:, 0], returned, preferred_element_type=F32)
    back_second = jnp.dot(pick[:, 1], returned, preferred_element_type=F32)
    block_out = (x_mid + gate_vals[:, :1] * back_first + gate_vals[:, 1:] * back_second).astype(BF)
    d_res = cotangent.astype(F32)
    d_gate_flat = d_gate_slot.reshape(slot_count)
    d_gates = jnp.sum(
        jnp.where(slot_id[:, :, None] == slots[None, None, :], d_gate_flat[None, None, :], 0.0), -1
    )
    d_chosen = gate_vals * (d_gates - jnp.sum(gate_vals * d_gates, -1, keepdims=True))
    d_logits = jnp.sum(jnp.where(route_hot, d_chosen[:, :, None], 0.0), 1)
    d_h_two = jnp.dot(
        pick[:, 0] + pick[:, 1], d_back.reshape(slot_count, width), preferred_element_type=F32
    )
    d_h_two = d_h_two + jnp.einsum("re,de->rd", d_logits, w_router.astype(F32))
    grad_router_l = jnp.einsum("rd,re->de", h_two.astype(F32), d_logits)
    unused_two, pull_two = jax.vjp(layer_norm, x_mid, gains[1], biases[1])
    d_mid_norm, d_gain_two, d_bias_two = pull_two(d_h_two)
    d_x_mid = d_res + d_mid_norm
    d_proj = d_x_mid.astype(BF)
    grad_out_l = jnp.einsum("rd,re->de", attn_out, d_proj, preferred_element_type=F32)
    d_attn = jnp.einsum("re,de->rd", d_proj, w_out, preferred_element_type=F32).astype(BF)
    d_attn_h = d_attn.reshape(row_count, head_count, HEAD)
    probs_back = jnp.exp(masked_scores(q_part, k_part, allowed) - log_total)
    d_probs = jnp.einsum("qhd,khd->hqk", d_attn_h, v_part, preferred_element_type=F32)
    d_vals = jnp.einsum(
        "hqk,qhd->khd", probs_back.astype(BF), d_attn_h, preferred_element_type=F32
    )
    row_delta = jnp.sum(probs_back * d_probs, -1, keepdims=True)
    d_scores = (probs_back * (d_probs - row_delta)).astype(BF)
    d_query = jnp.einsum("hqk,khd->qhd", d_scores, k_part, preferred_element_type=F32) * 0.125
    d_key = jnp.einsum("hqk,qhd->khd", d_scores, q_part, preferred_element_type=F32) * 0.125
    d_qkv = jnp.concatenate(
        (
            d_query.reshape(row_count, width),
            d_key.reshape(row_count, width),
            d_vals.reshape(row_count, width),
        ),
        1,
    ).astype(BF)
    grad_qkv_l = jnp.einsum("rd,re->de", h_one, d_qkv, preferred_element_type=F32)
    d_h_one = jnp.einsum("re,de->rd", d_qkv, w_qkv, preferred_element_type=F32)
    unused_one, pull_one = jax.vjp(layer_norm, x_in, gains[0], biases[0])
    d_in_norm, d_gain_one, d_bias_one = pull_one(d_h_one)
    input_grad = d_x_mid + d_in_norm
    small_l = jnp.concatenate(
        (grad_router_l, jnp.stack((d_gain_one, d_gain_two, d_bias_one, d_bias_two), 1)), 1
    )
    grads = jnp.concatenate(
        (grad_qkv_l.astype(BF), grad_out_l.astype(BF), jnp.pad(small_l.astype(BF), ((0, 0), (0, 108)))), 1
    )
    own = scatter_dense(grads)
    return (
        block_out,
        input_grad,
        own[:, :2304],
        own[:, 2304:3072],
        own[:, 3072:3088],
        own[:, 3088:3090].T,
        own[:, 3090:3092].T,
        grad_up,
        grad_down,
    )


def solution(mesh):
    fine = Mesh(mesh.devices.reshape(SIZES), NAMES)
    by_row = P(NAMES, None)
    by_column = P(None, NAMES)
    by_expert = P(NARROW, WIDE, None)
    return jax.shard_map(
        shards,
        mesh=fine,
        in_specs=(by_row, by_row, P(NAMES)) + (by_row,) * 5 + (by_column,) * 2 + (by_expert,) * 4,
        out_specs=(by_row,) * 5 + (by_column,) * 2 + (by_expert,) * 2,
        check_vma=False,
    )
```

```python
import jax
import jax.numpy as jnp
from jax import lax
from jax.experimental import pallas as pl
from jax.experimental.pallas import tpu as pltpu
from jax.sharding import Mesh
from jax.sharding import PartitionSpec as P

SIZES = (4, 2, 2, 4, 2)
NAMES = ("x", "yh", "c", "z", "yl")
WIDE = ("x", "yh", "c")
NARROW = ("z", "yl")
BF = jnp.bfloat16
F32 = jnp.float32
ROW = 512
D = 768
FF = 3072
CAP = 96
LINE = 112
SOURCES = 4
GELU_ONE = 0.7978845608028654
GELU_CUBE = GELU_ONE * 0.044715
MIB = 1024 * 1024


def nn(a, b):
    return jnp.dot(a, b, preferred_element_type=F32)


def nt(a, b):
    return lax.dot_general(a, b, (((1,), (1,)), ((), ())), preferred_element_type=F32)


def tn(a, b):
    return lax.dot_general(a, b, (((0,), (0,)), ((), ())), preferred_element_type=F32)


def iota(shape, dim):
    return lax.broadcasted_iota(jnp.int32, shape, dim)


def hot(mask):
    return jnp.where(mask, 1.0, 0.0).astype(BF)


def like(*dims, dtype=BF):
    return jax.ShapeDtypeStruct(dims, dtype)


def cost(flops, moved, transcendentals=0):
    return pl.CostEstimate(flops=flops, bytes_accessed=moved, transcendentals=transcendentals)


def tail_of(line):
    high = line.astype(BF).astype(F32)
    low = (line - high).astype(BF).astype(F32)
    full = jnp.concatenate([high, low, jnp.zeros((1, 512), F32)], 1)
    return jnp.where(iota((16, D), 0) == 0, jnp.broadcast_to(full, (16, D)), 0.0).astype(BF)


def line_of(tail):
    line = tail.astype(F32)[0:1]
    return line[:, :128] + line[:, 128:256]


def norm(x):
    centered = x - jnp.mean(x, -1, keepdims=True)
    scale = lax.rsqrt(jnp.mean(centered * centered, -1, keepdims=True) + 1e-5)
    return centered * scale, scale


def norm_back(d_out, x_hat, scale, gain):
    t = d_out * gain
    d_in = scale * (
        t - jnp.mean(t, -1, keepdims=True) - x_hat * jnp.mean(t * x_hat, -1, keepdims=True)
    )
    return d_in, jnp.sum(d_out * x_hat, 0, keepdims=True), jnp.sum(d_out, 0, keepdims=True)


def route_body(routes_ref, cot_ref, g_ref, sid_ref, sidt_ref):
    lane = iota((ROW, 128), 1)
    r0, r1 = routes_ref[:, 0:1], routes_ref[:, 1:2]
    either = hot((lane == r0) | (lane == r1))
    earlier = nn(hot(iota((ROW, ROW), 1) < iota((ROW, ROW), 0)), either)
    p0 = jnp.sum(jnp.where(lane == r0, earlier, 0.0), 1, keepdims=True).astype(jnp.int32)
    p1 = jnp.sum(jnp.where(lane == r1, earlier, 0.0), 1, keepdims=True).astype(jnp.int32)
    columns = (
        jnp.where(p0 < CAP, r0 * CAP + p0, -1),
        jnp.where(p1 < CAP, r1 * CAP + p1, -1),
        jnp.where(p0 < CAP, r0 * LINE + p0, -1),
        jnp.where(p1 < CAP, r1 * LINE + p1, -1),
        r0,
    )
    table = jnp.broadcast_to(r1, (ROW, 128))
    for at, column in enumerate(columns):
        table = jnp.where(lane == at, column, table)
    sid_ref[...] = table
    turned = jnp.transpose(table.astype(F32))[0:8].astype(jnp.int32)
    sidt_ref[...] = turned
    for part in range(4):
        slot = iota((4 * CAP, ROW), 0) + part * 4 * CAP
        pick = hot((slot == turned[0:1]) | (slot == turned[1:2]))
        g_ref[part * 4 * CAP : (part + 1) * 4 * CAP, :] = nn(pick, cot_ref[...]).astype(BF)


def route(routes, cotangent):
    return pl.pallas_call(
        route_body,
        out_shape=[like(16 * CAP, D), like(ROW, 128, dtype=jnp.int32), like(8, ROW, dtype=jnp.int32)],
        compiler_params=pltpu.CompilerParams(vmem_limit_bytes=32 * MIB),
        cost_estimate=cost(2 * 1536 * 512 * 768, 4 * 10**6),
    )(routes, cotangent)


def forward_body(*refs):
    lens_ref, nat_ref, mask_ref, tok_ref, sid_ref, sidt_ref = refs[:6]
    pieces = refs[6:14]
    (
        w_ref, h1p_ref, qkv_ref, probs_ref, attnp_ref, xmid_ref, h2_ref, gate_ref, vec_ref,
        router_ref, sent_ref, rest_ref, attn, bias,
    ) = refs[14:]
    for at, piece in enumerate(pieces):
        w_ref[at * 96 : (at + 1) * 96, :] = piece[:, :FF]
        rest_ref[at * 96 : (at + 1) * 96, :] = piece[:, FF:]
    turn = hot(iota((D, D), 0) == nat_ref[...])
    rest = nn(turn, rest_ref[...])
    vectors = jnp.transpose(rest)[16:24]
    router_ref[...] = rest.astype(BF)
    vec_ref[...] = vectors
    x = tok_ref[...].astype(F32)
    h1 = (norm(x)[0] * vectors[0:1] + vectors[2:3]).astype(BF)
    h1p_ref[...] = nn(h1, turn).astype(BF)
    for part in range(3):
        cols = slice(part * D, (part + 1) * D)
        qkv_ref[:, cols] = nn(h1p_ref[...], w_ref[:, cols]).astype(BF)

    end_one = lens_ref[0]
    end_two = end_one + lens_ref[1]

    def segment(place):
        return (place >= end_one).astype(jnp.int32) + (place >= end_two).astype(jnp.int32)

    query, key = iota((ROW, ROW), 0), iota((ROW, ROW), 1)
    same = segment(iota((ROW, 1), 0)) == segment(iota((1, ROW), 1))
    allowed = same & (key <= query) & ((mask_ref[...] == 1) | (key == query))
    bias[...] = jnp.where(allowed, 0.0, -1e30)
    low = iota((1, 128), 1) < 64
    half = ROW // 2
    zero = jnp.zeros((), BF)

    def pair(index, carry):
        at = pl.multiple_of(index * 128, 128)
        q = qkv_ref[:, pl.ds(at, 128)] * jnp.asarray(0.125, BF)
        k = qkv_ref[:, pl.ds(D + at, 128)]
        v = qkv_ref[:, pl.ds(2 * D + at, 128)]
        out = [None, None]
        for head in range(2):
            mine = low if head == 0 else jnp.logical_not(low)
            k_mine, v_mine = jnp.where(mine, k, zero), jnp.where(mine, v, zero)
            for block in range(2):
                count, rows = half * (block + 1), slice(block * half, (block + 1) * half)
                scores = nt(q[rows], k_mine[:count]) + bias[rows, :count]
                e = jnp.exp(scores - jnp.max(scores, 1, keepdims=True))
                probs = (e * (1.0 / jnp.sum(e, 1, keepdims=True))).astype(BF)
                probs_ref[2 * index + head, rows, :count] = probs
                if block == 0:
                    probs_ref[2 * index + head, rows, count:] = jnp.zeros((half, half), BF)
                term = nn(probs, v_mine[:count])
                out[block] = term if head == 0 else out[block] + term
        for block in range(2):
            attn[block * half : (block + 1) * half, pl.ds(at, 128)] = out[block].astype(BF)
        return carry

    lax.fori_loop(0, 6, pair, 0)
    attnp_ref[...] = nn(attn[...], turn).astype(BF)
    x_mid = x + nn(attnp_ref[...], w_ref[:, 3 * D :])
    xmid_ref[...] = x_mid
    h2 = (norm(x_mid)[0] * vectors[1:2] + vectors[3:4]).astype(BF)
    h2_ref[...] = h2
    logits = nn(h2, router_ref[...])
    lane = iota((ROW, 128), 1)
    s0, s1, r0, r1 = (sid_ref[:, at : at + 1] for at in (0, 1, 4, 5))
    c0 = jnp.sum(jnp.where(lane == r0, logits, 0.0), 1, keepdims=True)
    c1 = jnp.sum(jnp.where(lane == r1, logits, 0.0), 1, keepdims=True)
    g0, g1 = 1.0 / (1.0 + jnp.exp(c1 - c0)), 1.0 / (1.0 + jnp.exp(c0 - c1))
    gate_ref[...] = jnp.where(lane == 0, g0, jnp.where(lane == 1, g1, 0.0))
    first, second = sidt_ref[2:3], sidt_ref[3:4]
    for part in range(4):
        slot = iota((4 * LINE, ROW), 0) + part * 4 * LINE
        pick = hot((slot == first) | (slot == second))
        sent_ref[part * 4 * LINE : (part + 1) * 4 * LINE, :] = nn(pick, h2_ref[...]).astype(BF)
    for expert in range(16):
        slot = lane + expert * CAP
        line = jnp.sum(
            jnp.where(slot == s0, g0, 0.0) + jnp.where(slot == s1, g1, 0.0), 0, keepdims=True
        )
        sent_ref[expert * LINE + CAP : (expert + 1) * LINE, :] = tail_of(line)


def forward(lens, nat, mask, tokens, sid, sidt, pieces):
    vmem = pl.BlockSpec(memory_space=pltpu.VMEM)
    return pl.pallas_call(
        forward_body,
        in_specs=[pl.BlockSpec(memory_space=pltpu.SMEM)] + [vmem] * 13,
        out_shape=[
            like(D, FF),
            like(ROW, D),
            like(ROW, 3 * D),
            like(12, ROW, ROW),
            like(ROW, D),
            like(ROW, D, dtype=F32),
            like(ROW, D),
            like(ROW, 128, dtype=F32),
            like(8, D, dtype=F32),
            like(D, 128),
            like(16 * LINE, D),
        ],
        scratch_shapes=[
            pltpu.VMEM((D, 128), BF),
            pltpu.VMEM((ROW, D), BF),
            pltpu.VMEM((ROW, ROW), F32),
        ],
        compiler_params=pltpu.CompilerParams(vmem_limit_bytes=56 * MIB),
        cost_estimate=cost(2 * 512 * 768 * 6000, 20 * 10**6, 12 * 512 * 512),
    )(lens, nat, mask, tokens, sid, sidt, *pieces)


def expert_body(
    sent_ref, g_ref, up_ref, down_ref, out_ref, back_ref, x_ref, dout_ref, act_ref, dup_ref
):
    for s in range(SOURCES):
        rows = slice(s * CAP, (s + 1) * CAP)
        x_ref[rows, :] = sent_ref[s, :CAP, :]
        gate = line_of(sent_ref[s, CAP:LINE, :])
        column = jnp.transpose(jnp.broadcast_to(gate, (128, 128)))[:CAP, :1]
        dout_ref[rows, :] = (g_ref[s].astype(F32) * column).astype(BF)
    x, d_out = x_ref[...], dout_ref[...]
    for part in range(FF // 256):
        cols = slice(part * 256, (part + 1) * 256)
        up = nn(x, up_ref[:, cols])
        d_act = nt(d_out, down_ref[cols, :])
        square = up * up
        t = jnp.tanh(up * (GELU_ONE + GELU_CUBE * square))
        a = 0.5 + 0.5 * t
        act_ref[:, cols] = (up * a).astype(BF)
        slope = a + (up * (1.0 - t * t)) * (0.5 * GELU_ONE + 1.5 * GELU_CUBE * square)
        dup_ref[:, cols] = (d_act * slope).astype(BF)
    for part in range(D // 256):
        cols = slice(part * 256, (part + 1) * 256)
        out = nn(act_ref[...], down_ref[:, cols]).astype(BF)
        back = nt(dup_ref[...], up_ref[cols, :]).astype(BF)
        for s in range(SOURCES):
            out_ref[s, :, cols] = out[s * CAP : (s + 1) * CAP]
            back_ref[s, :CAP, cols] = back[s * CAP : (s + 1) * CAP]
    for s in range(SOURCES):
        d_gate = jnp.sum(out_ref[s].astype(F32) * g_ref[s].astype(F32), -1, keepdims=True)
        wide = jnp.concatenate(
            [jnp.broadcast_to(d_gate, (CAP, 128)), jnp.zeros((128 - CAP, 128), F32)], 0
        )
        back_ref[s, CAP:LINE, :] = tail_of(jnp.transpose(wide)[0:1])


def experts(sent, g, w_up, w_down):
    rows = SOURCES * CAP
    once = pl.Buffered(1)
    by_source = lambda size: pl.BlockSpec((SOURCES, size, D), lambda i: (i, 0, 0))
    by_rows = lambda width: pl.BlockSpec((rows, width), lambda i: (i, 0))
    return pl.pallas_call(
        expert_body,
        grid=(16 // SOURCES,),
        in_specs=[
            by_source(LINE),
            by_source(CAP),
            pl.BlockSpec((D, FF), lambda i: (0, 0), pipeline_mode=once),
            pl.BlockSpec((FF, D), lambda i: (0, 0), pipeline_mode=once),
        ],
        out_specs=[
            by_source(CAP), by_source(LINE), by_rows(D), by_rows(D), by_rows(FF), by_rows(FF),
        ],
        out_shape=[
            like(16, CAP, D),
            like(16, LINE, D),
            like(16 * CAP, D),
            like(16 * CAP, D),
            like(16 * CAP, FF),
            like(16 * CAP, FF),
        ],
        compiler_params=pltpu.CompilerParams(vmem_limit_bytes=60 * MIB),
        cost_estimate=cost(8 * 1536 * 768 * 3072, 40 * 10**6, 1536 * 3072),
    )(sent, g, w_up, w_down)


def back_one_body(
    nat_ref, sid_ref, dback_ref, gate_ref, router_ref, vec_ref, cot_ref, xmid_ref, h2_ref,
    attnp_ref, w_ref, dxm_ref, dattn_ref, grads_ref,
):
    lane = iota((ROW, 128), 1)
    s0, s1, w0, w1, r0, r1 = (sid_ref[:, at : at + 1] for at in range(6))
    a0 = a1 = jnp.zeros((ROW, 128), F32)
    for expert in range(16):
        line = line_of(dback_ref[expert * LINE + CAP : (expert + 1) * LINE, :])
        slot = jnp.where(lane < CAP, lane + expert * CAP, -2)
        a0 = a0 + jnp.where(slot == s0, line, 0.0)
        a1 = a1 + jnp.where(slot == s1, line, 0.0)
    dg0, dg1 = jnp.sum(a0, 1, keepdims=True), jnp.sum(a1, 1, keepdims=True)
    g0, g1 = gate_ref[:, 0:1], gate_ref[:, 1:2]
    both = g0 * dg0 + g1 * dg1
    d_logits = jnp.where(lane == r0, g0 * (dg0 - both), 0.0)
    d_logits = d_logits + jnp.where(lane == r1, g1 * (dg1 - both), 0.0)
    high = d_logits.astype(BF)
    low = (d_logits - high.astype(F32)).astype(BF)
    d_h2 = nt(high, router_ref[...]) + nt(low, router_ref[...])
    for part in range(4):
        slot = iota((ROW, 4 * LINE), 1) + part * 4 * LINE
        pick = hot((slot == w0) | (slot == w1))
        d_h2 = d_h2 + nn(pick, dback_ref[part * 4 * LINE : (part + 1) * 4 * LINE, :])
    x_hat, scale = norm(xmid_ref[...])
    d_in, d_gain, d_bias = norm_back(d_h2, x_hat, scale, vec_ref[1:2])
    d_x_mid = cot_ref[...].astype(F32) + d_in
    dxm_ref[...] = d_x_mid
    d_proj = d_x_mid.astype(BF)
    turn = hot(iota((D, D), 0) == nat_ref[...])
    dattn_ref[...] = nt(nt(d_proj, w_ref[...]).astype(BF), turn).astype(BF)
    grads_ref[:, :D] = tn(attnp_ref[...], d_proj).astype(BF)
    d_router = tn(h2_ref[...], high) + tn(h2_ref[...], low)
    sub = iota((128, D), 0)
    rows = jnp.where(sub == 17, d_gain, 0.0) + jnp.where(sub == 19, d_bias, 0.0)
    small = d_router + jnp.transpose(rows)
    grads_ref[:, D:] = tn(turn, small.astype(BF)).astype(BF)


def back_one(nat, sid, d_back, gate, router, vec, cotangent, x_mid, h2, attnp, w):
    vmem = pl.BlockSpec(memory_space=pltpu.VMEM)
    return pl.pallas_call(
        back_one_body,
        grid=(1,),
        in_specs=[vmem] * 10 + [pl.BlockSpec((D, D), lambda i: (0, 3))],
        out_specs=[vmem] * 3,
        out_shape=[like(ROW, D, dtype=F32), like(ROW, D), like(D, D + 128)],
        compiler_params=pltpu.CompilerParams(vmem_limit_bytes=48 * MIB),
        cost_estimate=cost(2 * 512 * 768 * 4300, 12 * 10**6),
    )(nat, sid, d_back, gate, router, vec, cotangent, x_mid, h2, attnp, w)


def back_two_body(
    nat_ref, dattn_ref, probs_ref, qkv_ref, h1p_ref, dxm_ref, tok_ref, vec_ref, w_ref,
    gx_ref, grads_ref, d_qkv,
):
    low = iota((1, 128), 1) < 64
    zero = jnp.zeros((), BF)
    half = ROW // 2

    def add(terms, at, term):
        terms[at] = term if terms[at] is None else terms[at] + term

    def pair(index, carry):
        at = pl.multiple_of(index * 128, 128)
        q, k, v = (qkv_ref[:, pl.ds(part * D + at, 128)] for part in range(3))
        d_attn = dattn_ref[:, pl.ds(at, 128)]
        dq, dk, dv = [None, None], [None, None], [None, None]
        for head in range(2):
            mine = low if head == 0 else jnp.logical_not(low)
            q_mine, k_mine, v_mine, d_mine = (jnp.where(mine, t, zero) for t in (q, k, v, d_attn))
            for block in range(2):
                count, rows = half * (block + 1), slice(block * half, (block + 1) * half)
                probs = probs_ref[2 * index + head, rows, :count]
                d_probs = nt(d_mine[rows], v_mine[:count])
                wide = probs.astype(F32)
                weighted = wide * d_probs
                delta = jnp.sum(weighted, 1, keepdims=True)
                d_scores = (weighted - wide * delta).astype(BF)
                add(dq, block, nn(d_scores, k_mine[:count]))
                for other in range(block + 1):
                    keys = slice(other * half, (other + 1) * half)
                    add(dk, other, tn(d_scores[:, keys], q_mine[rows]))
                    add(dv, other, tn(probs[:, keys], d_mine[rows]))
        for block in range(2):
            rows = slice(block * half, (block + 1) * half)
            d_qkv[rows, pl.ds(at, 128)] = (dq[block] * 0.125).astype(BF)
            d_qkv[rows, pl.ds(D + at, 128)] = (dk[block] * 0.125).astype(BF)
            d_qkv[rows, pl.ds(2 * D + at, 128)] = dv[block].astype(BF)
        return carry

    lax.fori_loop(0, 6, pair, 0)
    for part in range(3):
        cols = slice(part * D, (part + 1) * D)
        grads_ref[:, cols] = tn(h1p_ref[...], d_qkv[:, cols]).astype(BF)
    turn = hot(iota((D, D), 0) == nat_ref[...])
    d_h1 = nt(nt(d_qkv[...], w_ref[...]).astype(BF), turn)
    x_hat, scale = norm(tok_ref[...].astype(F32))
    d_in, d_gain, d_bias = norm_back(d_h1, x_hat, scale, vec_ref[0:1])
    gx_ref[...] = dxm_ref[...] + d_in
    sub = iota((128, D), 0)
    rows = jnp.where(sub == 16, d_gain, 0.0) + jnp.where(sub == 18, d_bias, 0.0)
    grads_ref[:, 3 * D :] = tn(turn, jnp.transpose(rows).astype(BF)).astype(BF)


def back_two(nat, d_attn, probs, qkv, h1p, d_x_mid, tokens, vec, w):
    vmem = pl.BlockSpec(memory_space=pltpu.VMEM)
    return pl.pallas_call(
        back_two_body,
        grid=(1,),
        in_specs=[vmem] * 8 + [pl.BlockSpec((D, 3 * D), lambda i: (0, 0))],
        out_specs=[vmem] * 2,
        out_shape=[like(ROW, D, dtype=F32), like(D, 3 * D + 128)],
        scratch_shapes=[pltpu.VMEM((ROW, 3 * D), BF)],
        compiler_params=pltpu.CompilerParams(vmem_limit_bytes=56 * MIB),
        cost_estimate=cost(2 * 512 * 768 * 9000, 22 * 10**6),
    )(nat, d_attn, probs, qkv, h1p, d_x_mid, tokens, vec, w)


def merge_body(sid_ref, ret_ref, gate_ref, xmid_ref, out_ref):
    s0, s1 = sid_ref[:, 0:1], sid_ref[:, 1:2]
    y0 = y1 = jnp.zeros((ROW, D), F32)
    for part in range(4):
        slot = iota((ROW, 4 * CAP), 1) + part * 4 * CAP
        values = ret_ref[part * 4 * CAP : (part + 1) * 4 * CAP, :]
        y0 = y0 + nn(hot(slot == s0), values)
        y1 = y1 + nn(hot(slot == s1), values)
    out_ref[...] = (xmid_ref[...] + (gate_ref[:, 0:1] * y0 + gate_ref[:, 1:2] * y1)).astype(BF)


def merge(sid, returned, gate, x_mid):
    return pl.pallas_call(
        merge_body,
        out_shape=like(ROW, D),
        compiler_params=pltpu.CompilerParams(vmem_limit_bytes=40 * MIB),
        cost_estimate=cost(4 * 512 * 1536 * 768, 6 * 10**6),
    )(sid, returned, gate, x_mid)


def shift(value, axis, by):
    count = lax.axis_size(axis)
    return lax.ppermute(value, axis, [(i, (i + by) % count) for i in range(count)])


def ordered(mine, other, index):
    first = jnp.where(index == 0, mine, other)
    second = jnp.where(index == 0, other, mine)
    return first, second


FAR = ("x", "yh", "yl")
PEERS = ("c", "z", "yl")


def to_all(rows, names):
    return lax.all_to_all(rows, names, split_axis=0, concat_axis=0, tiled=True)


def gather_dense(block):
    width = block.shape[1]
    near = to_all(jnp.broadcast_to(block[None], (16, 8, width)), FAR)
    rows = near[:, :6].reshape(96, width)
    return near, rows


def spread(rows):
    pieces = []
    parts = [rows] + [shift(rows, "z", step) for step in (1, 2, 3)]
    for part in parts:
        pieces += [part, shift(part, "c", 1)]
    return pieces


def natural_rows():
    c, z = lax.axis_index("c"), lax.axis_index("z")
    step, other, i = (jnp.arange(768) // 192, (jnp.arange(768) // 96) % 2, jnp.arange(768) % 96)
    core, deep = (c + other) % 2, (z - step) % 4
    return (((i // 12) * 2 + core) * 48 + (deep * 2 + (i // 6) % 2) * 6 + i % 6).astype(jnp.int32)


def scatter_dense(grads):
    width = grads.shape[1]
    parts = grads.reshape(4, 2, 96, width)
    sums = [
        parts[step, 0].astype(F32) + shift(parts[step, 1], "c", 1).astype(F32) for step in range(4)
    ]
    total = sums[0]
    for step in (1, 2, 3):
        total = total + shift(sums[step].astype(BF), "z", -step).astype(F32)
    blocks = jnp.pad(total.astype(BF).reshape(16, 6, width), ((0, 0), (0, 2), (0, 0)))
    return jnp.sum(to_all(blocks, FAR).astype(F32), 0)[:6]


def at(value, index, axis):
    return lax.dynamic_index_in_dim(value, index, axis, False)


def halves(grad):
    parts = grad.reshape(8, 2, grad.shape[0] // 16, grad.shape[1])
    got = lax.ppermute(parts[:, 1], "c", [(0, 1)])
    mine = jnp.where(lax.axis_index("c") == 0, parts[:, 0], got)
    return mine.reshape(4, 2, *mine.shape[1:])


def over_x(mine):
    x = lax.axis_index("x")
    total = at(mine, x, 0).astype(F32)
    for step in (1, 3, 2):
        total = total + shift(at(mine, (x + step) % 4, 0), "x", step).astype(F32)
    return total


def over_y(mine, axis):
    y = lax.axis_index("yh")
    return at(mine, y, axis).astype(F32) + shift(at(mine, 1 - y, axis).astype(BF), "yh", 1).astype(F32)


def shards(
    tokens,
    seq_lengths,
    key_mask,
    routes,
    cotangent,
    qkv_weight,
    out_weight,
    router_weight,
    norm_gains,
    norm_biases,
    up_train,
    down_train,
    up_frozen,
    down_frozen,
):
    core = lax.axis_index("c")

    small = jnp.concatenate((router_weight, norm_gains.T, norm_biases.T), 1)
    block = jnp.concatenate((qkv_weight, out_weight, jnp.pad(small, ((0, 0), (0, 108)))), 1)
    near, rows = gather_dense(jnp.pad(block.astype(BF), ((0, 2), (0, 0))))
    nat = natural_rows().reshape(1, D)

    g_slots, sid, sidt = route(routes, cotangent)
    g_slots, near = lax.optimization_barrier((g_slots, near))
    g_rows = to_all(g_slots.reshape(16, CAP, D), PEERS)

    up_t, down_t = up_train[0].astype(BF), down_train[0].astype(BF)
    up_f, down_f = up_frozen[0], down_frozen[0]
    up_other = shift(jnp.where(core == 0, up_f, up_t), "c", 1)
    down_other = shift(jnp.where(core == 0, down_f, down_t), "c", 1)
    up_two = jnp.concatenate(ordered(jnp.where(core == 0, up_t, up_f), up_other, core), 0)
    down_two = jnp.concatenate(ordered(jnp.where(core == 0, down_t, down_f), down_other, core), 0)
    w_up = lax.all_gather(up_two, ("x", "yh"), tiled=True)
    w_down = lax.all_gather(down_two, ("x", "yh"), tiled=True)

    pieces = spread(rows)
    pieces, g_rows = lax.optimization_barrier((pieces, g_rows))
    w, h1p, qkv, probs, attnp, x_mid, h2, gate, vec, router, sent = forward(
        seq_lengths[0], nat, key_mask.reshape(1, ROW), tokens, sid, sidt, pieces
    )

    arrived = to_all(sent.reshape(16, LINE, D), PEERS)
    out, back, x_rows, d_out, act, d_up = experts(arrived, g_rows, w_up, w_down)
    d_back = to_all(back, PEERS)
    grad_down_l = tn(act, d_out).astype(BF)
    grad_up_l = tn(x_rows, d_up).astype(BF)
    down_mine = halves(grad_down_l)
    up_mine = halves(grad_up_l)
    grad_down = over_x(over_y(down_mine, 1).astype(BF))[None]
    grad_up = over_y(over_x(up_mine), 0)[None]

    out, d_back = lax.optimization_barrier((out, d_back))
    returned = to_all(out, PEERS)
    d_x_mid, d_attn, grads_one = back_one(
        nat, sid, d_back.reshape(16 * LINE, D), gate, router, vec, cotangent, x_mid, h2, attnp, w
    )
    own_one = scatter_dense(grads_one)
    input_grad, grads_two = back_two(nat, d_attn, probs, qkv, h1p, d_x_mid, tokens, vec, w)
    own_two = scatter_dense(grads_two)
    block_out = merge(sid, returned.reshape(16 * CAP, D), gate, x_mid)
    small = own_one[:, D:] + own_two[:, 3 * D :]
    return (
        block_out,
        input_grad,
        own_two[:, : 3 * D],
        own_one[:, :D],
        small[:, :16],
        small[:, 16:18].T,
        small[:, 18:20].T,
        grad_up,
        grad_down,
    )


def solution(mesh):
    fine = Mesh(mesh.devices.reshape(SIZES), NAMES)
    by_row = P(NAMES, None)
    by_column = P(None, NAMES)
    by_expert = P(NARROW, WIDE, None)
    return jax.shard_map(
        shards,
        mesh=fine,
        in_specs=(by_row, by_row, P(NAMES)) + (by_row,) * 5 + (by_column,) * 2 + (by_expert,) * 4,
        out_specs=(by_row,) * 5 + (by_column,) * 2 + (by_expert,) * 2,
        check_vma=False,
    )
```

```python
import jax
import jax.numpy as jnp
from jax import lax
from jax.experimental import pallas as pl
from jax.experimental.pallas import tpu as pltpu
from jax.sharding import Mesh
from jax.sharding import PartitionSpec as P

SIZES = (4, 2, 2, 4, 2)
NAMES = ("x", "yh", "c", "z", "yl")
WIDE = ("x", "yh", "c")
NARROW = ("z", "yl")
BF = jnp.bfloat16
F32 = jnp.float32
ROW = 512
D = 768
FF = 3072
CAP = 96
LINE = 112
SOURCES = 4
GELU_ONE = 0.7978845608028654
GELU_CUBE = GELU_ONE * 0.044715
MIB = 1024 * 1024
SMALL = pl.CostEstimate(flops=10**6, bytes_accessed=10**4, transcendentals=0)


def nn(a, b):
    return jnp.dot(a, b, preferred_element_type=F32)


def nt(a, b):
    return lax.dot_general(a, b, (((1,), (1,)), ((), ())), preferred_element_type=F32)


def tn(a, b):
    return lax.dot_general(a, b, (((0,), (0,)), ((), ())), preferred_element_type=F32)


def iota(shape, dim):
    return lax.broadcasted_iota(jnp.int32, shape, dim)


def hot(mask):
    return jnp.where(mask, 1.0, 0.0).astype(BF)


def like(*dims, dtype=BF):
    return jax.ShapeDtypeStruct(dims, dtype)


def tail_of(line):
    high = line.astype(BF).astype(F32)
    low = (line - high).astype(BF).astype(F32)
    full = jnp.concatenate([high, low, jnp.zeros((1, 512), F32)], 1)
    return jnp.where(iota((16, D), 0) == 0, jnp.broadcast_to(full, (16, D)), 0.0).astype(BF)


def line_of(tail):
    line = tail.astype(F32)[0:1]
    return line[:, :128] + line[:, 128:256]


def norm(x):
    centered = x - jnp.mean(x, -1, keepdims=True)
    scale = lax.rsqrt(jnp.mean(centered * centered, -1, keepdims=True) + 1e-5)
    return centered * scale, scale


def norm_back(d_out, x_hat, scale, gain):
    t = d_out * gain
    d_in = scale * (
        t - jnp.mean(t, -1, keepdims=True) - x_hat * jnp.mean(t * x_hat, -1, keepdims=True)
    )
    return d_in, jnp.sum(d_out * x_hat, 0, keepdims=True), jnp.sum(d_out, 0, keepdims=True)


def route_body(routes_ref, cot_ref, g_ref, sid_ref, sidt_ref):
    lane = iota((ROW, 128), 1)
    r0, r1 = routes_ref[:, 0:1], routes_ref[:, 1:2]
    either = hot((lane == r0) | (lane == r1))
    earlier = nn(hot(iota((ROW, ROW), 1) < iota((ROW, ROW), 0)), either)
    p0 = jnp.sum(jnp.where(lane == r0, earlier, 0.0), 1, keepdims=True).astype(jnp.int32)
    p1 = jnp.sum(jnp.where(lane == r1, earlier, 0.0), 1, keepdims=True).astype(jnp.int32)
    columns = (
        jnp.where(p0 < CAP, r0 * CAP + p0, -1),
        jnp.where(p1 < CAP, r1 * CAP + p1, -1),
        jnp.where(p0 < CAP, r0 * LINE + p0, -1),
        jnp.where(p1 < CAP, r1 * LINE + p1, -1),
        r0,
    )
    table = jnp.broadcast_to(r1, (ROW, 128))
    for at, column in enumerate(columns):
        table = jnp.where(lane == at, column, table)
    sid_ref[...] = table
    turned = jnp.transpose(table.astype(F32))[0:8].astype(jnp.int32)
    sidt_ref[...] = turned
    for part in range(4):
        slot = iota((4 * CAP, ROW), 0) + part * 4 * CAP
        pick = hot((slot == turned[0:1]) | (slot == turned[1:2]))
        g_ref[part * 4 * CAP : (part + 1) * 4 * CAP, :] = nn(pick, cot_ref[...]).astype(BF)


def route(routes, cotangent):
    return pl.pallas_call(
        route_body,
        out_shape=[like(16 * CAP, D), like(ROW, 128, dtype=jnp.int32), like(8, ROW, dtype=jnp.int32)],
        compiler_params=pltpu.CompilerParams(vmem_limit_bytes=32 * MIB),
        cost_estimate=SMALL,
    )(routes, cotangent)


def forward_body(*refs):
    lens_ref, nat_ref, mask_ref, tok_ref, sid_ref, sidt_ref = refs[:6]
    pieces = refs[6:14]
    (
        w_ref, h1p_ref, qkv_ref, probs_ref, attnp_ref, xmid_ref, h2_ref, gate_ref, vec_ref,
        router_ref, sent_ref, rest_ref, attn, bias,
    ) = refs[14:]
    for at, piece in enumerate(pieces):
        w_ref[at * 96 : (at + 1) * 96, :] = piece[:, :FF]
        rest_ref[at * 96 : (at + 1) * 96, :] = piece[:, FF:]
    turn = hot(iota((D, D), 0) == nat_ref[...])
    rest = nn(turn, rest_ref[...])
    vectors = jnp.transpose(rest)[16:24]
    router_ref[...] = rest.astype(BF)
    vec_ref[...] = vectors
    x = tok_ref[...].astype(F32)
    h1 = (norm(x)[0] * vectors[0:1] + vectors[2:3]).astype(BF)
    h1p_ref[...] = nn(h1, turn).astype(BF)
    for part in range(3):
        cols = slice(part * D, (part + 1) * D)
        qkv_ref[:, cols] = nn(h1p_ref[...], w_ref[:, cols]).astype(BF)

    end_one = lens_ref[0]
    end_two = end_one + lens_ref[1]

    def segment(place):
        return (place >= end_one).astype(jnp.int32) + (place >= end_two).astype(jnp.int32)

    query, key = iota((ROW, ROW), 0), iota((ROW, ROW), 1)
    same = segment(iota((ROW, 1), 0)) == segment(iota((1, ROW), 1))
    allowed = same & (key <= query) & ((mask_ref[...] == 1) | (key == query))
    bias[...] = jnp.where(allowed, 0.0, -1e30)
    low = iota((1, 128), 1) < 64
    half = ROW // 2
    zero = jnp.zeros((), BF)

    def pair(index, carry):
        at = pl.multiple_of(index * 128, 128)
        q = qkv_ref[:, pl.ds(at, 128)] * jnp.asarray(0.125, BF)
        k = qkv_ref[:, pl.ds(D + at, 128)]
        v = qkv_ref[:, pl.ds(2 * D + at, 128)]
        out = [None, None]
        for head in range(2):
            mine = low if head == 0 else jnp.logical_not(low)
            k_mine, v_mine = jnp.where(mine, k, zero), jnp.where(mine, v, zero)
            for block in range(2):
                count, rows = half * (block + 1), slice(block * half, (block + 1) * half)
                scores = nt(q[rows], k_mine[:count]) + bias[rows, :count]
                e = jnp.exp(scores - jnp.max(scores, 1, keepdims=True))
                probs = (e * (1.0 / jnp.sum(e, 1, keepdims=True))).astype(BF)
                probs_ref[2 * index + head, rows, :count] = probs
                if block == 0:
                    probs_ref[2 * index + head, rows, count:] = jnp.zeros((half, half), BF)
                term = nn(probs, v_mine[:count])
                out[block] = term if head == 0 else out[block] + term
        for block in range(2):
            attn[block * half : (block + 1) * half, pl.ds(at, 128)] = out[block].astype(BF)
        return carry

    lax.fori_loop(0, 6, pair, 0)
    attnp_ref[...] = nn(attn[...], turn).astype(BF)
    x_mid = x + nn(attnp_ref[...], w_ref[:, 3 * D :])
    xmid_ref[...] = x_mid
    h2 = (norm(x_mid)[0] * vectors[1:2] + vectors[3:4]).astype(BF)
    h2_ref[...] = h2
    logits = nn(h2, router_ref[...])
    lane = iota((ROW, 128), 1)
    s0, s1, r0, r1 = (sid_ref[:, at : at + 1] for at in (0, 1, 4, 5))
    c0 = jnp.sum(jnp.where(lane == r0, logits, 0.0), 1, keepdims=True)
    c1 = jnp.sum(jnp.where(lane == r1, logits, 0.0), 1, keepdims=True)
    g0, g1 = 1.0 / (1.0 + jnp.exp(c1 - c0)), 1.0 / (1.0 + jnp.exp(c0 - c1))
    gate_ref[...] = jnp.where(lane == 0, g0, jnp.where(lane == 1, g1, 0.0))
    first, second = sidt_ref[2:3], sidt_ref[3:4]
    for part in range(4):
        slot = iota((4 * LINE, ROW), 0) + part * 4 * LINE
        pick = hot((slot == first) | (slot == second))
        sent_ref[part * 4 * LINE : (part + 1) * 4 * LINE, :] = nn(pick, h2_ref[...]).astype(BF)
    for expert in range(16):
        slot = lane + expert * CAP
        line = jnp.sum(
            jnp.where(slot == s0, g0, 0.0) + jnp.where(slot == s1, g1, 0.0), 0, keepdims=True
        )
        sent_ref[expert * LINE + CAP : (expert + 1) * LINE, :] = tail_of(line)


def forward(lens, nat, mask, tokens, sid, sidt, pieces):
    vmem = pl.BlockSpec(memory_space=pltpu.VMEM)
    return pl.pallas_call(
        forward_body,
        in_specs=[pl.BlockSpec(memory_space=pltpu.SMEM)] + [vmem] * 13,
        out_shape=[
            like(D, FF),
            like(ROW, D),
            like(ROW, 3 * D),
            like(12, ROW, ROW),
            like(ROW, D),
            like(ROW, D, dtype=F32),
            like(ROW, D),
            like(ROW, 128, dtype=F32),
            like(8, D, dtype=F32),
            like(D, 128),
            like(16 * LINE, D),
        ],
        scratch_shapes=[
            pltpu.VMEM((D, 128), BF),
            pltpu.VMEM((ROW, D), BF),
            pltpu.VMEM((ROW, ROW), F32),
        ],
        compiler_params=pltpu.CompilerParams(vmem_limit_bytes=56 * MIB),
        cost_estimate=SMALL,
    )(lens, nat, mask, tokens, sid, sidt, *pieces)


def expert_body(
    place_ref, sent_ref, g_ref, up_mine, up_other, down_mine, *refs
):
    down_other = refs[:4]
    out_ref, back_ref, x_ref, dout_ref, act_ref, dup_ref, up_ref, down_ref, sems = refs[4:]
    x_place, y_place = place_ref[0], place_ref[1]

    def loads():
        for i in range(4):
            mine, other = 2 * i + y_place, 2 * i + 1 - y_place
            far = 2 * lax.rem(x_place - i + 4, 4) + 1 - y_place
            yield up_mine.at[pl.ds(i * 96, 96), :], up_ref.at[pl.ds(mine * 96, 96), :]
            yield up_other.at[pl.ds(i * 96, 96), :], up_ref.at[pl.ds(other * 96, 96), :]
            yield down_mine.at[pl.ds(i * 384, 384), :], down_ref.at[pl.ds(mine * 384, 384), :]
            yield down_other[i], down_ref.at[pl.ds(far * 384, 384), :]

    @pl.when(pl.program_id(0) == 0)
    def _():
        copies = [
            pltpu.make_async_copy(source, target, sems.at[i])
            for i, (source, target) in enumerate(loads())
        ]
        for copy in copies:
            copy.start()
        for copy in copies:
            copy.wait()

    for s in range(SOURCES):
        first, last = s * CAP, (s + 1) * CAP
        x_ref[first:last, :] = sent_ref[s, :CAP, :]
        gate = line_of(sent_ref[s, CAP:LINE, :])
        column = jnp.transpose(jnp.broadcast_to(gate, (128, 128)))[:CAP, :1]
        dout_ref[first:last, :] = (g_ref[s].astype(F32) * column).astype(BF)
    x, d_out = x_ref[...], dout_ref[...]
    for part in range(FF // 256):
        cols = slice(part * 256, (part + 1) * 256)
        up = nn(x, up_ref[:, cols])
        d_act = nt(d_out, down_ref[cols, :])
        square = up * up
        t = jnp.tanh(up * (GELU_ONE + GELU_CUBE * square))
        a = 0.5 + 0.5 * t
        act_ref[:, cols] = (up * a).astype(BF)
        slope = a + (up * (1.0 - t * t)) * (0.5 * GELU_ONE + 1.5 * GELU_CUBE * square)
        dup_ref[:, cols] = (d_act * slope).astype(BF)
    for part in range(D // 256):
        cols = slice(part * 256, (part + 1) * 256)
        out = nn(act_ref[...], down_ref[:, cols]).astype(BF)
        back = nt(dup_ref[...], up_ref[cols, :]).astype(BF)
        for s in range(SOURCES):
            out_ref[s, :, cols] = out[s * CAP : (s + 1) * CAP]
            back_ref[s, :CAP, cols] = back[s * CAP : (s + 1) * CAP]
    for s in range(SOURCES):
        d_gate = jnp.sum(out_ref[s].astype(F32) * g_ref[s].astype(F32), -1, keepdims=True)
        d_gate = jnp.broadcast_to(d_gate, (CAP, 128))
        wide = jnp.concatenate([d_gate, jnp.zeros((128 - CAP, 128), F32)], 0)
        back_ref[s, CAP:LINE, :] = tail_of(jnp.transpose(wide)[0:1])


def experts(place, sent, g, up_mine, up_other, down_mine, down_other):
    rows = SOURCES * CAP
    anywhere = pl.BlockSpec(memory_space=pl.ANY)
    by_source = lambda size: pl.BlockSpec((SOURCES, size, D), lambda i: (i, 0, 0))
    by_rows = lambda width: pl.BlockSpec((rows, width), lambda i: (i, 0))
    return pl.pallas_call(
        expert_body,
        grid=(16 // SOURCES,),
        in_specs=[
            pl.BlockSpec(memory_space=pltpu.SMEM),
            by_source(LINE),
            by_source(CAP),
        ]
        + [anywhere] * 7,
        out_specs=[
            by_source(CAP), by_source(LINE), by_rows(D), by_rows(D), by_rows(FF), by_rows(FF),
        ],
        out_shape=[
            like(16, CAP, D),
            like(16, LINE, D),
            like(16 * CAP, D),
            like(16 * CAP, D),
            like(16 * CAP, FF),
            like(16 * CAP, FF),
        ],
        scratch_shapes=[
            pltpu.VMEM((D, FF), BF),
            pltpu.VMEM((FF, D), BF),
            pltpu.SemaphoreType.DMA((16,)),
        ],
        compiler_params=pltpu.CompilerParams(vmem_limit_bytes=60 * MIB),
        cost_estimate=SMALL,
    )(place, sent, g, up_mine, up_other, down_mine, *down_other)


def weight_body(x_ref, dout_ref, act_ref, dup_ref, up0_ref, up1_ref, down0_ref, down1_ref):
    up = tn(x_ref[...], dup_ref[...]).astype(BF)
    for block in range(8):
        rows = slice(block * 48, (block + 1) * 48)
        up0_ref[rows, :] = up[block * 96 : block * 96 + 48]
        up1_ref[rows, :] = up[block * 96 + 48 : (block + 1) * 96]
    down = tn(act_ref[...], dout_ref[...]).astype(BF)
    down0_ref[...] = down[:192]
    down1_ref[...] = down[192:]


def weights(x, d_out, act, d_up):
    whole = pl.BlockSpec((16 * CAP, D), lambda i: (0, 0))
    columns = pl.BlockSpec((16 * CAP, 384), lambda i: (0, i))
    up = pl.BlockSpec((384, 384), lambda i: (0, i))
    down = pl.BlockSpec((192, D), lambda i: (i, 0))
    return pl.pallas_call(
        weight_body,
        grid=(8,),
        in_specs=[whole, whole, columns, columns],
        out_specs=[up, up, down, down],
        out_shape=[like(384, FF), like(384, FF), like(1536, D), like(1536, D)],
        compiler_params=pltpu.CompilerParams(vmem_limit_bytes=48 * MIB),
        cost_estimate=SMALL,
    )(x, d_out, act, d_up)


def put_rows(keep_ref, away_ref, cols, values):
    for step in range(4):
        rows = slice(step * 96, (step + 1) * 96)
        keep_ref[rows, cols] = values[step * 192 : step * 192 + 96]
        away_ref[rows, cols] = values[step * 192 + 96 : (step + 1) * 192]


def back_one_body(
    nat_ref, sid_ref, dback_ref, gate_ref, router_ref, vec_ref, cot_ref, xmid_ref, h2_ref,
    attnp_ref, w_ref, dxm_ref, dattn_ref, keep_ref, away_ref,
):
    lane = iota((ROW, 128), 1)
    s0, s1, w0, w1, r0, r1 = (sid_ref[:, at : at + 1] for at in range(6))
    a0 = a1 = jnp.zeros((ROW, 128), F32)
    for expert in range(16):
        line = line_of(dback_ref[expert * LINE + CAP : (expert + 1) * LINE, :])
        slot = jnp.where(lane < CAP, lane + expert * CAP, -2)
        a0 = a0 + jnp.where(slot == s0, line, 0.0)
        a1 = a1 + jnp.where(slot == s1, line, 0.0)
    dg0, dg1 = jnp.sum(a0, 1, keepdims=True), jnp.sum(a1, 1, keepdims=True)
    g0, g1 = gate_ref[:, 0:1], gate_ref[:, 1:2]
    both = g0 * dg0 + g1 * dg1
    d_logits = jnp.where(lane == r0, g0 * (dg0 - both), 0.0)
    d_logits = d_logits + jnp.where(lane == r1, g1 * (dg1 - both), 0.0)
    high = d_logits.astype(BF)
    low = (d_logits - high.astype(F32)).astype(BF)
    d_h2 = nt(high, router_ref[...]) + nt(low, router_ref[...])
    for part in range(4):
        slot = iota((ROW, 4 * LINE), 1) + part * 4 * LINE
        pick = hot((slot == w0) | (slot == w1))
        d_h2 = d_h2 + nn(pick, dback_ref[part * 4 * LINE : (part + 1) * 4 * LINE, :])
    x_hat, scale = norm(xmid_ref[...])
    d_in, d_gain, d_bias = norm_back(d_h2, x_hat, scale, vec_ref[1:2])
    d_x_mid = cot_ref[...].astype(F32) + d_in
    dxm_ref[...] = d_x_mid
    d_proj = d_x_mid.astype(BF)
    turn = hot(iota((D, D), 0) == nat_ref[...])
    dattn_ref[...] = nt(nt(d_proj, w_ref[...]).astype(BF), turn).astype(BF)
    put_rows(keep_ref, away_ref, slice(0, D), tn(attnp_ref[...], d_proj).astype(BF))
    d_router = tn(h2_ref[...], high) + tn(h2_ref[...], low)
    sub = iota((128, D), 0)
    rows = jnp.where(sub == 17, d_gain, 0.0) + jnp.where(sub == 19, d_bias, 0.0)
    small = d_router + jnp.transpose(rows)
    put_rows(keep_ref, away_ref, slice(D, D + 128), tn(turn, small.astype(BF)).astype(BF))


def back_one(nat, sid, d_back, gate, router, vec, cotangent, x_mid, h2, attnp, w):
    vmem = pl.BlockSpec(memory_space=pltpu.VMEM)
    return pl.pallas_call(
        back_one_body,
        grid=(1,),
        in_specs=[vmem] * 10 + [pl.BlockSpec((D, D), lambda i: (0, 3))],
        out_specs=[vmem] * 4,
        out_shape=[like(ROW, D, dtype=F32), like(ROW, D), like(384, D + 128), like(384, D + 128)],
        compiler_params=pltpu.CompilerParams(vmem_limit_bytes=48 * MIB),
        cost_estimate=SMALL,
    )(nat, sid, d_back, gate, router, vec, cotangent, x_mid, h2, attnp, w)


def attention_back(base, dattn_ref, probs_ref, qkv_ref, d_qkv):
    low = iota((1, 128), 1) < 64
    zero = jnp.zeros((), BF)
    half = ROW // 2

    def add(terms, at, term):
        terms[at] = term if terms[at] is None else terms[at] + term

    def pair(index, carry):
        at = pl.multiple_of((base + index) * 128, 128)
        to = pl.multiple_of(index * 128, 128)
        q, k, v = (qkv_ref[:, pl.ds(part * D + at, 128)] for part in range(3))
        d_attn = dattn_ref[:, pl.ds(at, 128)]
        dq, dk, dv = [None, None], [None, None], [None, None]
        for head in range(2):
            mine = low if head == 0 else jnp.logical_not(low)
            q_mine, k_mine, v_mine, d_mine = (jnp.where(mine, t, zero) for t in (q, k, v, d_attn))
            for block in range(2):
                count, rows = half * (block + 1), slice(block * half, (block + 1) * half)
                probs = probs_ref[2 * index + head, rows, :count]
                d_probs = nt(d_mine[rows], v_mine[:count])
                wide = probs.astype(F32)
                weighted = wide * d_probs
                delta = jnp.sum(weighted, 1, keepdims=True)
                d_scores = (weighted - wide * delta).astype(BF)
                add(dq, block, nn(d_scores, k_mine[:count]))
                for other in range(block + 1):
                    keys = slice(other * half, (other + 1) * half)
                    add(dk, other, tn(d_scores[:, keys], q_mine[rows]))
                    add(dv, other, tn(probs[:, keys], d_mine[rows]))
        for block in range(2):
            rows = slice(block * half, (block + 1) * half)
            d_qkv[rows, pl.ds(to, 128)] = (dq[block] * 0.125).astype(BF)
            d_qkv[rows, pl.ds(384 + to, 128)] = (dk[block] * 0.125).astype(BF)
            d_qkv[rows, pl.ds(768 + to, 128)] = dv[block].astype(BF)
        return carry

    lax.fori_loop(0, 3, pair, 0)


def back_two_body(dattn_ref, probs_ref, qkv_ref, h1p_ref, dqkv_ref, keep_ref, away_ref):
    attention_back(0, dattn_ref, probs_ref, qkv_ref, dqkv_ref)
    for part in range(3):
        cols = slice(part * 384, (part + 1) * 384)
        put_rows(keep_ref, away_ref, cols, tn(h1p_ref[...], dqkv_ref[:, cols]).astype(BF))


def back_two(d_attn, probs, qkv, h1p):
    vmem = pl.BlockSpec(memory_space=pltpu.VMEM)
    return pl.pallas_call(
        back_two_body,
        grid=(1,),
        in_specs=[vmem, pl.BlockSpec((6, ROW, ROW), lambda i: (0, 0, 0)), vmem, vmem],
        out_specs=[vmem] * 3,
        out_shape=[like(ROW, 1152), like(384, 1152), like(384, 1152)],
        compiler_params=pltpu.CompilerParams(vmem_limit_bytes=40 * MIB),
        cost_estimate=SMALL,
    )(d_attn, probs, qkv, h1p)


def back_three_body(dattn_ref, probs_ref, qkv_ref, dqkv_ref):
    attention_back(3, dattn_ref, probs_ref, qkv_ref, dqkv_ref)


def back_three(d_attn, probs, qkv):
    vmem = pl.BlockSpec(memory_space=pltpu.VMEM)
    return pl.pallas_call(
        back_three_body,
        grid=(1,),
        in_specs=[vmem, pl.BlockSpec((6, ROW, ROW), lambda i: (1, 0, 0)), vmem],
        out_specs=vmem,
        out_shape=like(ROW, 1152),
        compiler_params=pltpu.CompilerParams(vmem_limit_bytes=40 * MIB),
        cost_estimate=SMALL,
    )(d_attn, probs, qkv)


def back_four_body(
    nat_ref, h1p_ref, first_ref, second_ref, dxm_ref, tok_ref, vec_ref, w_ref,
    gx_ref, keep_ref, away_ref,
):
    d_h1p = jnp.zeros((ROW, D), F32)
    for part in range(3):
        cols = slice(part * 384, (part + 1) * 384)
        d_h1p = d_h1p + nt(first_ref[:, cols], w_ref[:, part * D : part * D + 384])
        d_h1p = d_h1p + nt(second_ref[:, cols], w_ref[:, part * D + 384 : (part + 1) * D])
        put_rows(keep_ref, away_ref, cols, tn(h1p_ref[...], second_ref[:, cols]).astype(BF))
    turn = hot(iota((D, D), 0) == nat_ref[...])
    d_h1 = nt(d_h1p.astype(BF), turn)
    x_hat, scale = norm(tok_ref[...].astype(F32))
    d_in, d_gain, d_bias = norm_back(d_h1, x_hat, scale, vec_ref[0:1])
    gx_ref[...] = dxm_ref[...] + d_in
    sub = iota((128, D), 0)
    rows = jnp.where(sub == 16, d_gain, 0.0) + jnp.where(sub == 18, d_bias, 0.0)
    small = tn(turn, jnp.transpose(rows).astype(BF)).astype(BF)
    put_rows(keep_ref, away_ref, slice(1152, 1280), small)


def back_four(nat, h1p, first, second, d_x_mid, tokens, vec, w):
    vmem = pl.BlockSpec(memory_space=pltpu.VMEM)
    return pl.pallas_call(
        back_four_body,
        grid=(1,),
        in_specs=[vmem] * 7 + [pl.BlockSpec((D, 3 * D), lambda i: (0, 0))],
        out_specs=[vmem] * 3,
        out_shape=[like(ROW, D, dtype=F32), like(384, 1280), like(384, 1280)],
        compiler_params=pltpu.CompilerParams(vmem_limit_bytes=40 * MIB),
        cost_estimate=SMALL,
    )(nat, h1p, first, second, d_x_mid, tokens, vec, w)


def merge_body(sid_ref, ret_ref, gate_ref, xmid_ref, out_ref):
    s0, s1 = sid_ref[:, 0:1], sid_ref[:, 1:2]
    y0 = y1 = jnp.zeros((ROW, D), F32)
    for part in range(4):
        slot = iota((ROW, 4 * CAP), 1) + part * 4 * CAP
        values = ret_ref[part * 4 * CAP : (part + 1) * 4 * CAP, :]
        y0 = y0 + nn(hot(slot == s0), values)
        y1 = y1 + nn(hot(slot == s1), values)
    out_ref[...] = (xmid_ref[...] + (gate_ref[:, 0:1] * y0 + gate_ref[:, 1:2] * y1)).astype(BF)


def merge(sid, returned, gate, x_mid):
    return pl.pallas_call(
        merge_body,
        out_shape=like(ROW, D),
        compiler_params=pltpu.CompilerParams(vmem_limit_bytes=40 * MIB),
        cost_estimate=SMALL,
    )(sid, returned, gate, x_mid)


def to_blocks_body(place_ref, *refs):
    out_ref, total = refs[-2:]
    x, y = place_ref[0], 2 * place_ref[1] + place_ref[2]
    col = 0
    for group in range(3):
        own, parts = refs[4 * group], refs[4 * group + 1 : 4 * group + 4]
        width = own.shape[1]
        value = own[...]
        for part in parts:
            value = value + part[...].astype(F32)
        total[0:96, col : col + width] = value
        col += width
    total[96:104, :] = jnp.zeros((8, col), F32)
    for k in range(16):
        to = lax.rem(x - k % 4 + 4, 4) * 4 + lax.rem(y - k // 4 + 4, 4)
        out_ref[to] = total[6 * k : 6 * k + 8, :].astype(BF)


def to_blocks(place, parts):
    vmem = pl.BlockSpec(memory_space=pltpu.VMEM)
    width = sum(part.shape[1] for part in parts[::4])
    return pl.pallas_call(
        to_blocks_body,
        in_specs=[pl.BlockSpec(memory_space=pltpu.SMEM)] + [vmem] * 12,
        out_shape=like(16, 8, width),
        scratch_shapes=[pltpu.VMEM((104, width), F32)],
        compiler_params=pltpu.CompilerParams(vmem_limit_bytes=24 * MIB),
        cost_estimate=SMALL,
    )(place, *parts)


def from_blocks_body(in_ref, qkv_ref, out_ref, small_ref):
    total = in_ref[0].astype(F32)
    for k in range(1, 16):
        total = total + in_ref[k].astype(F32)
    out_ref[...] = total[:6, :D]
    for part in range(3):
        at = 896 + part * 384
        qkv_ref[:, part * D : part * D + 384] = total[:6, at : at + 384]
        qkv_ref[:, part * D + 384 : (part + 1) * D] = total[:6, at + 1152 : at + 1536]
    small_ref[...] = total[:6, D : D + 128] + total[:6, 3200:3328]


def from_blocks(blocks):
    return pl.pallas_call(
        from_blocks_body,
        out_shape=[like(6, 3 * D, dtype=F32), like(6, D, dtype=F32), like(6, 128, dtype=F32)],
        compiler_params=pltpu.CompilerParams(vmem_limit_bytes=16 * MIB),
        cost_estimate=SMALL,
    )(blocks)


def block_body(qkv_ref, out_ref, small_ref, to_ref):
    to_ref[...] = jnp.zeros(to_ref.shape, BF)
    to_ref[0:6, : 3 * D] = qkv_ref[...].astype(BF)
    to_ref[0:6, 3 * D : FF] = out_ref[...].astype(BF)
    to_ref[0:6, FF : FF + 20] = small_ref[...].astype(BF)


def block_of(qkv, out, small):
    return pl.pallas_call(
        block_body,
        out_shape=like(8, FF + 128),
        compiler_params=pltpu.CompilerParams(vmem_limit_bytes=16 * MIB),
        cost_estimate=SMALL,
    )(qkv, out, small)


def shift(value, axis, by):
    count = lax.axis_size(axis)
    return lax.ppermute(value, axis, [(i, (i + by) % count) for i in range(count)])


def ordered(mine, other, index):
    first = jnp.where(index == 0, mine, other)
    second = jnp.where(index == 0, other, mine)
    return first, second


FAR = ("x", "yh", "yl")
PEERS = ("c", "z", "yl")


def to_all(rows, names):
    return lax.all_to_all(rows, names, split_axis=0, concat_axis=0, tiled=True)


def spread_x(block):
    return jnp.stack([block] + [shift(block, "x", step) for step in (1, 2, 3)])


def spread_y(along_x):
    near = [along_x] + [shift(along_x, ("yh", "yl"), step) for step in (1, 2, 3)]
    return jnp.stack(near)[:, :, :6].reshape(96, along_x.shape[2])


def natural_rows():
    x, c, z = (lax.axis_index(name) for name in ("x", "c", "z"))
    y = lax.axis_index("yh") * 2 + lax.axis_index("yl")
    row = jnp.arange(768)
    step, other, i = row // 192, (row // 96) % 2, row % 96
    core, deep = (c + other) % 2, (z - step) % 4
    high, long = (y - i // 24) % 4, (x - (i // 6) % 4) % 4
    device = ((long * 2 + high // 2) * 2 + core) * 8 + deep * 2 + high % 2
    return (device * 6 + i % 6).astype(jnp.int32)


def over_core(keep, away):
    return (keep.astype(F32) + shift(away, "c", 1).astype(F32)).reshape(4, 96, keep.shape[1])


def along_z(sums):
    return [sums[0]] + [shift(sums[step].astype(BF), "z", -step) for step in (1, 2, 3)]


def at(value, index, axis):
    return lax.dynamic_index_in_dim(value, index, axis, False)


def halves(kept, sent):
    got = lax.ppermute(sent, "c", [(0, 1)])
    mine = jnp.where(lax.axis_index("c") == 0, kept, got)
    return mine.reshape(4, 2, mine.shape[0] // 8, mine.shape[1])


def over_x(mine):
    x = lax.axis_index("x")
    total = at(mine, x, 0).astype(F32)
    for step in (1, 3, 2):
        total = total + shift(at(mine, (x + step) % 4, 0), "x", step).astype(F32)
    return total


def over_y(mine, axis):
    y = lax.axis_index("yh")
    return at(mine, y, axis).astype(F32) + shift(at(mine, 1 - y, axis).astype(BF), "yh", 1).astype(F32)


def shards(
    tokens,
    seq_lengths,
    key_mask,
    routes,
    cotangent,
    qkv_weight,
    out_weight,
    router_weight,
    norm_gains,
    norm_biases,
    up_train,
    down_train,
    up_frozen,
    down_frozen,
):
    core = lax.axis_index("c")

    place = jnp.stack([lax.axis_index(name) for name in ("x", "yh", "yl")]).astype(jnp.int32)

    small = jnp.concatenate((router_weight, norm_gains.T, norm_biases.T), 1)
    block = block_of(qkv_weight, out_weight, small)
    block, routes, up_train, down_train, up_frozen, down_frozen = lax.optimization_barrier(
        (block, routes, up_train, down_train, up_frozen, down_frozen)
    )
    rows = spread_y(spread_x(block))
    nat = natural_rows().reshape(1, D)
    g_slots, sid, sidt = route(routes, cotangent)

    up_t, down_t = up_train[0].astype(BF), down_train[0].astype(BF)

    def for_core(trained, frozen):
        other = shift(jnp.where(core == 0, frozen, trained), "c", 1)
        return jnp.concatenate(ordered(jnp.where(core == 0, trained, frozen), other, core), 0)

    up_two, down_two = for_core(up_t, up_frozen[0]), for_core(down_t, down_frozen[0])
    up_mine = lax.all_gather(up_two, "x", tiled=True)
    down_mine = lax.all_gather(down_two, "x", tiled=True)

    rows, g_slots, up_two, down_two = lax.optimization_barrier((rows, g_slots, up_two, down_two))
    parts = [rows] + [shift(rows, "z", step) for step in (1, 2, 3)]
    up_far, down_far = shift(up_two, "yh", 1), shift(down_two, "yh", 1)
    parts, up_far, down_far, g_slots = lax.optimization_barrier((parts, up_far, down_far, g_slots))
    pieces = []
    for part in parts:
        pieces += [part, shift(part, "c", 1)]
    up_other = lax.all_gather(up_far, "x", tiled=True)
    down_other = [down_far] + [shift(down_far, "x", step) for step in (1, 2, 3)]

    g_rows = to_all(g_slots.reshape(16, CAP, D), PEERS)
    w, h1p, qkv, probs, attnp, x_mid, h2, gate, vec, router, sent = forward(
        seq_lengths[0], nat, key_mask.reshape(1, ROW), tokens, sid, sidt, pieces
    )
    sent, g_rows = lax.optimization_barrier((sent, g_rows))

    arrived = to_all(sent.reshape(16, LINE, D), PEERS)
    out, back, x_rows, d_out, act, d_up = experts(
        place, arrived, g_rows, up_mine, up_other, down_mine, down_other
    )
    d_back = to_all(back, PEERS)
    grads = weights(x_rows, d_out, act, d_up)
    d_back, out, grads = lax.optimization_barrier((d_back, out, grads))

    returned = to_all(out, PEERS)
    down_all = halves(grads[2], grads[3])
    up_all = halves(grads[0], grads[1])
    d_x_mid, d_attn, keep, away = back_one(
        nat, sid, d_back.reshape(16 * LINE, D), gate, router, vec, cotangent, x_mid, h2, attnp, w
    )
    d_attn, down_all, up_all = lax.optimization_barrier((d_attn, down_all, up_all))
    down_half = over_y(down_all, 1).astype(BF)
    up_half = over_x(up_all)
    sums_one = over_core(keep, away)
    first, keep, away = back_two(d_attn, probs, qkv, h1p)
    first, sums_one = lax.optimization_barrier((first, sums_one))
    parts_one = along_z(sums_one)
    sums_two = over_core(keep, away)
    second = back_three(d_attn, probs, qkv)
    second, sums_two, down_half, up_half = lax.optimization_barrier(
        (second, sums_two, down_half, up_half)
    )
    parts_two = along_z(sums_two)
    grad_down = over_x(down_half)[None]
    grad_up = over_y(up_half, 0)[None]
    input_grad, keep, away = back_four(nat, h1p, first, second, d_x_mid, tokens, vec, w)
    keep, away, returned, parts_one, grad_up, grad_down = lax.optimization_barrier(
        (keep, away, returned, parts_one, grad_up, grad_down)
    )
    parts_three = along_z(over_core(keep, away))
    blocks = to_all(to_blocks(place, parts_one + parts_two + parts_three), FAR)
    own_qkv, own_out, small = from_blocks(blocks)
    block_out = merge(sid, returned.reshape(16 * CAP, D), gate, x_mid)
    return (
        block_out,
        input_grad,
        own_qkv,
        own_out,
        small[:, :16],
        small[:, 16:18].T,
        small[:, 18:20].T,
        grad_up,
        grad_down,
    )


def solution(mesh):
    fine = Mesh(mesh.devices.reshape(SIZES), NAMES)
    by_row = P(NAMES, None)
    by_column = P(None, NAMES)
    by_expert = P(NARROW, WIDE, None)
    return jax.shard_map(
        shards,
        mesh=fine,
        in_specs=(by_row, by_row, P(NAMES)) + (by_row,) * 5 + (by_column,) * 2 + (by_expert,) * 4,
        out_specs=(by_row,) * 5 + (by_column,) * 2 + (by_expert,) * 2,
        check_vma=False,
    )
```

```python
import jax
import jax.numpy as jnp
from jax import lax
from jax.experimental import pallas as pl
from jax.experimental.pallas import tpu as pltpu
from jax.sharding import Mesh
from jax.sharding import PartitionSpec as P

SIZES = (4, 2, 2, 4, 2)
NAMES = ("x", "yh", "c", "z", "yl")
WIDE = ("x", "yh", "c")
NARROW = ("z", "yl")
BF = jnp.bfloat16
F32 = jnp.float32
ROW = 512
D = 768
FF = 3072
CAP = 96
LINE = 112
SOURCES = 4
GELU_ONE = 0.7978845608028654
GELU_CUBE = GELU_ONE * 0.044715
MIB = 1024 * 1024
SMALL = pl.CostEstimate(flops=10**6, bytes_accessed=10**4, transcendentals=0)


def nn(a, b):
    return jnp.dot(a, b, preferred_element_type=F32)


def nt(a, b):
    return lax.dot_general(a, b, (((1,), (1,)), ((), ())), preferred_element_type=F32)


def tn(a, b):
    return lax.dot_general(a, b, (((0,), (0,)), ((), ())), preferred_element_type=F32)


def iota(shape, dim):
    return lax.broadcasted_iota(jnp.int32, shape, dim)


def hot(mask):
    return jnp.where(mask, 1.0, 0.0).astype(BF)


def like(*dims, dtype=BF):
    return jax.ShapeDtypeStruct(dims, dtype)


def tail_of(line):
    high = line.astype(BF).astype(F32)
    low = (line - high).astype(BF).astype(F32)
    full = jnp.concatenate([high, low, jnp.zeros((1, 512), F32)], 1)
    return jnp.where(iota((16, D), 0) == 0, jnp.broadcast_to(full, (16, D)), 0.0).astype(BF)


def line_of(tail):
    line = tail.astype(F32)[0:1]
    return line[:, :128] + line[:, 128:256]


def norm(x):
    centered = x - jnp.mean(x, -1, keepdims=True)
    scale = lax.rsqrt(jnp.mean(centered * centered, -1, keepdims=True) + 1e-5)
    return centered * scale, scale


def norm_back(d_out, x_hat, scale, gain):
    t = d_out * gain
    d_in = scale * (
        t - jnp.mean(t, -1, keepdims=True) - x_hat * jnp.mean(t * x_hat, -1, keepdims=True)
    )
    return d_in, jnp.sum(d_out * x_hat, 0, keepdims=True), jnp.sum(d_out, 0, keepdims=True)


def route_body(routes_ref, cot_ref, g_ref, sid_ref, sidt_ref):
    lane = iota((ROW, 128), 1)
    r0, r1 = routes_ref[:, 0:1], routes_ref[:, 1:2]
    either = hot((lane == r0) | (lane == r1))
    earlier = nn(hot(iota((ROW, ROW), 1) < iota((ROW, ROW), 0)), either)
    p0 = jnp.sum(jnp.where(lane == r0, earlier, 0.0), 1, keepdims=True).astype(jnp.int32)
    p1 = jnp.sum(jnp.where(lane == r1, earlier, 0.0), 1, keepdims=True).astype(jnp.int32)
    columns = (
        jnp.where(p0 < CAP, r0 * CAP + p0, -1),
        jnp.where(p1 < CAP, r1 * CAP + p1, -1),
        jnp.where(p0 < CAP, r0 * LINE + p0, -1),
        jnp.where(p1 < CAP, r1 * LINE + p1, -1),
        r0,
    )
    table = jnp.broadcast_to(r1, (ROW, 128))
    for at, column in enumerate(columns):
        table = jnp.where(lane == at, column, table)
    sid_ref[...] = table
    turned = jnp.transpose(table.astype(F32))[0:8].astype(jnp.int32)
    sidt_ref[...] = turned
    for part in range(4):
        slot = iota((4 * CAP, ROW), 0) + part * 4 * CAP
        pick = hot((slot == turned[0:1]) | (slot == turned[1:2]))
        g_ref[part * 4 * CAP : (part + 1) * 4 * CAP, :] = nn(pick, cot_ref[...]).astype(BF)


def route(routes, cotangent):
    return pl.pallas_call(
        route_body,
        out_shape=[like(16 * CAP, D), like(ROW, 128, dtype=jnp.int32), like(8, ROW, dtype=jnp.int32)],
        compiler_params=pltpu.CompilerParams(vmem_limit_bytes=32 * MIB),
        cost_estimate=SMALL,
    )(routes, cotangent)


def forward_body(*refs):
    lens_ref, nat_ref, mask_ref, tok_ref, sid_ref, sidt_ref = refs[:6]
    pieces = refs[6:14]
    (
        w_ref, h1p_ref, qkv_ref, probs_ref, attnp_ref, xmid_ref, h2_ref, gate_ref, vec_ref,
        router_ref, sent_ref, rest_ref, attn, bias,
    ) = refs[14:]
    for at, piece in enumerate(pieces):
        w_ref[at * 96 : (at + 1) * 96, :] = piece[:, :FF]
        rest_ref[at * 96 : (at + 1) * 96, :] = piece[:, FF:]
    turn = hot(iota((D, D), 0) == nat_ref[...])
    rest = nn(turn, rest_ref[...])
    vectors = jnp.transpose(rest)[16:24]
    router_ref[...] = rest.astype(BF)
    vec_ref[...] = vectors
    x = tok_ref[...].astype(F32)
    h1 = (norm(x)[0] * vectors[0:1] + vectors[2:3]).astype(BF)
    h1p_ref[...] = nn(h1, turn).astype(BF)
    for part in range(3):
        cols = slice(part * D, (part + 1) * D)
        qkv_ref[:, cols] = nn(h1p_ref[...], w_ref[:, cols]).astype(BF)

    end_one = lens_ref[0]
    end_two = end_one + lens_ref[1]

    def segment(place):
        return (place >= end_one).astype(jnp.int32) + (place >= end_two).astype(jnp.int32)

    query, key = iota((ROW, ROW), 0), iota((ROW, ROW), 1)
    same = segment(iota((ROW, 1), 0)) == segment(iota((1, ROW), 1))
    allowed = same & (key <= query) & ((mask_ref[...] == 1) | (key == query))
    bias[...] = jnp.where(allowed, 0.0, -1e30)
    low = iota((1, 128), 1) < 64
    half = ROW // 2
    zero = jnp.zeros((), BF)

    def pair(index, carry):
        at = pl.multiple_of(index * 128, 128)
        q = qkv_ref[:, pl.ds(at, 128)] * jnp.asarray(0.125, BF)
        k = qkv_ref[:, pl.ds(D + at, 128)]
        v = qkv_ref[:, pl.ds(2 * D + at, 128)]
        out = [None, None]
        for head in range(2):
            mine = low if head == 0 else jnp.logical_not(low)
            k_mine, v_mine = jnp.where(mine, k, zero), jnp.where(mine, v, zero)
            for block in range(2):
                count, rows = half * (block + 1), slice(block * half, (block + 1) * half)
                scores = nt(q[rows], k_mine[:count]) + bias[rows, :count]
                e = jnp.exp(scores - jnp.max(scores, 1, keepdims=True))
                probs = (e * (1.0 / jnp.sum(e, 1, keepdims=True))).astype(BF)
                probs_ref[2 * index + head, rows, :count] = probs
                if block == 0:
                    probs_ref[2 * index + head, rows, count:] = jnp.zeros((half, half), BF)
                term = nn(probs, v_mine[:count])
                out[block] = term if head == 0 else out[block] + term
        for block in range(2):
            attn[block * half : (block + 1) * half, pl.ds(at, 128)] = out[block].astype(BF)
        return carry

    lax.fori_loop(0, 6, pair, 0)
    attnp_ref[...] = nn(attn[...], turn).astype(BF)
    x_mid = x + nn(attnp_ref[...], w_ref[:, 3 * D :])
    xmid_ref[...] = x_mid
    h2 = (norm(x_mid)[0] * vectors[1:2] + vectors[3:4]).astype(BF)
    h2_ref[...] = h2
    logits = nn(h2, router_ref[...])
    lane = iota((ROW, 128), 1)
    s0, s1, r0, r1 = (sid_ref[:, at : at + 1] for at in (0, 1, 4, 5))
    c0 = jnp.sum(jnp.where(lane == r0, logits, 0.0), 1, keepdims=True)
    c1 = jnp.sum(jnp.where(lane == r1, logits, 0.0), 1, keepdims=True)
    g0, g1 = 1.0 / (1.0 + jnp.exp(c1 - c0)), 1.0 / (1.0 + jnp.exp(c0 - c1))
    gate_ref[...] = jnp.where(lane == 0, g0, jnp.where(lane == 1, g1, 0.0))
    first, second = sidt_ref[2:3], sidt_ref[3:4]
    for part in range(4):
        slot = iota((4 * LINE, ROW), 0) + part * 4 * LINE
        pick = hot((slot == first) | (slot == second))
        sent_ref[part * 4 * LINE : (part + 1) * 4 * LINE, :] = nn(pick, h2_ref[...]).astype(BF)
    for expert in range(16):
        slot = lane + expert * CAP
        line = jnp.sum(
            jnp.where(slot == s0, g0, 0.0) + jnp.where(slot == s1, g1, 0.0), 0, keepdims=True
        )
        sent_ref[expert * LINE + CAP : (expert + 1) * LINE, :] = tail_of(line)


def forward(lens, nat, mask, tokens, sid, sidt, pieces):
    vmem = pl.BlockSpec(memory_space=pltpu.VMEM)
    return pl.pallas_call(
        forward_body,
        in_specs=[pl.BlockSpec(memory_space=pltpu.SMEM)] + [vmem] * 13,
        out_shape=[
            like(D, FF),
            like(ROW, D),
            like(ROW, 3 * D),
            like(12, ROW, ROW),
            like(ROW, D),
            like(ROW, D, dtype=F32),
            like(ROW, D),
            like(ROW, 128, dtype=F32),
            like(8, D, dtype=F32),
            like(D, 128),
            like(16 * LINE, D),
        ],
        scratch_shapes=[
            pltpu.VMEM((D, 128), BF),
            pltpu.VMEM((ROW, D), BF),
            pltpu.VMEM((ROW, ROW), F32),
        ],
        compiler_params=pltpu.CompilerParams(vmem_limit_bytes=56 * MIB),
        cost_estimate=SMALL,
    )(lens, nat, mask, tokens, sid, sidt, *pieces)


def expert_body(
    place_ref, sent_ref, g_ref, up_mine, up_other, down_mine, *refs
):
    down_other = refs[:4]
    out_ref, back_ref, x_ref, dout_ref, act_ref, dup_ref, up_ref, down_ref, sems = refs[4:]
    x_place, y_place = place_ref[0], place_ref[1]

    def loads():
        for i in range(4):
            mine, other = 2 * i + y_place, 2 * i + 1 - y_place
            far = 2 * lax.rem(x_place - i + 4, 4) + 1 - y_place
            yield up_mine.at[pl.ds(i * 96, 96), :], up_ref.at[pl.ds(mine * 96, 96), :]
            yield up_other.at[pl.ds(i * 96, 96), :], up_ref.at[pl.ds(other * 96, 96), :]
            yield down_mine.at[pl.ds(i * 384, 384), :], down_ref.at[pl.ds(mine * 384, 384), :]
            yield down_other[i], down_ref.at[pl.ds(far * 384, 384), :]

    @pl.when(pl.program_id(0) == 0)
    def _():
        copies = [
            pltpu.make_async_copy(source, target, sems.at[i])
            for i, (source, target) in enumerate(loads())
        ]
        for copy in copies:
            copy.start()
        for copy in copies:
            copy.wait()

    for s in range(SOURCES):
        first, last = s * CAP, (s + 1) * CAP
        x_ref[first:last, :] = sent_ref[s, :CAP, :]
        gate = line_of(sent_ref[s, CAP:LINE, :])
        column = jnp.transpose(jnp.broadcast_to(gate, (128, 128)))[:CAP, :1]
        dout_ref[first:last, :] = (g_ref[s].astype(F32) * column).astype(BF)
    x, d_out = x_ref[...], dout_ref[...]
    for part in range(FF // 256):
        cols = slice(part * 256, (part + 1) * 256)
        up = nn(x, up_ref[:, cols])
        d_act = nt(d_out, down_ref[cols, :])
        square = up * up
        t = jnp.tanh(up * (GELU_ONE + GELU_CUBE * square))
        a = 0.5 + 0.5 * t
        act_ref[:, cols] = (up * a).astype(BF)
        slope = a + (up * (1.0 - t * t)) * (0.5 * GELU_ONE + 1.5 * GELU_CUBE * square)
        dup_ref[:, cols] = (d_act * slope).astype(BF)
    for part in range(D // 256):
        cols = slice(part * 256, (part + 1) * 256)
        out = nn(act_ref[...], down_ref[:, cols]).astype(BF)
        back = nt(dup_ref[...], up_ref[cols, :]).astype(BF)
        for s in range(SOURCES):
            out_ref[s, :, cols] = out[s * CAP : (s + 1) * CAP]
            back_ref[s, :CAP, cols] = back[s * CAP : (s + 1) * CAP]
    for s in range(SOURCES):
        d_gate = jnp.sum(out_ref[s].astype(F32) * g_ref[s].astype(F32), -1, keepdims=True)
        d_gate = jnp.broadcast_to(d_gate, (CAP, 128))
        wide = jnp.concatenate([d_gate, jnp.zeros((128 - CAP, 128), F32)], 0)
        back_ref[s, CAP:LINE, :] = tail_of(jnp.transpose(wide)[0:1])


def experts(place, sent, g, up_mine, up_other, down_mine, down_other):
    rows = SOURCES * CAP
    anywhere = pl.BlockSpec(memory_space=pl.ANY)
    by_source = lambda size: pl.BlockSpec((SOURCES, size, D), lambda i: (i, 0, 0))
    by_rows = lambda width: pl.BlockSpec((rows, width), lambda i: (i, 0))
    return pl.pallas_call(
        expert_body,
        grid=(16 // SOURCES,),
        in_specs=[
            pl.BlockSpec(memory_space=pltpu.SMEM),
            by_source(LINE),
            by_source(CAP),
        ]
        + [anywhere] * 7,
        out_specs=[
            by_source(CAP), by_source(LINE), by_rows(D), by_rows(D), by_rows(FF), by_rows(FF),
        ],
        out_shape=[
            like(16, CAP, D),
            like(16, LINE, D),
            like(16 * CAP, D),
            like(16 * CAP, D),
            like(16 * CAP, FF),
            like(16 * CAP, FF),
        ],
        scratch_shapes=[
            pltpu.VMEM((D, FF), BF),
            pltpu.VMEM((FF, D), BF),
            pltpu.SemaphoreType.DMA((16,)),
        ],
        compiler_params=pltpu.CompilerParams(vmem_limit_bytes=60 * MIB),
        cost_estimate=SMALL,
    )(place, sent, g, up_mine, up_other, down_mine, *down_other)


def weight_body(x_ref, dout_ref, act_ref, dup_ref, *refs):
    up_refs, down_refs = refs[:3], refs[3:]
    up = tn(x_ref[...], dup_ref[...]).astype(BF)
    for block in range(8):
        rows, low = block * 96, (block % 4) * 48
        up_refs[0][block * 48 : (block + 1) * 48, :] = up[rows : rows + 48]
        up_refs[1 + block // 4][low : low + 48, :] = up[rows + 48 : rows + 96]
    down = tn(act_ref[...], dout_ref[...]).astype(BF)
    down_refs[0][...] = down[:192]
    for part in range(2):

        @pl.when(pl.program_id(0) // 4 == part)
        def _():
            down_refs[1 + part][...] = down[192:]


def weights(x, d_out, act, d_up):
    whole = pl.BlockSpec((16 * CAP, D), lambda i: (0, 0))
    columns = pl.BlockSpec((16 * CAP, 384), lambda i: (0, i))
    up = lambda rows: pl.BlockSpec((rows, 384), lambda i: (0, i))
    down = lambda index: pl.BlockSpec((192, D), index)
    return pl.pallas_call(
        weight_body,
        grid=(8,),
        in_specs=[whole, whole, columns, columns],
        out_specs=[
            up(384),
            up(192),
            up(192),
            down(lambda i: (i, 0)),
            down(lambda i: (jnp.minimum(i, 3), 0)),
            down(lambda i: (jnp.maximum(i - 4, 0), 0)),
        ],
        out_shape=[
            like(384, FF), like(192, FF), like(192, FF), like(1536, D), like(768, D), like(768, D),
        ],
        compiler_params=pltpu.CompilerParams(vmem_limit_bytes=48 * MIB),
        cost_estimate=SMALL,
    )(x, d_out, act, d_up)


def put_rows(keep_ref, away_ref, cols, values):
    for step in range(4):
        rows = slice(step * 96, (step + 1) * 96)
        keep_ref[rows, cols] = values[step * 192 : step * 192 + 96]
        away_ref[rows, cols] = values[step * 192 + 96 : (step + 1) * 192]


def back_one_body(
    nat_ref, sid_ref, dback_ref, gate_ref, router_ref, vec_ref, cot_ref, xmid_ref, h2_ref,
    attnp_ref, w_ref, dxm_ref, dattn_ref, keep_ref, away_ref,
):
    lane = iota((ROW, 128), 1)
    s0, s1, w0, w1, r0, r1 = (sid_ref[:, at : at + 1] for at in range(6))
    a0 = a1 = jnp.zeros((ROW, 128), F32)
    for expert in range(16):
        line = line_of(dback_ref[expert * LINE + CAP : (expert + 1) * LINE, :])
        slot = jnp.where(lane < CAP, lane + expert * CAP, -2)
        a0 = a0 + jnp.where(slot == s0, line, 0.0)
        a1 = a1 + jnp.where(slot == s1, line, 0.0)
    dg0, dg1 = jnp.sum(a0, 1, keepdims=True), jnp.sum(a1, 1, keepdims=True)
    g0, g1 = gate_ref[:, 0:1], gate_ref[:, 1:2]
    both = g0 * dg0 + g1 * dg1
    d_logits = jnp.where(lane == r0, g0 * (dg0 - both), 0.0)
    d_logits = d_logits + jnp.where(lane == r1, g1 * (dg1 - both), 0.0)
    high = d_logits.astype(BF)
    low = (d_logits - high.astype(F32)).astype(BF)
    d_h2 = nt(high, router_ref[...]) + nt(low, router_ref[...])
    for part in range(4):
        slot = iota((ROW, 4 * LINE), 1) + part * 4 * LINE
        pick = hot((slot == w0) | (slot == w1))
        d_h2 = d_h2 + nn(pick, dback_ref[part * 4 * LINE : (part + 1) * 4 * LINE, :])
    x_hat, scale = norm(xmid_ref[...])
    d_in, d_gain, d_bias = norm_back(d_h2, x_hat, scale, vec_ref[1:2])
    d_x_mid = cot_ref[...].astype(F32) + d_in
    dxm_ref[...] = d_x_mid
    d_proj = d_x_mid.astype(BF)
    turn = hot(iota((D, D), 0) == nat_ref[...])
    dattn_ref[...] = nt(nt(d_proj, w_ref[...]).astype(BF), turn).astype(BF)
    put_rows(keep_ref, away_ref, slice(0, D), tn(attnp_ref[...], d_proj).astype(BF))
    d_router = tn(h2_ref[...], high) + tn(h2_ref[...], low)
    sub = iota((128, D), 0)
    rows = jnp.where(sub == 17, d_gain, 0.0) + jnp.where(sub == 19, d_bias, 0.0)
    small = d_router + jnp.transpose(rows)
    put_rows(keep_ref, away_ref, slice(D, D + 128), tn(turn, small.astype(BF)).astype(BF))


def back_one(nat, sid, d_back, gate, router, vec, cotangent, x_mid, h2, attnp, w):
    vmem = pl.BlockSpec(memory_space=pltpu.VMEM)
    return pl.pallas_call(
        back_one_body,
        grid=(1,),
        in_specs=[vmem] * 10 + [pl.BlockSpec((D, D), lambda i: (0, 3))],
        out_specs=[vmem] * 4,
        out_shape=[like(ROW, D, dtype=F32), like(ROW, D), like(384, D + 128), like(384, D + 128)],
        compiler_params=pltpu.CompilerParams(vmem_limit_bytes=48 * MIB),
        cost_estimate=SMALL,
    )(nat, sid, d_back, gate, router, vec, cotangent, x_mid, h2, attnp, w)


def attention_back(base, pairs, dattn_ref, probs_ref, qkv_ref, d_qkv):
    width = 128 * pairs
    low = iota((1, 128), 1) < 64
    zero = jnp.zeros((), BF)
    half = ROW // 2

    def add(terms, at, term):
        terms[at] = term if terms[at] is None else terms[at] + term

    def pair(index, carry):
        at = pl.multiple_of((base + index) * 128, 128)
        to = pl.multiple_of(index * 128, 128)
        q, k, v = (qkv_ref[:, pl.ds(part * D + at, 128)] for part in range(3))
        d_attn = dattn_ref[:, pl.ds(at, 128)]
        dq, dk, dv = [None, None], [None, None], [None, None]
        for head in range(2):
            mine = low if head == 0 else jnp.logical_not(low)
            q_mine, k_mine, v_mine, d_mine = (jnp.where(mine, t, zero) for t in (q, k, v, d_attn))
            for block in range(2):
                count, rows = half * (block + 1), slice(block * half, (block + 1) * half)
                probs = probs_ref[2 * index + head, rows, :count]
                d_probs = nt(d_mine[rows], v_mine[:count])
                wide = probs.astype(F32)
                weighted = wide * d_probs
                delta = jnp.sum(weighted, 1, keepdims=True)
                d_scores = (weighted - wide * delta).astype(BF)
                add(dq, block, nn(d_scores, k_mine[:count]))
                for other in range(block + 1):
                    keys = slice(other * half, (other + 1) * half)
                    add(dk, other, tn(d_scores[:, keys], q_mine[rows]))
                    add(dv, other, tn(probs[:, keys], d_mine[rows]))
        for block in range(2):
            rows = slice(block * half, (block + 1) * half)
            d_qkv[rows, pl.ds(to, 128)] = (dq[block] * 0.125).astype(BF)
            d_qkv[rows, pl.ds(width + to, 128)] = (dk[block] * 0.125).astype(BF)
            d_qkv[rows, pl.ds(2 * width + to, 128)] = dv[block].astype(BF)
        return carry

    lax.fori_loop(0, pairs, pair, 0)


def back_two_body(dattn_ref, probs_ref, qkv_ref, h1p_ref, dqkv_ref, keep_ref, away_ref):
    attention_back(0, 4, dattn_ref, probs_ref, qkv_ref, dqkv_ref)
    for part in range(3):
        cols = slice(part * 512, (part + 1) * 512)
        put_rows(keep_ref, away_ref, cols, tn(h1p_ref[...], dqkv_ref[:, cols]).astype(BF))


def back_two(d_attn, probs, qkv, h1p):
    vmem = pl.BlockSpec(memory_space=pltpu.VMEM)
    return pl.pallas_call(
        back_two_body,
        grid=(1,),
        in_specs=[vmem, pl.BlockSpec((8, ROW, ROW), lambda i: (0, 0, 0)), vmem, vmem],
        out_specs=[vmem] * 3,
        out_shape=[like(ROW, 1536), like(384, 1536), like(384, 1536)],
        compiler_params=pltpu.CompilerParams(vmem_limit_bytes=40 * MIB),
        cost_estimate=SMALL,
    )(d_attn, probs, qkv, h1p)


def back_three_body(dattn_ref, probs_ref, qkv_ref, h1p_ref, dqkv_ref, keep_ref, away_ref):
    attention_back(4, 2, dattn_ref, probs_ref, qkv_ref, dqkv_ref)
    for part in range(3):
        cols = slice(part * 256, (part + 1) * 256)
        put_rows(keep_ref, away_ref, cols, tn(h1p_ref[...], dqkv_ref[:, cols]).astype(BF))


def back_three(d_attn, probs, qkv, h1p):
    vmem = pl.BlockSpec(memory_space=pltpu.VMEM)
    return pl.pallas_call(
        back_three_body,
        grid=(1,),
        in_specs=[vmem, pl.BlockSpec((4, ROW, ROW), lambda i: (2, 0, 0)), vmem, vmem],
        out_specs=[vmem] * 3,
        out_shape=[like(ROW, 768), like(384, 768), like(384, 768)],
        compiler_params=pltpu.CompilerParams(vmem_limit_bytes=40 * MIB),
        cost_estimate=SMALL,
    )(d_attn, probs, qkv, h1p)


def back_four_body(
    nat_ref, first_ref, second_ref, dxm_ref, tok_ref, vec_ref, w_ref, gx_ref, keep_ref, away_ref
):
    d_h1p = jnp.zeros((ROW, D), F32)
    for part in range(3):
        middle = part * D + 512
        d_h1p = d_h1p + nt(first_ref[:, part * 512 : (part + 1) * 512], w_ref[:, part * D : middle])
        d_h1p = d_h1p + nt(
            second_ref[:, part * 256 : (part + 1) * 256], w_ref[:, middle : (part + 1) * D]
        )
    turn = hot(iota((D, D), 0) == nat_ref[...])
    d_h1 = nt(d_h1p.astype(BF), turn)
    x_hat, scale = norm(tok_ref[...].astype(F32))
    d_in, d_gain, d_bias = norm_back(d_h1, x_hat, scale, vec_ref[0:1])
    gx_ref[...] = dxm_ref[...] + d_in
    sub = iota((128, D), 0)
    rows = jnp.where(sub == 16, d_gain, 0.0) + jnp.where(sub == 18, d_bias, 0.0)
    small = tn(turn, jnp.transpose(rows).astype(BF)).astype(BF)
    put_rows(keep_ref, away_ref, slice(0, 128), small)


def back_four(nat, first, second, d_x_mid, tokens, vec, w):
    vmem = pl.BlockSpec(memory_space=pltpu.VMEM)
    return pl.pallas_call(
        back_four_body,
        grid=(1,),
        in_specs=[vmem] * 6 + [pl.BlockSpec((D, 3 * D), lambda i: (0, 0))],
        out_specs=[vmem] * 3,
        out_shape=[like(ROW, D, dtype=F32), like(384, 128), like(384, 128)],
        compiler_params=pltpu.CompilerParams(vmem_limit_bytes=40 * MIB),
        cost_estimate=SMALL,
    )(nat, first, second, d_x_mid, tokens, vec, w)


def merge_body(sid_ref, ret_ref, gate_ref, xmid_ref, out_ref):
    s0, s1 = sid_ref[:, 0:1], sid_ref[:, 1:2]
    y0 = y1 = jnp.zeros((ROW, D), F32)
    for part in range(4):
        slot = iota((ROW, 4 * CAP), 1) + part * 4 * CAP
        values = ret_ref[part * 4 * CAP : (part + 1) * 4 * CAP, :]
        y0 = y0 + nn(hot(slot == s0), values)
        y1 = y1 + nn(hot(slot == s1), values)
    out_ref[...] = (xmid_ref[...] + (gate_ref[:, 0:1] * y0 + gate_ref[:, 1:2] * y1)).astype(BF)


def merge(sid, returned, gate, x_mid):
    return pl.pallas_call(
        merge_body,
        out_shape=like(ROW, D),
        compiler_params=pltpu.CompilerParams(vmem_limit_bytes=40 * MIB),
        cost_estimate=SMALL,
    )(sid, returned, gate, x_mid)


def to_blocks_body(place_ref, *refs):
    out_ref, total = refs[-2:]
    parts, col = refs[:-2], 0
    for group in range(len(parts) // 4):
        value = parts[4 * group][...]
        for part in parts[4 * group + 1 : 4 * group + 4]:
            value = value + part[...].astype(F32)
        total[0:96, col : col + value.shape[1]] = value
        col += value.shape[1]
    total[96:104, :] = jnp.zeros((8, col), F32)
    x, y = place_ref[0], 2 * place_ref[1] + place_ref[2]
    for k in range(16):
        to = lax.rem(x - k % 4 + 4, 4) * 4 + lax.rem(y - k // 4 + 4, 4)
        out_ref[to] = total[6 * k : 6 * k + 8, :].astype(BF)


def to_blocks(place, parts):
    vmem = pl.BlockSpec(memory_space=pltpu.VMEM)
    width = sum(part.shape[1] for part in parts[::4])
    return pl.pallas_call(
        to_blocks_body,
        in_specs=[pl.BlockSpec(memory_space=pltpu.SMEM)] + [vmem] * len(parts),
        out_shape=like(16, 8, width),
        scratch_shapes=[pltpu.VMEM((104, width), F32)],
        compiler_params=pltpu.CompilerParams(vmem_limit_bytes=24 * MIB),
        cost_estimate=SMALL,
    )(place, *parts)


def from_blocks_body(in_ref, qkv_ref, out_ref, small_ref):
    total = in_ref[0].astype(F32)
    for k in range(1, 16):
        total = total + in_ref[k].astype(F32)
    out_ref[...] = total[:6, :D]
    for part in range(3):
        qkv_ref[:, part * D : part * D + 512] = total[:6, 896 + part * 512 : 1408 + part * 512]
        qkv_ref[:, part * D + 512 : (part + 1) * D] = total[:6, 2432 + part * 256 : 2688 + part * 256]
    small_ref[...] = total[:6, D : D + 128] + total[:6, 3200:3328]


def from_blocks(blocks):
    return pl.pallas_call(
        from_blocks_body,
        out_shape=[like(6, 3 * D, dtype=F32), like(6, D, dtype=F32), like(6, 128, dtype=F32)],
        compiler_params=pltpu.CompilerParams(vmem_limit_bytes=16 * MIB),
        cost_estimate=SMALL,
    )(blocks)


def block_body(qkv_ref, out_ref, small_ref, to_ref):
    to_ref[...] = jnp.zeros(to_ref.shape, BF)
    to_ref[0:6, : 3 * D] = qkv_ref[...].astype(BF)
    to_ref[0:6, 3 * D : FF] = out_ref[...].astype(BF)
    to_ref[0:6, FF : FF + 20] = small_ref[...].astype(BF)


def block_of(qkv, out, small):
    return pl.pallas_call(
        block_body,
        out_shape=like(8, FF + 128),
        compiler_params=pltpu.CompilerParams(vmem_limit_bytes=16 * MIB),
        cost_estimate=SMALL,
    )(qkv, out, small)


def shift(value, axis, by):
    count = lax.axis_size(axis)
    return lax.ppermute(value, axis, [(i, (i + by) % count) for i in range(count)])


def ordered(mine, other, index):
    first = jnp.where(index == 0, mine, other)
    second = jnp.where(index == 0, other, mine)
    return first, second


FAR = ("x", "yh", "yl")
PEERS = ("c", "z", "yl")


def to_all(rows, names):
    return lax.all_to_all(rows, names, split_axis=0, concat_axis=0, tiled=True)


def spread_x(block):
    return jnp.stack([block] + [shift(block, "x", step) for step in (1, 2, 3)])


def spread_y(along_x):
    near = [along_x] + [shift(along_x, ("yh", "yl"), step) for step in (1, 2, 3)]
    return jnp.stack(near)[:, :, :6].reshape(96, along_x.shape[2])


def natural_rows():
    x, c, z = (lax.axis_index(name) for name in ("x", "c", "z"))
    y = lax.axis_index("yh") * 2 + lax.axis_index("yl")
    row = jnp.arange(768)
    step, other, i = row // 192, (row // 96) % 2, row % 96
    core, deep = (c + other) % 2, (z - step) % 4
    high, long = (y - i // 24) % 4, (x - (i // 6) % 4) % 4
    device = ((long * 2 + high // 2) * 2 + core) * 8 + deep * 2 + high % 2
    return (device * 6 + i % 6).astype(jnp.int32)


def over_core(keep, away):
    return (keep.astype(F32) + shift(away, "c", 1).astype(F32)).reshape(4, 96, keep.shape[1])


def along_z(sums):
    return [sums[0]] + [shift(sums[step].astype(BF), "z", -step) for step in (1, 2, 3)]


def halves(kept, *sent):
    got = [lax.ppermute(part, "c", [(0, 1)]) for part in sent]
    return jnp.where(lax.axis_index("c") == 0, kept, jnp.concatenate(got, 0))


def owned(mine, axis):
    return lax.psum_scatter(mine, axis, scatter_dimension=0, tiled=True)


def shards(
    tokens,
    seq_lengths,
    key_mask,
    routes,
    cotangent,
    qkv_weight,
    out_weight,
    router_weight,
    norm_gains,
    norm_biases,
    up_train,
    down_train,
    up_frozen,
    down_frozen,
):
    core = lax.axis_index("c")

    place = jnp.stack([lax.axis_index(name) for name in ("x", "yh", "yl")]).astype(jnp.int32)

    small = jnp.concatenate((router_weight, norm_gains.T, norm_biases.T), 1)
    block = block_of(qkv_weight, out_weight, small)
    block, routes, up_train, down_train, up_frozen, down_frozen = lax.optimization_barrier(
        (block, routes, up_train, down_train, up_frozen, down_frozen)
    )
    along_x = spread_x(block)

    up_t, down_t = up_train[0].astype(BF), down_train[0].astype(BF)

    def for_core(trained, frozen):
        other = shift(jnp.where(core == 0, frozen, trained), "c", 1)
        return jnp.concatenate(ordered(jnp.where(core == 0, trained, frozen), other, core), 0)

    up_two, down_two = for_core(up_t, up_frozen[0]), for_core(down_t, down_frozen[0])
    along_x, up_two, down_two = lax.optimization_barrier((along_x, up_two, down_two))
    rows = spread_y(along_x)
    nat = natural_rows().reshape(1, D)
    g_slots, sid, sidt = route(routes, cotangent)
    up_mine = lax.all_gather(up_two, "x", tiled=True)
    down_mine = lax.all_gather(down_two, "x", tiled=True)

    rows, g_slots, up_two, down_two = lax.optimization_barrier((rows, g_slots, up_two, down_two))
    parts = [rows] + [shift(rows, "z", step) for step in (1, 2, 3)]
    up_far, down_far = shift(up_two, "yh", 1), shift(down_two, "yh", 1)
    parts, up_far, down_far, g_slots = lax.optimization_barrier((parts, up_far, down_far, g_slots))
    pieces = []
    for part in parts:
        pieces += [part, shift(part, "c", 1)]
    up_other = lax.all_gather(up_far, "x", tiled=True)
    down_other = [down_far] + [shift(down_far, "x", step) for step in (1, 2, 3)]

    g_rows = to_all(g_slots.reshape(16, CAP, D), PEERS)
    w, h1p, qkv, probs, attnp, x_mid, h2, gate, vec, router, sent = forward(
        seq_lengths[0], nat, key_mask.reshape(1, ROW), tokens, sid, sidt, pieces
    )
    sent, g_rows = lax.optimization_barrier((sent, g_rows))

    arrived = to_all(sent.reshape(16, LINE, D), PEERS)
    out, back, x_rows, d_out, act, d_up = experts(
        place, arrived, g_rows, up_mine, up_other, down_mine, down_other
    )
    d_back = to_all(back, PEERS)
    grads = weights(x_rows, d_out, act, d_up)
    up_all, down_all = halves(*grads[:3]), halves(*grads[3:])
    d_back, out, up_all, down_all = lax.optimization_barrier((d_back, out, up_all, down_all))

    returned = to_all(out, PEERS)
    up_all, down_all = owned(up_all, "x"), owned(down_all, "x")
    d_x_mid, d_attn, keep, away = back_one(
        nat, sid, d_back.reshape(16 * LINE, D), gate, router, vec, cotangent, x_mid, h2, attnp, w
    )
    sums_one = over_core(keep, away)
    first, keep, away = back_two(d_attn, probs, qkv, h1p)
    first, sums_one, d_attn, returned = lax.optimization_barrier(
        (first, sums_one, d_attn, returned)
    )
    parts_one = along_z(sums_one)
    sums_two = over_core(keep, away)
    second, keep, away = back_three(d_attn, probs, qkv, h1p)
    second, sums_two, parts_one, up_all, down_all = lax.optimization_barrier(
        (second, sums_two, parts_one, up_all, down_all)
    )
    up_all, down_all = owned(up_all, "yh"), owned(down_all, "yh")
    parts_two = along_z(sums_two)
    input_grad, *last = back_four(nat, first, second, d_x_mid, tokens, vec, w)
    keep, away = jnp.concatenate((keep, last[0]), 1), jnp.concatenate((away, last[1]), 1)
    keep, away, parts_two = lax.optimization_barrier((keep, away, parts_two))
    parts_three = along_z(over_core(keep, away))
    parts_three, up_all, down_all = lax.optimization_barrier((parts_three, up_all, down_all))
    grad_up, grad_down = up_all.astype(F32)[None], down_all.astype(F32)[None]
    blocks = to_all(to_blocks(place, parts_one + parts_two + parts_three), FAR)
    own_qkv, own_out, small = from_blocks(blocks)
    block_out = merge(sid, returned.reshape(16 * CAP, D), gate, x_mid)
    return (
        block_out,
        input_grad,
        own_qkv,
        own_out,
        small[:, :16],
        small[:, 16:18].T,
        small[:, 18:20].T,
        grad_up,
        grad_down,
    )


def solution(mesh):
    fine = Mesh(mesh.devices.reshape(SIZES), NAMES)
    by_row = P(NAMES, None)
    by_column = P(None, NAMES)
    by_expert = P(NARROW, WIDE, None)
    return jax.shard_map(
        shards,
        mesh=fine,
        in_specs=(by_row, by_row, P(NAMES)) + (by_row,) * 5 + (by_column,) * 2 + (by_expert,) * 4,
        out_specs=(by_row,) * 5 + (by_column,) * 2 + (by_expert,) * 2,
        check_vma=False,
    )
```

```python
import jax
import jax.numpy as jnp
from jax import lax
from jax.experimental import pallas as pl
from jax.experimental.pallas import tpu as pltpu
from jax.sharding import Mesh
from jax.sharding import PartitionSpec as P

SIZES = (4, 2, 2, 4, 2)
NAMES = ("x", "yh", "c", "z", "yl")
WIDE = ("x", "yh", "c")
NARROW = ("z", "yl")
BF = jnp.bfloat16
F32 = jnp.float32
ROW = 512
D = 768
FF = 3072
CAP = 96
LINE = 112
SOURCES = 4
GELU_ONE = 0.7978845608028654
GELU_CUBE = GELU_ONE * 0.044715
MIB = 1024 * 1024
SMALL = pl.CostEstimate(flops=10**6, bytes_accessed=10**4, transcendentals=0)


def nn(a, b):
    return jnp.dot(a, b, preferred_element_type=F32)


def nt(a, b):
    return lax.dot_general(a, b, (((1,), (1,)), ((), ())), preferred_element_type=F32)


def tn(a, b):
    return lax.dot_general(a, b, (((0,), (0,)), ((), ())), preferred_element_type=F32)


def iota(shape, dim):
    return lax.broadcasted_iota(jnp.int32, shape, dim)


def hot(mask):
    return jnp.where(mask, 1.0, 0.0).astype(BF)


def like(*dims, dtype=BF):
    return jax.ShapeDtypeStruct(dims, dtype)


def tail_of(line):
    high = line.astype(BF).astype(F32)
    low = (line - high).astype(BF).astype(F32)
    full = jnp.concatenate([high, low, jnp.zeros((1, 512), F32)], 1)
    return jnp.where(iota((16, D), 0) == 0, jnp.broadcast_to(full, (16, D)), 0.0).astype(BF)


def line_of(tail):
    line = tail.astype(F32)[0:1]
    return line[:, :128] + line[:, 128:256]


def begin(sems, first, *pairs):
    copies = [
        pltpu.make_async_copy(source, target, sems.at[first + i])
        for i, (source, target) in enumerate(pairs)
    ]
    for copy in copies:
        copy.start()
    return copies


def finish(copies):
    for copy in copies:
        copy.wait()


def norm(x):
    centered = x - jnp.mean(x, -1, keepdims=True)
    scale = lax.rsqrt(jnp.mean(centered * centered, -1, keepdims=True) + 1e-5)
    return centered * scale, scale


def norm_back(d_out, x_hat, scale, gain):
    t = d_out * gain
    d_in = scale * (
        t - jnp.mean(t, -1, keepdims=True) - x_hat * jnp.mean(t * x_hat, -1, keepdims=True)
    )
    return d_in, jnp.sum(d_out * x_hat, 0, keepdims=True), jnp.sum(d_out, 0, keepdims=True)


def route_body(routes_ref, cot_ref, g_ref, sid_ref, sidt_ref):
    lane = iota((ROW, 128), 1)
    r0, r1 = routes_ref[:, 0:1], routes_ref[:, 1:2]
    either = hot((lane == r0) | (lane == r1))
    earlier = nn(hot(iota((ROW, ROW), 1) < iota((ROW, ROW), 0)), either)
    p0 = jnp.sum(jnp.where(lane == r0, earlier, 0.0), 1, keepdims=True).astype(jnp.int32)
    p1 = jnp.sum(jnp.where(lane == r1, earlier, 0.0), 1, keepdims=True).astype(jnp.int32)
    columns = (
        jnp.where(p0 < CAP, r0 * CAP + p0, -1),
        jnp.where(p1 < CAP, r1 * CAP + p1, -1),
        jnp.where(p0 < CAP, r0 * LINE + p0, -1),
        jnp.where(p1 < CAP, r1 * LINE + p1, -1),
        r0,
    )
    table = jnp.broadcast_to(r1, (ROW, 128))
    for at, column in enumerate(columns):
        table = jnp.where(lane == at, column, table)
    sid_ref[...] = table
    turned = jnp.transpose(table.astype(F32))[0:8].astype(jnp.int32)
    sidt_ref[...] = turned
    for part in range(4):
        slot = iota((4 * CAP, ROW), 0) + part * 4 * CAP
        pick = hot((slot == turned[0:1]) | (slot == turned[1:2]))
        g_ref[part * 4 * CAP : (part + 1) * 4 * CAP, :] = nn(pick, cot_ref[...]).astype(BF)


def route(routes, cotangent):
    return pl.pallas_call(
        route_body,
        out_shape=[like(16 * CAP, D), like(ROW, 128, dtype=jnp.int32), like(8, ROW, dtype=jnp.int32)],
        compiler_params=pltpu.CompilerParams(vmem_limit_bytes=32 * MIB),
        cost_estimate=SMALL,
    )(routes, cotangent)


def forward_body(*refs):
    lens_ref, nat_ref, mask_ref, tok_ref, sid_ref, sidt_ref = refs[:6]
    pieces, refs = refs[6:14], refs[14:]
    w_out, h1p_out, qkv_out, probs_out, attnp_out, xmid_out, h2_out = refs[:7]
    gate_ref, vec_ref, router_ref, sent_ref = refs[7:11]
    w_ref, rest_ref, h1p_ref, qkv_ref, probs_ref, attn, attnp_ref, xmid_ref, h2_ref, bias = refs[11:21]
    sems = refs[21]
    rows = [pl.ds(at * 96, 96) for at in range(8)]
    small = [(piece.at[:, FF:], rest_ref.at[to, :]) for piece, to in zip(pieces, rows)]
    large = [(piece.at[:, :FF], w_ref.at[to, :]) for piece, to in zip(pieces, rows)]
    small, large = begin(sems, 0, *small), begin(sems, 8, *large)
    turn = hot(iota((D, D), 0) == nat_ref[...])
    x = tok_ref[...].astype(F32)
    x_hat = norm(x)[0]
    finish(small)
    rest = nn(turn, rest_ref[...])
    vectors = jnp.transpose(rest)[16:24]
    router_ref[...] = rest.astype(BF)
    vec_ref[...] = vectors
    h1 = (x_hat * vectors[0:1] + vectors[2:3]).astype(BF)
    h1p_ref[...] = nn(h1, turn).astype(BF)
    finish(large)
    away = begin(sems, 0, (w_ref, w_out), (h1p_ref, h1p_out))
    for part in range(3):
        cols = slice(part * D, (part + 1) * D)
        qkv_ref[:, cols] = nn(h1p_ref[...], w_ref[:, cols]).astype(BF)
    away += begin(sems, 2, (qkv_ref, qkv_out))

    end_one = lens_ref[0]
    end_two = end_one + lens_ref[1]

    def segment(place):
        return (place >= end_one).astype(jnp.int32) + (place >= end_two).astype(jnp.int32)

    query, key = iota((ROW, ROW), 0), iota((ROW, ROW), 1)
    same = segment(iota((ROW, 1), 0)) == segment(iota((1, ROW), 1))
    allowed = same & (key <= query) & ((mask_ref[...] == 1) | (key == query))
    bias[...] = jnp.where(allowed, 0.0, -1e30)
    low = iota((1, 128), 1) < 64
    half = ROW // 2
    zero = jnp.zeros((), BF)

    def pair(index, carry):
        at = pl.multiple_of(index * 128, 128)
        q = qkv_ref[:, pl.ds(at, 128)] * jnp.asarray(0.125, BF)
        k = qkv_ref[:, pl.ds(D + at, 128)]
        v = qkv_ref[:, pl.ds(2 * D + at, 128)]
        out = [None, None]
        for head in range(2):
            mine = low if head == 0 else jnp.logical_not(low)
            k_mine, v_mine = jnp.where(mine, k, zero), jnp.where(mine, v, zero)
            for block in range(2):
                count, rows = half * (block + 1), slice(block * half, (block + 1) * half)
                scores = nt(q[rows], k_mine[:count]) + bias[rows, :count]
                e = jnp.exp(scores - jnp.max(scores, 1, keepdims=True))
                probs = (e * (1.0 / jnp.sum(e, 1, keepdims=True))).astype(BF)
                probs_ref[2 * index + head, rows, :count] = probs
                if block == 0:
                    probs_ref[2 * index + head, rows, count:] = jnp.zeros((half, half), BF)
                term = nn(probs, v_mine[:count])
                out[block] = term if head == 0 else out[block] + term
        for block in range(2):
            attn[block * half : (block + 1) * half, pl.ds(at, 128)] = out[block].astype(BF)
        heads = pl.ds(2 * index, 2)
        begin(sems, 8 + index, (probs_ref.at[heads], probs_out.at[heads]))
        return carry

    lax.fori_loop(0, 6, pair, 0)
    for index in range(6):
        heads = pl.ds(2 * index, 2)
        away.append(
            pltpu.make_async_copy(probs_ref.at[heads], probs_out.at[heads], sems.at[8 + index])
        )
    attnp_ref[...] = nn(attn[...], turn).astype(BF)
    x_mid = x + nn(attnp_ref[...], w_ref[:, 3 * D :])
    xmid_ref[...] = x_mid
    h2 = (norm(x_mid)[0] * vectors[1:2] + vectors[3:4]).astype(BF)
    h2_ref[...] = h2
    away += begin(sems, 3, (attnp_ref, attnp_out), (xmid_ref, xmid_out), (h2_ref, h2_out))
    logits = nn(h2, router_ref[...])
    lane = iota((ROW, 128), 1)
    s0, s1, r0, r1 = (sid_ref[:, at : at + 1] for at in (0, 1, 4, 5))
    c0 = jnp.sum(jnp.where(lane == r0, logits, 0.0), 1, keepdims=True)
    c1 = jnp.sum(jnp.where(lane == r1, logits, 0.0), 1, keepdims=True)
    g0, g1 = 1.0 / (1.0 + jnp.exp(c1 - c0)), 1.0 / (1.0 + jnp.exp(c0 - c1))
    gate_ref[...] = jnp.where(lane == 0, g0, jnp.where(lane == 1, g1, 0.0))
    first, second = sidt_ref[2:3], sidt_ref[3:4]
    for part in range(4):
        slot = iota((4 * LINE, ROW), 0) + part * 4 * LINE
        pick = hot((slot == first) | (slot == second))
        sent_ref[part * 4 * LINE : (part + 1) * 4 * LINE, :] = nn(pick, h2_ref[...]).astype(BF)
    for expert in range(16):
        slot = lane + expert * CAP
        line = jnp.sum(
            jnp.where(slot == s0, g0, 0.0) + jnp.where(slot == s1, g1, 0.0), 0, keepdims=True
        )
        sent_ref[expert * LINE + CAP : (expert + 1) * LINE, :] = tail_of(line)
    finish(away)


def forward(lens, nat, mask, tokens, sid, sidt, pieces):
    vmem = pl.BlockSpec(memory_space=pltpu.VMEM)
    anywhere = pl.BlockSpec(memory_space=pl.ANY)
    moved = [
        like(D, FF),
        like(ROW, D),
        like(ROW, 3 * D),
        like(12, ROW, ROW),
        like(ROW, D),
        like(ROW, D, dtype=F32),
        like(ROW, D),
    ]
    held = [like(ROW, 128, dtype=F32), like(8, D, dtype=F32), like(D, 128), like(16 * LINE, D)]
    buffers = [like(D, FF), like(D, 128), *moved[1:4], like(ROW, D), *moved[4:]]
    return pl.pallas_call(
        forward_body,
        in_specs=[pl.BlockSpec(memory_space=pltpu.SMEM)] + [vmem] * 5 + [anywhere] * 8,
        out_specs=[anywhere] * 7 + [vmem] * 4,
        out_shape=moved + held,
        scratch_shapes=[pltpu.VMEM(b.shape, b.dtype) for b in buffers]
        + [pltpu.VMEM((ROW, ROW), F32), pltpu.SemaphoreType.DMA((16,))],
        compiler_params=pltpu.CompilerParams(vmem_limit_bytes=56 * MIB),
        cost_estimate=SMALL,
    )(lens, nat, mask, tokens, sid, sidt, *pieces)


def expert_body(
    place_ref, sent_ref, g_ref, up_mine, up_other, down_mine, *refs
):
    down_other = refs[:4]
    out_ref, back_ref, x_ref, dout_ref, act_ref, dup_ref, up_ref, down_ref, sems = refs[4:]
    x_place, y_place = place_ref[0], place_ref[1]

    def loads():
        for i in range(4):
            mine, other = 2 * i + y_place, 2 * i + 1 - y_place
            far = 2 * lax.rem(x_place - i + 4, 4) + 1 - y_place
            yield up_mine.at[pl.ds(i * 96, 96), :], up_ref.at[pl.ds(mine * 96, 96), :]
            yield up_other.at[pl.ds(i * 96, 96), :], up_ref.at[pl.ds(other * 96, 96), :]
            yield down_mine.at[pl.ds(i * 384, 384), :], down_ref.at[pl.ds(mine * 384, 384), :]
            yield down_other[i], down_ref.at[pl.ds(far * 384, 384), :]

    @pl.when(pl.program_id(0) == 0)
    def _():
        copies = [
            pltpu.make_async_copy(source, target, sems.at[i])
            for i, (source, target) in enumerate(loads())
        ]
        for copy in copies:
            copy.start()
        for copy in copies:
            copy.wait()

    for s in range(SOURCES):
        first, last = s * CAP, (s + 1) * CAP
        x_ref[first:last, :] = sent_ref[s, :CAP, :]
        gate = line_of(sent_ref[s, CAP:LINE, :])
        column = jnp.transpose(jnp.broadcast_to(gate, (128, 128)))[:CAP, :1]
        dout_ref[first:last, :] = (g_ref[s].astype(F32) * column).astype(BF)
    x, d_out = x_ref[...], dout_ref[...]
    for part in range(FF // 256):
        cols = slice(part * 256, (part + 1) * 256)
        up = nn(x, up_ref[:, cols])
        d_act = nt(d_out, down_ref[cols, :])
        square = up * up
        t = jnp.tanh(up * (GELU_ONE + GELU_CUBE * square))
        a = 0.5 + 0.5 * t
        act_ref[:, cols] = (up * a).astype(BF)
        slope = a + (up * (1.0 - t * t)) * (0.5 * GELU_ONE + 1.5 * GELU_CUBE * square)
        dup_ref[:, cols] = (d_act * slope).astype(BF)
    out = nn(act_ref[...], down_ref[...]).astype(BF)
    back = nt(dup_ref[...], up_ref[...]).astype(BF)
    for s in range(SOURCES):
        out_ref[s] = out[s * CAP : (s + 1) * CAP]
        back_ref[s, :CAP, :] = back[s * CAP : (s + 1) * CAP]
    for s in range(SOURCES):
        d_gate = jnp.sum(out_ref[s].astype(F32) * g_ref[s].astype(F32), -1, keepdims=True)
        d_gate = jnp.broadcast_to(d_gate, (CAP, 128))
        wide = jnp.concatenate([d_gate, jnp.zeros((128 - CAP, 128), F32)], 0)
        back_ref[s, CAP:LINE, :] = tail_of(jnp.transpose(wide)[0:1])


def experts(place, sent, g, up_mine, up_other, down_mine, down_other):
    rows = SOURCES * CAP
    anywhere = pl.BlockSpec(memory_space=pl.ANY)
    by_source = lambda size: pl.BlockSpec((SOURCES, size, D), lambda i: (i, 0, 0))
    by_rows = lambda width: pl.BlockSpec((rows, width), lambda i: (i, 0))
    return pl.pallas_call(
        expert_body,
        grid=(16 // SOURCES,),
        in_specs=[
            pl.BlockSpec(memory_space=pltpu.SMEM),
            by_source(LINE),
            by_source(CAP),
        ]
        + [anywhere] * 7,
        out_specs=[
            by_source(CAP), by_source(LINE), by_rows(D), by_rows(D), by_rows(FF), by_rows(FF),
        ],
        out_shape=[
            like(16, CAP, D),
            like(16, LINE, D),
            like(16 * CAP, D),
            like(16 * CAP, D),
            like(16 * CAP, FF),
            like(16 * CAP, FF),
        ],
        scratch_shapes=[
            pltpu.VMEM((D, FF), BF),
            pltpu.VMEM((FF, D), BF),
            pltpu.SemaphoreType.DMA((16,)),
        ],
        compiler_params=pltpu.CompilerParams(vmem_limit_bytes=60 * MIB),
        cost_estimate=SMALL,
    )(place, sent, g, up_mine, up_other, down_mine, *down_other)


def weight_body(x_ref, dout_ref, act_ref, dup_ref, *refs):
    up_refs, down_refs = refs[:3], refs[3:]
    up = tn(x_ref[...], dup_ref[...]).astype(BF)
    for block in range(8):
        rows, low = block * 96, (block % 4) * 48
        up_refs[0][block * 48 : (block + 1) * 48, :] = up[rows : rows + 48]
        up_refs[1 + block // 4][low : low + 48, :] = up[rows + 48 : rows + 96]
    down = tn(act_ref[...], dout_ref[...]).astype(BF)
    down_refs[0][...] = down[:192]
    for part in range(2):

        @pl.when(pl.program_id(0) // 4 == part)
        def _():
            down_refs[1 + part][...] = down[192:]


def weights(x, d_out, act, d_up):
    whole = pl.BlockSpec((16 * CAP, D), lambda i: (0, 0))
    columns = pl.BlockSpec((16 * CAP, 384), lambda i: (0, i))
    up = lambda rows: pl.BlockSpec((rows, 384), lambda i: (0, i))
    down = lambda index: pl.BlockSpec((192, D), index)
    return pl.pallas_call(
        weight_body,
        grid=(8,),
        in_specs=[whole, whole, columns, columns],
        out_specs=[
            up(384),
            up(192),
            up(192),
            down(lambda i: (i, 0)),
            down(lambda i: (jnp.minimum(i, 3), 0)),
            down(lambda i: (jnp.maximum(i - 4, 0), 0)),
        ],
        out_shape=[
            like(384, FF), like(192, FF), like(192, FF), like(1536, D), like(768, D), like(768, D),
        ],
        compiler_params=pltpu.CompilerParams(vmem_limit_bytes=48 * MIB),
        cost_estimate=SMALL,
    )(x, d_out, act, d_up)


def put_rows(keep_ref, away_ref, cols, values):
    for step in range(4):
        rows = slice(step * 96, (step + 1) * 96)
        keep_ref[rows, cols] = values[step * 192 : step * 192 + 96]
        away_ref[rows, cols] = values[step * 192 + 96 : (step + 1) * 192]


def attention_back(base, pairs, dattn_ref, probs_ref, qkv_ref, d_qkv):
    width = 128 * pairs
    low = iota((1, 128), 1) < 64
    zero = jnp.zeros((), BF)
    half = ROW // 2

    def add(terms, at, term):
        terms[at] = term if terms[at] is None else terms[at] + term

    def pair(index, carry):
        at = pl.multiple_of((base + index) * 128, 128)
        to = pl.multiple_of(index * 128, 128)
        q, k, v = (qkv_ref[:, pl.ds(part * D + at, 128)] for part in range(3))
        d_attn = dattn_ref[:, pl.ds(at, 128)]
        dq, dk, dv = [None, None], [None, None], [None, None]
        for head in range(2):
            mine = low if head == 0 else jnp.logical_not(low)
            q_mine, k_mine, v_mine, d_mine = (jnp.where(mine, t, zero) for t in (q, k, v, d_attn))
            for block in range(2):
                count, rows = half * (block + 1), slice(block * half, (block + 1) * half)
                probs = probs_ref[2 * index + head, rows, :count]
                d_probs = nt(d_mine[rows], v_mine[:count])
                wide = probs.astype(F32)
                weighted = wide * d_probs
                delta = jnp.sum(weighted, 1, keepdims=True)
                d_scores = (weighted - wide * delta).astype(BF)
                add(dq, block, nn(d_scores, k_mine[:count]))
                for other in range(block + 1):
                    keys = slice(other * half, (other + 1) * half)
                    add(dk, other, tn(d_scores[:, keys], q_mine[rows]))
                    add(dv, other, tn(probs[:, keys], d_mine[rows]))
        for block in range(2):
            rows = slice(block * half, (block + 1) * half)
            d_qkv[rows, pl.ds(to, 128)] = (dq[block] * 0.125).astype(BF)
            d_qkv[rows, pl.ds(width + to, 128)] = (dk[block] * 0.125).astype(BF)
            d_qkv[rows, pl.ds(2 * width + to, 128)] = dv[block].astype(BF)
        return carry

    lax.fori_loop(0, pairs, pair, 0)


def back_one_body(
    nat_ref, sid_ref, gate_ref, router_ref, vec_ref, dback_in, xmid_in, cot_in, w_in, attnp_in,
    h2_in, probs_in, qkv_in, h1p_in, dxm_out, dattn_out, dqkv_out, keep_out, away_out,
    dback_ref, xmid_ref, cot_ref, w_ref, attnp_ref, h2_ref, probs_ref, qkv_ref, h1p_ref, dxm_ref,
    dattn_ref, dqkv_ref, keep_ref, away_ref, sems,
):
    sources = (
        dback_in, xmid_in, cot_in, w_in.at[:, 3 * D :], attnp_in, h2_in, qkv_in, probs_in.at[:8], h1p_in,
    )
    targets = (dback_ref, xmid_ref, cot_ref, w_ref, attnp_ref, h2_ref, qkv_ref, probs_ref, h1p_ref)
    pairs = list(zip(sources, targets))
    loads = begin(sems, 0, *pairs[:1])
    turn = hot(iota((D, D), 0) == nat_ref[...])
    lane = iota((ROW, 128), 1)
    s0, s1, w0, w1, r0, r1 = (sid_ref[:, at : at + 1] for at in range(6))
    finish(loads)
    loads += begin(sems, 1, *pairs[1:])
    a0 = a1 = jnp.zeros((ROW, 128), F32)
    for expert in range(16):
        line = line_of(dback_ref[expert * LINE + CAP : (expert + 1) * LINE, :])
        slot = jnp.where(lane < CAP, lane + expert * CAP, -2)
        a0 = a0 + jnp.where(slot == s0, line, 0.0)
        a1 = a1 + jnp.where(slot == s1, line, 0.0)
    dg0, dg1 = jnp.sum(a0, 1, keepdims=True), jnp.sum(a1, 1, keepdims=True)
    g0, g1 = gate_ref[:, 0:1], gate_ref[:, 1:2]
    both = g0 * dg0 + g1 * dg1
    d_logits = jnp.where(lane == r0, g0 * (dg0 - both), 0.0)
    d_logits = d_logits + jnp.where(lane == r1, g1 * (dg1 - both), 0.0)
    high = d_logits.astype(BF)
    low = (d_logits - high.astype(F32)).astype(BF)
    d_h2 = nt(high, router_ref[...]) + nt(low, router_ref[...])
    for part in range(4):
        slot = iota((ROW, 4 * LINE), 1) + part * 4 * LINE
        pick = hot((slot == w0) | (slot == w1))
        d_h2 = d_h2 + nn(pick, dback_ref[part * 4 * LINE : (part + 1) * 4 * LINE, :])
    finish(loads[1:3])
    x_hat, scale = norm(xmid_ref[...])
    d_in, d_gain, d_bias = norm_back(d_h2, x_hat, scale, vec_ref[1:2])
    d_x_mid = cot_ref[...].astype(F32) + d_in
    dxm_ref[...] = d_x_mid
    d_proj = d_x_mid.astype(BF)
    finish(loads[3:6])
    dattn_ref[...] = nt(nt(d_proj, w_ref[...]).astype(BF), turn).astype(BF)
    leaving = begin(sems, 9, (dxm_ref, dxm_out), (dattn_ref, dattn_out))
    put_rows(keep_ref, away_ref, slice(0, D), tn(attnp_ref[...], d_proj).astype(BF))
    d_router = tn(h2_ref[...], high) + tn(h2_ref[...], low)
    sub = iota((128, D), 0)
    rows = jnp.where(sub == 17, d_gain, 0.0) + jnp.where(sub == 19, d_bias, 0.0)
    small = d_router + jnp.transpose(rows)
    put_rows(keep_ref, away_ref, slice(D, D + 128), tn(turn, small.astype(BF)).astype(BF))
    cols = slice(0, D + 128)
    leaving += begin(
        sems, 11, (keep_ref.at[:, cols], keep_out.at[:, cols]), (away_ref.at[:, cols], away_out.at[:, cols])
    )
    finish(loads[6:8])
    attention_back(0, 4, dattn_ref, probs_ref, qkv_ref, dqkv_ref)
    leaving += begin(sems, 13, (dqkv_ref, dqkv_out))
    finish(loads[8:])
    for part in range(3):
        cols = slice(D + 128 + part * 512, D + 128 + (part + 1) * 512)
        grad = tn(h1p_ref[...], dqkv_ref[:, part * 512 : (part + 1) * 512]).astype(BF)
        put_rows(keep_ref, away_ref, cols, grad)
        leaving += begin(
            sems,
            14 + 2 * part,
            (keep_ref.at[:, cols], keep_out.at[:, cols]),
            (away_ref.at[:, cols], away_out.at[:, cols]),
        )
    finish(leaving)


def back_one(nat, sid, gate, router, vec, d_back, x_mid, cotangent, w, attnp, h2, probs, qkv, h1p):
    vmem = pl.BlockSpec(memory_space=pltpu.VMEM)
    anywhere = pl.BlockSpec(memory_space=pl.ANY)
    ins = [
        like(16 * LINE, D), like(ROW, D, dtype=F32), like(ROW, D), like(D, D), like(ROW, D),
        like(ROW, D), like(8, ROW, ROW), like(ROW, 3 * D), like(ROW, D),
    ]
    outs = [
        like(ROW, D, dtype=F32), like(ROW, D), like(ROW, 1536), like(384, 2432), like(384, 2432),
    ]
    return pl.pallas_call(
        back_one_body,
        in_specs=[vmem] * 5 + [anywhere] * 9,
        out_specs=[anywhere] * 5,
        out_shape=outs,
        scratch_shapes=[pltpu.VMEM(b.shape, b.dtype) for b in ins + outs]
        + [pltpu.SemaphoreType.DMA((20,))],
        compiler_params=pltpu.CompilerParams(vmem_limit_bytes=56 * MIB),
        cost_estimate=SMALL,
    )(nat, sid, gate, router, vec, d_back, x_mid, cotangent, w, attnp, h2, probs, qkv, h1p)


def back_two_body(
    nat_ref, vec_ref, dattn_in, probs_in, qkv_in, h1p_in, first_in, w_in, tok_in, dxm_in,
    gx_out, keep_out, away_out, dattn_ref, probs_ref, qkv_ref, h1p_ref, first_ref, w_ref, tok_ref,
    dxm_ref, gx_ref, keep_ref, away_ref, second_ref, sems,
):
    sources = (
        dattn_in, qkv_in, probs_in.at[8:], h1p_in, first_in, w_in.at[:, : 3 * D], tok_in, dxm_in,
    )
    targets = (dattn_ref, qkv_ref, probs_ref, h1p_ref, first_ref, w_ref, tok_ref, dxm_ref)
    pairs = list(zip(sources, targets))
    loads = begin(sems, 0, *pairs[:3])
    turn = hot(iota((D, D), 0) == nat_ref[...])
    finish(loads)
    loads += begin(sems, 3, *pairs[3:])
    attention_back(4, 2, dattn_ref, probs_ref, qkv_ref, second_ref)
    finish(loads[3:6])
    d_h1p = jnp.zeros((ROW, D), F32)
    for part in range(3):
        middle = part * D + 512
        d_second = second_ref[:, part * 256 : (part + 1) * 256]
        grad = tn(h1p_ref[...], d_second).astype(BF)
        put_rows(keep_ref, away_ref, slice(part * 256, (part + 1) * 256), grad)
        d_h1p = d_h1p + nt(first_ref[:, part * 512 : (part + 1) * 512], w_ref[:, part * D : middle])
        d_h1p = d_h1p + nt(d_second, w_ref[:, middle : (part + 1) * D])
    cols = slice(0, D)
    leaving = begin(
        sems, 8, (keep_ref.at[:, cols], keep_out.at[:, cols]), (away_ref.at[:, cols], away_out.at[:, cols])
    )
    finish(loads[6:])
    d_h1 = nt(d_h1p.astype(BF), turn)
    x_hat, scale = norm(tok_ref[...].astype(F32))
    d_in, d_gain, d_bias = norm_back(d_h1, x_hat, scale, vec_ref[0:1])
    gx_ref[...] = dxm_ref[...] + d_in
    leaving += begin(sems, 10, (gx_ref, gx_out))
    sub = iota((128, D), 0)
    rows = jnp.where(sub == 16, d_gain, 0.0) + jnp.where(sub == 18, d_bias, 0.0)
    small = tn(turn, jnp.transpose(rows).astype(BF)).astype(BF)
    cols = slice(D, D + 128)
    put_rows(keep_ref, away_ref, cols, small)
    leaving += begin(
        sems, 11, (keep_ref.at[:, cols], keep_out.at[:, cols]), (away_ref.at[:, cols], away_out.at[:, cols])
    )
    finish(leaving)


def back_two(nat, vec, d_attn, probs, qkv, h1p, first, w, tokens, d_x_mid):
    vmem = pl.BlockSpec(memory_space=pltpu.VMEM)
    anywhere = pl.BlockSpec(memory_space=pl.ANY)
    ins = [
        like(ROW, D), like(4, ROW, ROW), like(ROW, 3 * D), like(ROW, D), like(ROW, 1536),
        like(D, 3 * D), like(ROW, D), like(ROW, D, dtype=F32),
    ]
    outs = [like(ROW, D, dtype=F32), like(384, 896), like(384, 896)]
    return pl.pallas_call(
        back_two_body,
        in_specs=[vmem] * 2 + [anywhere] * 8,
        out_specs=[anywhere] * 3,
        out_shape=outs,
        scratch_shapes=[pltpu.VMEM(b.shape, b.dtype) for b in ins + outs]
        + [pltpu.VMEM((ROW, D), BF), pltpu.SemaphoreType.DMA((13,))],
        compiler_params=pltpu.CompilerParams(vmem_limit_bytes=56 * MIB),
        cost_estimate=SMALL,
    )(nat, vec, d_attn, probs, qkv, h1p, first, w, tokens, d_x_mid)


def merge_body(sid_ref, ret_ref, gate_ref, xmid_ref, out_ref):
    s0, s1 = sid_ref[:, 0:1], sid_ref[:, 1:2]
    y0 = y1 = jnp.zeros((ROW, D), F32)
    for part in range(4):
        slot = iota((ROW, 4 * CAP), 1) + part * 4 * CAP
        values = ret_ref[part * 4 * CAP : (part + 1) * 4 * CAP, :]
        y0 = y0 + nn(hot(slot == s0), values)
        y1 = y1 + nn(hot(slot == s1), values)
    out_ref[...] = (xmid_ref[...] + (gate_ref[:, 0:1] * y0 + gate_ref[:, 1:2] * y1)).astype(BF)


def merge(sid, returned, gate, x_mid):
    return pl.pallas_call(
        merge_body,
        out_shape=like(ROW, D),
        compiler_params=pltpu.CompilerParams(vmem_limit_bytes=40 * MIB),
        cost_estimate=SMALL,
    )(sid, returned, gate, x_mid)


def to_blocks_body(place_ref, *refs):
    count = (len(refs) - 3) // 2
    held = refs[count + 1 : 2 * count + 1]
    out_ref, total, sems = refs[count], refs[-2], refs[-1]
    sources = [ref.at[pl.ds(0, 96), :] for ref in refs[:count]]
    loads = begin(sems, 0, *zip(sources, held))
    col = 0
    total[96:104, :] = jnp.zeros((8, total.shape[1]), F32)
    for group in range(count // 5):
        mine = slice(5 * group, 5 * group + 5)
        finish(loads[mine])
        value = held[5 * group][...].astype(F32)
        for part in held[mine][1:]:
            value = value + part[...].astype(F32)
        total[0:96, col : col + value.shape[1]] = value
        col += value.shape[1]
    x, y = place_ref[0], 2 * place_ref[1] + place_ref[2]
    for k in range(16):
        to = lax.rem(x - k % 4 + 4, 4) * 4 + lax.rem(y - k // 4 + 4, 4)
        out_ref[to] = total[6 * k : 6 * k + 8, :].astype(BF)


def to_blocks(place, parts):
    width = sum(part.shape[1] for part in parts[::5])
    return pl.pallas_call(
        to_blocks_body,
        in_specs=[pl.BlockSpec(memory_space=pltpu.SMEM)]
        + [pl.BlockSpec(memory_space=pl.ANY)] * len(parts),
        out_shape=like(16, 8, width),
        scratch_shapes=[pltpu.VMEM((96, part.shape[1]), BF) for part in parts]
        + [pltpu.VMEM((104, width), F32), pltpu.SemaphoreType.DMA((len(parts),))],
        compiler_params=pltpu.CompilerParams(vmem_limit_bytes=60 * MIB),
        cost_estimate=SMALL,
    )(place, *parts)


def from_blocks_body(in_ref, qkv_ref, out_ref, small_ref):
    total = in_ref[0].astype(F32)
    for k in range(1, 16):
        total = total + in_ref[k].astype(F32)
    out_ref[...] = total[:6, :D]
    for part in range(3):
        qkv_ref[:, part * D : part * D + 512] = total[:6, 896 + part * 512 : 1408 + part * 512]
        qkv_ref[:, part * D + 512 : (part + 1) * D] = total[:6, 2432 + part * 256 : 2688 + part * 256]
    small_ref[...] = total[:6, D : D + 128] + total[:6, 3200:3328]


def from_blocks(blocks):
    return pl.pallas_call(
        from_blocks_body,
        out_shape=[like(6, 3 * D, dtype=F32), like(6, D, dtype=F32), like(6, 128, dtype=F32)],
        compiler_params=pltpu.CompilerParams(vmem_limit_bytes=16 * MIB),
        cost_estimate=SMALL,
    )(blocks)


def block_body(qkv_ref, out_ref, small_ref, to_ref):
    to_ref[...] = jnp.zeros(to_ref.shape, BF)
    to_ref[0:6, : 3 * D] = qkv_ref[...].astype(BF)
    to_ref[0:6, 3 * D : FF] = out_ref[...].astype(BF)
    to_ref[0:6, FF : FF + 20] = small_ref[...].astype(BF)


def block_of(qkv, out, small):
    return pl.pallas_call(
        block_body,
        out_shape=like(8, FF + 128),
        compiler_params=pltpu.CompilerParams(vmem_limit_bytes=16 * MIB),
        cost_estimate=SMALL,
    )(qkv, out, small)


def shift(value, axis, by):
    count = lax.axis_size(axis)
    return lax.ppermute(value, axis, [(i, (i + by) % count) for i in range(count)])


def ordered(mine, other, index):
    first = jnp.where(index == 0, mine, other)
    second = jnp.where(index == 0, other, mine)
    return first, second


FAR = ("x", "yh", "yl")
PEERS = ("c", "z", "yl")


def to_all(rows, names):
    return lax.all_to_all(rows, names, split_axis=0, concat_axis=0, tiled=True)


def spread_x(block):
    return jnp.stack([block] + [shift(block, "x", step) for step in (1, 2, 3)])


def spread_y(along_x):
    near = [along_x] + [shift(along_x, ("yh", "yl"), step) for step in (1, 2, 3)]
    return jnp.stack(near)[:, :, :6].reshape(96, along_x.shape[2])


def natural_rows():
    x, c, z = (lax.axis_index(name) for name in ("x", "c", "z"))
    y = lax.axis_index("yh") * 2 + lax.axis_index("yl")
    row = jnp.arange(768)
    step, other, i = row // 192, (row // 96) % 2, row % 96
    core, deep = (c + other) % 2, (z - step) % 4
    high, long = (y - i // 24) % 4, (x - (i // 6) % 4) % 4
    device = ((long * 2 + high // 2) * 2 + core) * 8 + deep * 2 + high % 2
    return (device * 6 + i % 6).astype(jnp.int32)


def along_z(keep, got):
    parts = [keep, got]
    for step in (1, 2, 3):
        rows = slice(step * 96, (step + 1) * 96)
        both = keep[rows].astype(F32) + got[rows].astype(F32)
        parts.append(shift(both.astype(BF), "z", -step))
    return parts


def halves(kept, *sent):
    got = [lax.ppermute(part, "c", [(0, 1)]) for part in sent]
    return jnp.where(lax.axis_index("c") == 0, kept, jnp.concatenate(got, 0))


def owned(mine, axis):
    return lax.psum_scatter(mine, axis, scatter_dimension=0, tiled=True)


def shards(
    tokens,
    seq_lengths,
    key_mask,
    routes,
    cotangent,
    qkv_weight,
    out_weight,
    router_weight,
    norm_gains,
    norm_biases,
    up_train,
    down_train,
    up_frozen,
    down_frozen,
):
    core = lax.axis_index("c")

    place = jnp.stack([lax.axis_index(name) for name in ("x", "yh", "yl")]).astype(jnp.int32)

    small = jnp.concatenate((router_weight, norm_gains.T, norm_biases.T), 1)
    block = block_of(qkv_weight, out_weight, small)
    block, routes, up_train, down_train, up_frozen, down_frozen = lax.optimization_barrier(
        (block, routes, up_train, down_train, up_frozen, down_frozen)
    )
    along_x = spread_x(block)

    up_t, down_t = up_train[0].astype(BF), down_train[0].astype(BF)

    def for_core(trained, frozen):
        other = shift(jnp.where(core == 0, frozen, trained), "c", 1)
        return jnp.concatenate(ordered(jnp.where(core == 0, trained, frozen), other, core), 0)

    up_two, down_two = for_core(up_t, up_frozen[0]), for_core(down_t, down_frozen[0])
    along_x, up_two, down_two = lax.optimization_barrier((along_x, up_two, down_two))
    rows = spread_y(along_x)
    nat = natural_rows().reshape(1, D)
    g_slots, sid, sidt = route(routes, cotangent)
    up_mine = lax.all_gather(up_two, "x", tiled=True)
    down_mine = lax.all_gather(down_two, "x", tiled=True)

    rows, g_slots, up_two, down_two = lax.optimization_barrier((rows, g_slots, up_two, down_two))
    parts = [rows] + [shift(rows, "z", step) for step in (1, 2, 3)]
    up_far, down_far = shift(up_two, "yh", 1), shift(down_two, "yh", 1)
    parts, up_far, down_far, g_slots = lax.optimization_barrier((parts, up_far, down_far, g_slots))
    pieces = []
    for part in parts:
        pieces += [part, shift(part, "c", 1)]
    up_other = lax.all_gather(up_far, "x", tiled=True)
    down_other = [down_far] + [shift(down_far, "x", step) for step in (1, 2, 3)]

    g_rows = to_all(g_slots.reshape(16, CAP, D), PEERS)
    w, h1p, qkv, probs, attnp, x_mid, h2, gate, vec, router, sent = forward(
        seq_lengths[0], nat, key_mask.reshape(1, ROW), tokens, sid, sidt, pieces
    )
    sent, g_rows = lax.optimization_barrier((sent, g_rows))

    arrived = to_all(sent.reshape(16, LINE, D), PEERS)
    out, back, x_rows, d_out, act, d_up = experts(
        place, arrived, g_rows, up_mine, up_other, down_mine, down_other
    )
    d_back = to_all(back, PEERS)
    grads = weights(x_rows, d_out, act, d_up)
    up_all, down_all = halves(*grads[:3]), halves(*grads[3:])
    d_back, out, up_all, down_all = lax.optimization_barrier((d_back, out, up_all, down_all))

    returned = to_all(out, PEERS)
    up_all, down_all = owned(up_all, "x"), owned(down_all, "x")
    d_x_mid, d_attn, first, keep, away = back_one(
        nat, sid, gate, router, vec, d_back.reshape(16 * LINE, D), x_mid, cotangent, w, attnp, h2,
        probs, qkv, h1p,
    )
    input_grad, *last = back_two(nat, vec, d_attn, probs, qkv, h1p, first, w, tokens, d_x_mid)
    got = shift(away, "c", 1)
    keep, got, returned = lax.optimization_barrier((keep, got, returned))
    parts_one = along_z(keep, got)
    near, last, up_all = lax.optimization_barrier((parts_one[2::2], last, up_all))
    parts_one[2::2] = near
    up_all = owned(up_all, "yh")
    parts_two = along_z(last[0], shift(last[1], "c", 1))
    parts_two, down_all = lax.optimization_barrier((parts_two, down_all))
    down_all = owned(down_all, "yh")
    blocks = to_blocks(place, parts_one + parts_two)
    blocks, returned = lax.optimization_barrier((blocks, returned))
    own_qkv, own_out, small = from_blocks(to_all(blocks, FAR))
    grad_up, grad_down = up_all.astype(F32)[None], down_all.astype(F32)[None]
    block_out = merge(sid, returned.reshape(16 * CAP, D), gate, x_mid)
    return (
        block_out,
        input_grad,
        own_qkv,
        own_out,
        small[:, :16],
        small[:, 16:18].T,
        small[:, 18:20].T,
        grad_up,
        grad_down,
    )


def solution(mesh):
    fine = Mesh(mesh.devices.reshape(SIZES), NAMES)
    by_row = P(NAMES, None)
    by_column = P(None, NAMES)
    by_expert = P(NARROW, WIDE, None)
    return jax.shard_map(
        shards,
        mesh=fine,
        in_specs=(by_row, by_row, P(NAMES)) + (by_row,) * 5 + (by_column,) * 2 + (by_expert,) * 4,
        out_specs=(by_row,) * 5 + (by_column,) * 2 + (by_expert,) * 2,
        check_vma=False,
    )
```

```python
import functools

import jax
import jax.numpy as jnp
from jax import lax
from jax.experimental import pallas as pl
from jax.experimental.pallas import tpu as pltpu
from jax.sharding import Mesh
from jax.sharding import PartitionSpec as P

SIZES = (4, 2, 2, 4, 2)
NAMES = ("x", "yh", "c", "z", "yl")
WIDE = ("x", "yh", "c")
NARROW = ("z", "yl")
BF = jnp.bfloat16
F32 = jnp.float32
ROW = 512
D = 768
FF = 3072
CAP = 96
LINE = 592
SOURCES = 4
GELU_ONE = 0.7978845608028654
GELU_CUBE = GELU_ONE * 0.044715
MIB = 1024 * 1024
SMALL = pl.CostEstimate(flops=10**6, bytes_accessed=10**4, transcendentals=0)


def nn(a, b):
    return jnp.dot(a, b, preferred_element_type=F32)


def nt(a, b):
    return lax.dot_general(a, b, (((1,), (1,)), ((), ())), preferred_element_type=F32)


def tn(a, b):
    return lax.dot_general(a, b, (((0,), (0,)), ((), ())), preferred_element_type=F32)


def iota(shape, dim):
    return lax.broadcasted_iota(jnp.int32, shape, dim)


def hot(mask):
    return jnp.where(mask, 1.0, 0.0).astype(BF)


def like(*dims, dtype=BF):
    return jax.ShapeDtypeStruct(dims, dtype)


def tail_of(line):
    high = line.astype(BF).astype(F32)
    row = iota((16, 128), 0)
    return jnp.where(row == 0, high, jnp.where(row == 1, line - high, 0.0)).astype(BF)


def line_of(tail):
    tail = tail.astype(F32)
    return tail[0:1] + tail[1:2]


def begin(sems, first, *pairs):
    copies = [
        pltpu.make_async_copy(source, target, sems.at[first + i])
        for i, (source, target) in enumerate(pairs)
    ]
    for copy in copies:
        copy.start()
    return copies


def finish(copies):
    for copy in copies:
        copy.wait()


def norm(x):
    centered = x - jnp.mean(x, -1, keepdims=True)
    scale = lax.rsqrt(jnp.mean(centered * centered, -1, keepdims=True) + 1e-5)
    return centered * scale, scale


def norm_back(d_out, x_hat, scale, gain):
    t = d_out * gain
    d_in = scale * (
        t - jnp.mean(t, -1, keepdims=True) - x_hat * jnp.mean(t * x_hat, -1, keepdims=True)
    )
    return d_in, jnp.sum(d_out * x_hat, 0, keepdims=True), jnp.sum(d_out, 0, keepdims=True)


def route_body(routes_ref, cot_ref, g_ref, sid_ref, sidt_ref):
    lane = iota((ROW, 128), 1)
    r0, r1 = routes_ref[:, 0:1], routes_ref[:, 1:2]
    either = hot((lane == r0) | (lane == r1))
    earlier = nn(hot(iota((ROW, ROW), 1) < iota((ROW, ROW), 0)), either)
    p0 = jnp.sum(jnp.where(lane == r0, earlier, 0.0), 1, keepdims=True).astype(jnp.int32)
    p1 = jnp.sum(jnp.where(lane == r1, earlier, 0.0), 1, keepdims=True).astype(jnp.int32)
    columns = (
        jnp.where(p0 < CAP, r0 * CAP + p0, -1),
        jnp.where(p1 < CAP, r1 * CAP + p1, -1),
        r0,
    )
    table = jnp.broadcast_to(r1, (ROW, 128))
    for at, column in enumerate(columns):
        table = jnp.where(lane == at, column, table)
    sid_ref[...] = table
    turned = jnp.transpose(table.astype(F32))[0:8].astype(jnp.int32)
    sidt_ref[...] = turned
    for part in range(4):
        slot = iota((4 * CAP, ROW), 0) + part * 4 * CAP
        pick = hot((slot == turned[0:1]) | (slot == turned[1:2]))
        g_ref[part * 4 * CAP : (part + 1) * 4 * CAP, :] = nn(pick, cot_ref[...]).astype(BF)


def route(routes, cotangent):
    return pl.pallas_call(
        route_body,
        out_shape=[like(16 * CAP, D), like(ROW, 128, dtype=jnp.int32), like(8, ROW, dtype=jnp.int32)],
        compiler_params=pltpu.CompilerParams(vmem_limit_bytes=32 * MIB),
        cost_estimate=SMALL,
    )(routes, cotangent)


def forward_body(*refs):
    lens_ref, nat_ref, mask_ref, tok_ref, sid_ref, sidt_ref = refs[:6]
    pieces, refs = refs[6:14], refs[14:]
    w_out, h1p_out, qkv_out, probs_out, attnp_out, xmid_out, h2_out = refs[:7]
    gate_ref, vec_ref, router_ref, sent_ref = refs[7:11]
    w_ref, rest_ref, h1p_ref, qkv_ref, probs_ref, attn, attnp_ref, xmid_ref, h2_ref, bias = refs[11:21]
    sems = refs[21]
    rows = [pl.ds(at * 96, 96) for at in range(8)]
    small = [(piece.at[:, FF:], rest_ref.at[to, :]) for piece, to in zip(pieces, rows)]
    large = [(piece.at[:, :FF], w_ref.at[to, :]) for piece, to in zip(pieces, rows)]
    small, large = begin(sems, 0, *small), begin(sems, 8, *large)
    turn = hot(iota((D, D), 0) == nat_ref[...])
    x = tok_ref[...].astype(F32)
    x_hat = norm(x)[0]
    finish(small)
    rest = nn(turn, rest_ref[...])
    vectors = jnp.transpose(rest)[16:24]
    router_ref[...] = rest.astype(BF)
    vec_ref[...] = vectors
    h1 = (x_hat * vectors[0:1] + vectors[2:3]).astype(BF)
    h1p_ref[...] = nn(h1, turn).astype(BF)
    finish(large)
    away = begin(sems, 0, (w_ref, w_out), (h1p_ref, h1p_out))
    for part in range(3):
        cols = slice(part * D, (part + 1) * D)
        qkv_ref[:, cols] = nn(h1p_ref[...], w_ref[:, cols]).astype(BF)
    away += begin(sems, 2, (qkv_ref, qkv_out))

    end_one = lens_ref[0]
    end_two = end_one + lens_ref[1]

    def segment(place):
        return (place >= end_one).astype(jnp.int32) + (place >= end_two).astype(jnp.int32)

    query, key = iota((ROW, ROW), 0), iota((ROW, ROW), 1)
    same = segment(iota((ROW, 1), 0)) == segment(iota((1, ROW), 1))
    allowed = same & (key <= query) & ((mask_ref[...] == 1) | (key == query))
    bias[...] = jnp.where(allowed, 0.0, -1e30)
    low = iota((1, 128), 1) < 64
    half = ROW // 2
    zero = jnp.zeros((), BF)

    def pair(index, carry):
        at = pl.multiple_of(index * 128, 128)
        q = qkv_ref[:, pl.ds(at, 128)] * jnp.asarray(0.125, BF)
        k = qkv_ref[:, pl.ds(D + at, 128)]
        v = qkv_ref[:, pl.ds(2 * D + at, 128)]
        out = [None, None]
        for head in range(2):
            mine = low if head == 0 else jnp.logical_not(low)
            k_mine, v_mine = jnp.where(mine, k, zero), jnp.where(mine, v, zero)
            for block in range(2):
                count, rows = half * (block + 1), slice(block * half, (block + 1) * half)
                scores = nt(q[rows], k_mine[:count]) + bias[rows, :count]
                e = jnp.exp(scores - jnp.max(scores, 1, keepdims=True))
                probs = (e * (1.0 / jnp.sum(e, 1, keepdims=True))).astype(BF)
                probs_ref[2 * index + head, rows, :count] = probs
                if block == 0:
                    probs_ref[2 * index + head, rows, count:] = jnp.zeros((half, half), BF)
                term = nn(probs, v_mine[:count])
                out[block] = term if head == 0 else out[block] + term
        for block in range(2):
            attn[block * half : (block + 1) * half, pl.ds(at, 128)] = out[block].astype(BF)
        heads = pl.ds(2 * index, 2)
        begin(sems, 8 + index, (probs_ref.at[heads], probs_out.at[heads]))
        return carry

    lax.fori_loop(0, 6, pair, 0)
    for index in range(6):
        heads = pl.ds(2 * index, 2)
        away.append(
            pltpu.make_async_copy(probs_ref.at[heads], probs_out.at[heads], sems.at[8 + index])
        )
    attnp_ref[...] = nn(attn[...], turn).astype(BF)
    x_mid = x + nn(attnp_ref[...], w_ref[:, 3 * D :])
    xmid_ref[...] = x_mid
    h2 = (norm(x_mid)[0] * vectors[1:2] + vectors[3:4]).astype(BF)
    h2_ref[...] = h2
    away += begin(sems, 3, (attnp_ref, attnp_out), (xmid_ref, xmid_out), (h2_ref, h2_out))
    logits = nn(h2, router_ref[...])
    lane = iota((ROW, 128), 1)
    s0, s1, r0, r1 = (sid_ref[:, at : at + 1] for at in range(4))
    c0 = jnp.sum(jnp.where(lane == r0, logits, 0.0), 1, keepdims=True)
    c1 = jnp.sum(jnp.where(lane == r1, logits, 0.0), 1, keepdims=True)
    g0, g1 = 1.0 / (1.0 + jnp.exp(c1 - c0)), 1.0 / (1.0 + jnp.exp(c0 - c1))
    gate_ref[...] = jnp.where(lane == 0, g0, jnp.where(lane == 1, g1, 0.0))
    for part in range(4):
        slot = iota((4 * CAP, ROW), 0) + part * 4 * CAP
        pick = hot((slot == sidt_ref[0:1]) | (slot == sidt_ref[1:2]))
        rows = nn(pick, h2_ref[...]).astype(BF)
        for i in range(4):
            for j in range(6):
                block = rows[i * CAP : (i + 1) * CAP, j * 128 : (j + 1) * 128]
                sent_ref[4 * part + i, j * CAP : (j + 1) * CAP, :] = block
    for expert in range(16):
        slot = lane + expert * CAP
        line = jnp.sum(
            jnp.where(slot == s0, g0, 0.0) + jnp.where(slot == s1, g1, 0.0), 0, keepdims=True
        )
        sent_ref[expert, 6 * CAP : LINE, :] = tail_of(line)
    finish(away)


def forward(lens, nat, mask, tokens, sid, sidt, pieces):
    vmem = pl.BlockSpec(memory_space=pltpu.VMEM)
    anywhere = pl.BlockSpec(memory_space=pl.ANY)
    moved = [
        like(D, FF),
        like(ROW, D),
        like(ROW, 3 * D),
        like(12, ROW, ROW),
        like(ROW, D),
        like(ROW, D, dtype=F32),
        like(ROW, D),
    ]
    held = [like(ROW, 128, dtype=F32), like(8, D, dtype=F32), like(D, 128), like(16, LINE, 128)]
    buffers = [like(D, FF), like(D, 128), *moved[1:4], like(ROW, D), *moved[4:]]
    return pl.pallas_call(
        forward_body,
        in_specs=[pl.BlockSpec(memory_space=pltpu.SMEM)] + [vmem] * 5 + [anywhere] * 8,
        out_specs=[anywhere] * 7 + [vmem] * 4,
        out_shape=moved + held,
        scratch_shapes=[pltpu.VMEM(b.shape, b.dtype) for b in buffers]
        + [pltpu.VMEM((ROW, ROW), F32), pltpu.SemaphoreType.DMA((16,))],
        compiler_params=pltpu.CompilerParams(vmem_limit_bytes=56 * MIB),
        cost_estimate=SMALL,
    )(lens, nat, mask, tokens, sid, sidt, *pieces)


def expert_body(
    place_ref, sent_ref, g_ref, near_in, far_in, out_ref, back_ref, x_ref, dout_ref, act_ref,
    dup_ref, up_ref, down_ref, sems,
):
    def loads():
        for source, y in ((near_in, place_ref[1]), (far_in, 1 - place_ref[1])):
            for x in range(4):
                block = 2 * x + y
                for j in range(4):
                    rows, cols = pl.ds(block * 96, 96), pl.ds(j * D, D)
                    yield source.at[pl.ds(x * D + j * 96, 96), :], up_ref.at[rows, cols]
                rows = pl.ds(block * 384, 384)
                yield source.at[pl.ds(x * D + 384, 384), :], down_ref.at[rows, :]

    @pl.when(pl.program_id(0) == 0)
    def _():
        copies = [
            pltpu.make_async_copy(source, target, sems.at[i])
            for i, (source, target) in enumerate(loads())
        ]
        for copy in copies:
            copy.start()
        for copy in copies:
            copy.wait()

    for s in range(SOURCES):
        first, last = s * CAP, (s + 1) * CAP
        for j in range(6):
            x_ref[first:last, j * 128 : (j + 1) * 128] = sent_ref[s, j * CAP : (j + 1) * CAP, :]
        gate = line_of(sent_ref[s, 6 * CAP : LINE, :])
        column = jnp.transpose(jnp.broadcast_to(gate, (128, 128)))[:CAP, :1]
        dout_ref[first:last, :] = (g_ref[s].astype(F32) * column).astype(BF)
    x, d_out = x_ref[...], dout_ref[...]
    for part in range(FF // 256):
        cols = slice(part * 256, (part + 1) * 256)
        up = nn(x, up_ref[:, cols])
        d_act = nt(d_out, down_ref[cols, :])
        square = up * up
        t = jnp.tanh(up * (GELU_ONE + GELU_CUBE * square))
        a = 0.5 + 0.5 * t
        act_ref[:, cols] = (up * a).astype(BF)
        slope = a + (up * (1.0 - t * t)) * (0.5 * GELU_ONE + 1.5 * GELU_CUBE * square)
        dup_ref[:, cols] = (d_act * slope).astype(BF)
    out = nn(act_ref[...], down_ref[...]).astype(BF)
    back = nt(dup_ref[...], up_ref[...]).astype(BF)
    for s in range(SOURCES):
        out_ref[s] = out[s * CAP : (s + 1) * CAP]
        for j in range(6):
            block = back[s * CAP : (s + 1) * CAP, j * 128 : (j + 1) * 128]
            back_ref[s, j * CAP : (j + 1) * CAP, :] = block
    for s in range(SOURCES):
        d_gate = jnp.sum(out_ref[s].astype(F32) * g_ref[s].astype(F32), -1, keepdims=True)
        d_gate = jnp.broadcast_to(d_gate, (CAP, 128))
        wide = jnp.concatenate([d_gate, jnp.zeros((128 - CAP, 128), F32)], 0)
        back_ref[s, 6 * CAP : LINE, :] = tail_of(jnp.transpose(wide)[0:1])


def experts(place, sent, g, near, far):
    rows = SOURCES * CAP
    anywhere = pl.BlockSpec(memory_space=pl.ANY)
    by_source = pl.BlockSpec((SOURCES, CAP, D), lambda i: (i, 0, 0))
    message = pl.BlockSpec((SOURCES, LINE, 128), lambda i: (i, 0, 0))
    by_rows = lambda width: pl.BlockSpec((rows, width), lambda i: (i, 0))
    return pl.pallas_call(
        expert_body,
        grid=(16 // SOURCES,),
        in_specs=[
            pl.BlockSpec(memory_space=pltpu.SMEM),
            message,
            by_source,
        ]
        + [anywhere] * 2,
        out_specs=[
            by_source, message, by_rows(D), by_rows(D), by_rows(FF), by_rows(FF),
        ],
        out_shape=[
            like(16, CAP, D),
            like(16, LINE, 128),
            like(16 * CAP, D),
            like(16 * CAP, D),
            like(16 * CAP, FF),
            like(16 * CAP, FF),
        ],
        scratch_shapes=[
            pltpu.VMEM((D, FF), BF),
            pltpu.VMEM((FF, D), BF),
            pltpu.SemaphoreType.DMA((40,)),
        ],
        compiler_params=pltpu.CompilerParams(vmem_limit_bytes=60 * MIB),
        cost_estimate=SMALL,
    )(place, sent, g, near, far)


def up_grad_body(x_ref, dup_ref, keep_ref, first_ref, last_ref):
    grad = tn(x_ref[...], dup_ref[...]).astype(BF)
    for block in range(8):
        rows, low = block * 96, (block % 4) * 48
        keep_ref[block * 48 : (block + 1) * 48, :] = grad[rows : rows + 48]
        away_ref = (first_ref, last_ref)[block // 4]
        away_ref[low : low + 48, :] = grad[rows + 48 : rows + 96]


def up_grad(x, d_up):
    columns = lambda rows: pl.BlockSpec((rows, D), lambda i: (0, i))
    return pl.pallas_call(
        up_grad_body,
        grid=(4,),
        in_specs=[pl.BlockSpec((16 * CAP, D), lambda i: (0, 0)), columns(16 * CAP)],
        out_specs=[columns(384), columns(192), columns(192)],
        out_shape=[like(384, FF), like(192, FF), like(192, FF)],
        compiler_params=pltpu.CompilerParams(vmem_limit_bytes=48 * MIB),
        cost_estimate=SMALL,
    )(x, d_up)


def down_grad_body(dout_ref, act_ref, keep_ref, first_ref, last_ref):
    grad = tn(act_ref[...], dout_ref[...]).astype(BF)
    for block in range(2):
        keep_ref[block * 192 : (block + 1) * 192, :] = grad[block * 384 : block * 384 + 192]
    away = jnp.concatenate([grad[192:384], grad[576:768]], 0)
    for part, away_ref in enumerate((first_ref, last_ref)):

        @pl.when(pl.program_id(0) // 2 == part)
        def _():
            away_ref[...] = away


def down_grad(d_out, act):
    rows = lambda index: pl.BlockSpec((384, D), index)
    return pl.pallas_call(
        down_grad_body,
        grid=(4,),
        in_specs=[
            pl.BlockSpec((16 * CAP, D), lambda i: (0, 0)),
            pl.BlockSpec((16 * CAP, D), lambda i: (0, i)),
        ],
        out_specs=[
            rows(lambda i: (i, 0)),
            rows(lambda i: (jnp.minimum(i, 1), 0)),
            rows(lambda i: (jnp.maximum(i - 2, 0), 0)),
        ],
        out_shape=[like(1536, D), like(768, D), like(768, D)],
        compiler_params=pltpu.CompilerParams(vmem_limit_bytes=48 * MIB),
        cost_estimate=SMALL,
    )(d_out, act)


def put_rows(keep_ref, away_ref, cols, values):
    for step in range(4):
        rows = slice(step * 96, (step + 1) * 96)
        keep_ref[rows, cols] = values[step * 192 : step * 192 + 96]
        away_ref[rows, cols] = values[step * 192 + 96 : (step + 1) * 192]


def attention_back(base, pairs, dattn_ref, probs_ref, qkv_ref, d_qkv):
    width = 128 * pairs
    low = iota((1, 128), 1) < 64
    zero = jnp.zeros((), BF)
    half = ROW // 2

    def add(terms, at, term):
        terms[at] = term if terms[at] is None else terms[at] + term

    def pair(index, carry):
        at = pl.multiple_of((base + index) * 128, 128)
        to = pl.multiple_of(index * 128, 128)
        q, k, v = (qkv_ref[:, pl.ds(part * D + at, 128)] for part in range(3))
        d_attn = dattn_ref[:, pl.ds(at, 128)]
        dq, dk, dv = [None, None], [None, None], [None, None]
        for head in range(2):
            mine = low if head == 0 else jnp.logical_not(low)
            q_mine, k_mine, v_mine, d_mine = (jnp.where(mine, t, zero) for t in (q, k, v, d_attn))
            for block in range(2):
                count, rows = half * (block + 1), slice(block * half, (block + 1) * half)
                probs = probs_ref[2 * index + head, rows, :count]
                d_probs = nt(d_mine[rows], v_mine[:count])
                wide = probs.astype(F32)
                weighted = wide * d_probs
                delta = jnp.sum(weighted, 1, keepdims=True)
                d_scores = (weighted - wide * delta).astype(BF)
                add(dq, block, nn(d_scores, k_mine[:count]))
                for other in range(block + 1):
                    keys = slice(other * half, (other + 1) * half)
                    add(dk, other, tn(d_scores[:, keys], q_mine[rows]))
                    add(dv, other, tn(probs[:, keys], d_mine[rows]))
        for block in range(2):
            rows = slice(block * half, (block + 1) * half)
            d_qkv[rows, pl.ds(to, 128)] = (dq[block] * 0.125).astype(BF)
            d_qkv[rows, pl.ds(width + to, 128)] = (dk[block] * 0.125).astype(BF)
            d_qkv[rows, pl.ds(2 * width + to, 128)] = dv[block].astype(BF)
        return carry

    lax.fori_loop(0, pairs, pair, 0)


def back_one_body(
    nat_ref, sid_ref, gate_ref, router_ref, vec_ref, dback_in, xmid_in, cot_in, w_in, attnp_in,
    h2_in, probs_in, qkv_in, h1p_in, dxm_out, dattn_out, dqkv_out, keep_out, away_out,
    dback_ref, xmid_ref, cot_ref, w_ref, attnp_ref, h2_ref, probs_ref, qkv_ref, h1p_ref, dxm_ref,
    dattn_ref, dqkv_ref, keep_ref, away_ref, slots_ref, sems,
):
    sources = (
        dback_in, xmid_in, cot_in, w_in.at[:, 3 * D :], attnp_in, h2_in, qkv_in, probs_in.at[:8], h1p_in,
    )
    targets = (dback_ref, xmid_ref, cot_ref, w_ref, attnp_ref, h2_ref, qkv_ref, probs_ref, h1p_ref)
    pairs = list(zip(sources, targets))
    loads = begin(sems, 0, *pairs[:1])
    turn = hot(iota((D, D), 0) == nat_ref[...])
    lane = iota((ROW, 128), 1)
    s0, s1, r0, r1 = (sid_ref[:, at : at + 1] for at in range(4))
    finish(loads)
    loads += begin(sems, 1, *pairs[1:])
    a0 = a1 = jnp.zeros((ROW, 128), F32)
    for expert in range(16):
        line = line_of(dback_ref[expert, 6 * CAP : LINE, :])
        slot = jnp.where(lane < CAP, lane + expert * CAP, -2)
        a0 = a0 + jnp.where(slot == s0, line, 0.0)
        a1 = a1 + jnp.where(slot == s1, line, 0.0)
    dg0, dg1 = jnp.sum(a0, 1, keepdims=True), jnp.sum(a1, 1, keepdims=True)
    g0, g1 = gate_ref[:, 0:1], gate_ref[:, 1:2]
    both = g0 * dg0 + g1 * dg1
    d_logits = jnp.where(lane == r0, g0 * (dg0 - both), 0.0)
    d_logits = d_logits + jnp.where(lane == r1, g1 * (dg1 - both), 0.0)
    high = d_logits.astype(BF)
    low = (d_logits - high.astype(F32)).astype(BF)
    d_h2 = nt(high, router_ref[...]) + nt(low, router_ref[...])
    for part in range(4):
        for i in range(4):
            for j in range(6):
                block = dback_ref[4 * part + i, j * CAP : (j + 1) * CAP, :]
                slots_ref[i * CAP : (i + 1) * CAP, j * 128 : (j + 1) * 128] = block
        slot = iota((ROW, 4 * CAP), 1) + part * 4 * CAP
        pick = hot((slot == s0) | (slot == s1))
        d_h2 = d_h2 + nn(pick, slots_ref[...])
    finish(loads[1:3])
    x_hat, scale = norm(xmid_ref[...])
    d_in, d_gain, d_bias = norm_back(d_h2, x_hat, scale, vec_ref[1:2])
    d_x_mid = cot_ref[...].astype(F32) + d_in
    dxm_ref[...] = d_x_mid
    d_proj = d_x_mid.astype(BF)
    finish(loads[3:6])
    dattn_ref[...] = nt(nt(d_proj, w_ref[...]).astype(BF), turn).astype(BF)
    leaving = begin(sems, 9, (dxm_ref, dxm_out), (dattn_ref, dattn_out))
    put_rows(keep_ref, away_ref, slice(0, D), tn(attnp_ref[...], d_proj).astype(BF))
    d_router = tn(h2_ref[...], high) + tn(h2_ref[...], low)
    sub = iota((128, D), 0)
    rows = jnp.where(sub == 17, d_gain, 0.0) + jnp.where(sub == 19, d_bias, 0.0)
    small = d_router + jnp.transpose(rows)
    put_rows(keep_ref, away_ref, slice(D, D + 128), tn(turn, small.astype(BF)).astype(BF))
    cols = slice(0, D + 128)
    leaving += begin(
        sems, 11, (keep_ref.at[:, cols], keep_out.at[:, cols]), (away_ref.at[:, cols], away_out.at[:, cols])
    )
    finish(loads[6:8])
    attention_back(0, 4, dattn_ref, probs_ref, qkv_ref, dqkv_ref)
    leaving += begin(sems, 13, (dqkv_ref, dqkv_out))
    finish(loads[8:])
    for part in range(3):
        cols = slice(D + 128 + part * 512, D + 128 + (part + 1) * 512)
        grad = tn(h1p_ref[...], dqkv_ref[:, part * 512 : (part + 1) * 512]).astype(BF)
        put_rows(keep_ref, away_ref, cols, grad)
        leaving += begin(
            sems,
            14 + 2 * part,
            (keep_ref.at[:, cols], keep_out.at[:, cols]),
            (away_ref.at[:, cols], away_out.at[:, cols]),
        )
    finish(leaving)


def back_one(nat, sid, gate, router, vec, d_back, x_mid, cotangent, w, attnp, h2, probs, qkv, h1p):
    vmem = pl.BlockSpec(memory_space=pltpu.VMEM)
    anywhere = pl.BlockSpec(memory_space=pl.ANY)
    ins = [
        like(16, LINE, 128), like(ROW, D, dtype=F32), like(ROW, D), like(D, D), like(ROW, D),
        like(ROW, D), like(8, ROW, ROW), like(ROW, 3 * D), like(ROW, D),
    ]
    outs = [
        like(ROW, D, dtype=F32), like(ROW, D), like(ROW, 1536), like(384, 2432), like(384, 2432),
    ]
    return pl.pallas_call(
        back_one_body,
        in_specs=[vmem] * 5 + [anywhere] * 9,
        out_specs=[anywhere] * 5,
        out_shape=outs,
        scratch_shapes=[pltpu.VMEM(b.shape, b.dtype) for b in ins + outs]
        + [pltpu.VMEM((4 * CAP, D), BF), pltpu.SemaphoreType.DMA((20,))],
        compiler_params=pltpu.CompilerParams(vmem_limit_bytes=56 * MIB),
        cost_estimate=SMALL,
    )(nat, sid, gate, router, vec, d_back, x_mid, cotangent, w, attnp, h2, probs, qkv, h1p)


def back_two_body(
    nat_ref, vec_ref, dattn_in, probs_in, qkv_in, h1p_in, first_in, w_in, tok_in, dxm_in,
    gx_out, keep_out, away_out, dattn_ref, probs_ref, qkv_ref, h1p_ref, first_ref, w_ref, tok_ref,
    dxm_ref, gx_ref, keep_ref, away_ref, second_ref, sems,
):
    sources = (
        dattn_in, qkv_in, probs_in.at[8:], h1p_in, first_in, w_in.at[:, : 3 * D], tok_in, dxm_in,
    )
    targets = (dattn_ref, qkv_ref, probs_ref, h1p_ref, first_ref, w_ref, tok_ref, dxm_ref)
    pairs = list(zip(sources, targets))
    loads = begin(sems, 0, *pairs[:3])
    turn = hot(iota((D, D), 0) == nat_ref[...])
    finish(loads)
    loads += begin(sems, 3, *pairs[3:])
    attention_back(4, 2, dattn_ref, probs_ref, qkv_ref, second_ref)
    finish(loads[3:6])
    d_h1p = jnp.zeros((ROW, D), F32)
    for part in range(3):
        middle = part * D + 512
        d_second = second_ref[:, part * 256 : (part + 1) * 256]
        grad = tn(h1p_ref[...], d_second).astype(BF)
        put_rows(keep_ref, away_ref, slice(part * 256, (part + 1) * 256), grad)
        d_h1p = d_h1p + nt(first_ref[:, part * 512 : (part + 1) * 512], w_ref[:, part * D : middle])
        d_h1p = d_h1p + nt(d_second, w_ref[:, middle : (part + 1) * D])
    cols = slice(0, D)
    leaving = begin(
        sems, 8, (keep_ref.at[:, cols], keep_out.at[:, cols]), (away_ref.at[:, cols], away_out.at[:, cols])
    )
    finish(loads[6:])
    d_h1 = nt(d_h1p.astype(BF), turn)
    x_hat, scale = norm(tok_ref[...].astype(F32))
    d_in, d_gain, d_bias = norm_back(d_h1, x_hat, scale, vec_ref[0:1])
    gx_ref[...] = dxm_ref[...] + d_in
    leaving += begin(sems, 10, (gx_ref, gx_out))
    sub = iota((128, D), 0)
    rows = jnp.where(sub == 16, d_gain, 0.0) + jnp.where(sub == 18, d_bias, 0.0)
    small = tn(turn, jnp.transpose(rows).astype(BF)).astype(BF)
    cols = slice(D, D + 128)
    put_rows(keep_ref, away_ref, cols, small)
    leaving += begin(
        sems, 11, (keep_ref.at[:, cols], keep_out.at[:, cols]), (away_ref.at[:, cols], away_out.at[:, cols])
    )
    finish(leaving)


def back_two(nat, vec, d_attn, probs, qkv, h1p, first, w, tokens, d_x_mid):
    vmem = pl.BlockSpec(memory_space=pltpu.VMEM)
    anywhere = pl.BlockSpec(memory_space=pl.ANY)
    ins = [
        like(ROW, D), like(4, ROW, ROW), like(ROW, 3 * D), like(ROW, D), like(ROW, 1536),
        like(D, 3 * D), like(ROW, D), like(ROW, D, dtype=F32),
    ]
    outs = [like(ROW, D, dtype=F32), like(384, 896), like(384, 896)]
    return pl.pallas_call(
        back_two_body,
        in_specs=[vmem] * 2 + [anywhere] * 8,
        out_specs=[anywhere] * 3,
        out_shape=outs,
        scratch_shapes=[pltpu.VMEM(b.shape, b.dtype) for b in ins + outs]
        + [pltpu.VMEM((ROW, D), BF), pltpu.SemaphoreType.DMA((13,))],
        compiler_params=pltpu.CompilerParams(vmem_limit_bytes=56 * MIB),
        cost_estimate=SMALL,
    )(nat, vec, d_attn, probs, qkv, h1p, first, w, tokens, d_x_mid)


def merge_body(sid_ref, ret_ref, gate_ref, xmid_ref, out_ref):
    s0, s1 = sid_ref[:, 0:1], sid_ref[:, 1:2]
    y0 = y1 = jnp.zeros((ROW, D), F32)
    for part in range(4):
        slot = iota((ROW, 4 * CAP), 1) + part * 4 * CAP
        values = ret_ref[part * 4 * CAP : (part + 1) * 4 * CAP, :]
        y0 = y0 + nn(hot(slot == s0), values)
        y1 = y1 + nn(hot(slot == s1), values)
    out_ref[...] = (xmid_ref[...] + (gate_ref[:, 0:1] * y0 + gate_ref[:, 1:2] * y1)).astype(BF)


def merge(sid, returned, gate, x_mid):
    return pl.pallas_call(
        merge_body,
        out_shape=like(ROW, D),
        compiler_params=pltpu.CompilerParams(vmem_limit_bytes=40 * MIB),
        cost_estimate=SMALL,
    )(sid, returned, gate, x_mid)


def to_blocks_body(place_ref, *refs):
    count = (len(refs) - 3) // 2
    held = refs[count + 1 : 2 * count + 1]
    out_ref, total, sems = refs[count], refs[-2], refs[-1]
    sources = [ref.at[pl.ds(0, 96), :] for ref in refs[:count]]
    loads = begin(sems, 0, *zip(sources, held))
    col = 0
    total[96:104, :] = jnp.zeros((8, total.shape[1]), F32)
    for group in range(count // 5):
        mine = slice(5 * group, 5 * group + 5)
        finish(loads[mine])
        value = held[5 * group][...].astype(F32)
        for part in held[mine][1:]:
            value = value + part[...].astype(F32)
        total[0:96, col : col + value.shape[1]] = value
        col += value.shape[1]
    x, y = place_ref[0], 2 * place_ref[1] + place_ref[2]
    for k in range(16):
        to = lax.rem(x - k % 4 + 4, 4) * 4 + lax.rem(y - k // 4 + 4, 4)
        out_ref[to] = total[6 * k : 6 * k + 8, :].astype(BF)


def to_blocks(place, parts):
    width = sum(part.shape[1] for part in parts[::5])
    return pl.pallas_call(
        to_blocks_body,
        in_specs=[pl.BlockSpec(memory_space=pltpu.SMEM)]
        + [pl.BlockSpec(memory_space=pl.ANY)] * len(parts),
        out_shape=like(16, 8, width),
        scratch_shapes=[pltpu.VMEM((96, part.shape[1]), BF) for part in parts]
        + [pltpu.VMEM((104, width), F32), pltpu.SemaphoreType.DMA((len(parts),))],
        compiler_params=pltpu.CompilerParams(vmem_limit_bytes=60 * MIB),
        cost_estimate=SMALL,
    )(place, *parts)


def from_blocks_body(in_ref, qkv_ref, out_ref, small_ref):
    total = in_ref[0].astype(F32)
    for k in range(1, 16):
        total = total + in_ref[k].astype(F32)
    out_ref[...] = total[:6, :D]
    for part in range(3):
        qkv_ref[:, part * D : part * D + 512] = total[:6, 896 + part * 512 : 1408 + part * 512]
        qkv_ref[:, part * D + 512 : (part + 1) * D] = total[:6, 2432 + part * 256 : 2688 + part * 256]
    small_ref[...] = total[:6, D : D + 128] + total[:6, 3200:3328]


def from_blocks(blocks):
    return pl.pallas_call(
        from_blocks_body,
        out_shape=[like(6, 3 * D, dtype=F32), like(6, D, dtype=F32), like(6, 128, dtype=F32)],
        compiler_params=pltpu.CompilerParams(vmem_limit_bytes=16 * MIB),
        cost_estimate=SMALL,
    )(blocks)


def prepare_body(core_ref, *refs):
    sources, (block_ref, mine_ref, other_ref) = refs[:9], refs[9:12]
    held, turned, sems = refs[12:21], refs[21], refs[22]
    loads = begin(sems, 0, *zip(sources, held))
    qkv_ref, out_ref, router_ref, gains_ref, biases_ref, up_t, down_t, up_f, down_f = held
    finish(loads[:5])
    block_ref[...] = jnp.zeros(block_ref.shape, BF)
    block_ref[0:6, : 3 * D] = qkv_ref[...].astype(BF)
    block_ref[0:6, 3 * D : FF] = out_ref[...].astype(BF)
    turned[...] = jnp.zeros((128, 128), F32)
    turned[16:18, 0:6] = gains_ref[...]
    turned[18:20, 0:6] = biases_ref[...]
    vectors = jnp.transpose(turned[...])[0:8]
    turned[0:6, 0:16] = router_ref[...]
    keep = iota((8, 128), 1) < 16
    small = jnp.where(keep, turned[0:8, :], vectors)
    small = jnp.where(iota((8, 128), 0) < 6, small, 0.0)
    block_ref[:, FF:] = small.astype(BF)
    trained = core_ref[0] == 0
    finish(loads[5:])
    for j in range(4):
        cols, rows = slice(j * D, (j + 1) * D), slice(j * 48, (j + 1) * 48)
        low, fixed = up_t[0, :, cols].astype(BF), up_f[0, :, cols]
        mine_ref[rows, :] = jnp.where(trained, low, fixed)
        other_ref[rows, :] = jnp.where(trained, fixed, low)
    low = down_t[0].astype(BF)
    mine_ref[192:, :] = jnp.where(trained, low, down_f[0])
    other_ref[192:, :] = jnp.where(trained, down_f[0], low)


def prepare(core, *arrays):
    anywhere = pl.BlockSpec(memory_space=pl.ANY)
    return pl.pallas_call(
        prepare_body,
        in_specs=[pl.BlockSpec(memory_space=pltpu.SMEM)] + [anywhere] * 9,
        out_shape=[like(8, FF + 128), like(384, D), like(384, D)],
        scratch_shapes=[pltpu.VMEM(array.shape, array.dtype) for array in arrays]
        + [pltpu.VMEM((128, 128), F32), pltpu.SemaphoreType.DMA((9,))],
        compiler_params=pltpu.CompilerParams(vmem_limit_bytes=60 * MIB),
        cost_estimate=SMALL,
    )(core, *arrays)


def pack_body(core_ref, mine_in, got_in, to_ref, sems):
    pairs = []
    for source, core in ((mine_in, core_ref[0]), (got_in, 1 - core_ref[0])):
        for j in range(4):
            rows = pl.ds(j * 96 + core * 48, 48)
            pairs.append((source.at[pl.ds(j * 48, 48), :], to_ref.at[rows, :]))
        pairs.append((source.at[pl.ds(192, 192), :], to_ref.at[pl.ds(384 + core * 192, 192), :]))
    finish(begin(sems, 0, *pairs))


def pack(core, mine, got):
    anywhere = pl.BlockSpec(memory_space=pl.ANY)
    return pl.pallas_call(
        pack_body,
        in_specs=[pl.BlockSpec(memory_space=pltpu.SMEM)] + [anywhere] * 2,
        out_shape=like(D, D),
        scratch_shapes=[pltpu.SemaphoreType.DMA((10,))],
        compiler_params=pltpu.CompilerParams(vmem_limit_bytes=16 * MIB),
        cost_estimate=SMALL,
    )(core, mine, got)


def shift(value, axis, by):
    count = lax.axis_size(axis)
    return lax.ppermute(value, axis, [(i, (i + by) % count) for i in range(count)])


def ordered(mine, other, index):
    first = jnp.where(index == 0, mine, other)
    second = jnp.where(index == 0, other, mine)
    return first, second


FAR = ("x", "yh", "yl")
PEERS = ("c", "z", "yl")


def to_all(rows, names):
    return lax.all_to_all(rows, names, split_axis=0, concat_axis=0, tiled=True)


def spread_x(block):
    return jnp.stack([block] + [shift(block, "x", step) for step in (1, 2, 3)])


def spread_y(along_x):
    near = [along_x] + [shift(along_x, ("yh", "yl"), step) for step in (1, 2, 3)]
    return jnp.stack(near)[:, :, :6].reshape(96, along_x.shape[2])


def natural_rows():
    x, c, z = (lax.axis_index(name) for name in ("x", "c", "z"))
    y = lax.axis_index("yh") * 2 + lax.axis_index("yl")
    row = jnp.arange(768)
    step, other, i = row // 192, (row // 96) % 2, row % 96
    core, deep = (c + other) % 2, (z - step) % 4
    high, long = (y - i // 24) % 4, (x - (i // 6) % 4) % 4
    device = ((long * 2 + high // 2) * 2 + core) * 8 + deep * 2 + high % 2
    return (device * 6 + i % 6).astype(jnp.int32)


def along_z(keep, got):
    parts = [keep, got]
    for step in (1, 2, 3):
        rows = slice(step * 96, (step + 1) * 96)
        both = keep[rows].astype(F32) + got[rows].astype(F32)
        parts.append(shift(both.astype(BF), "z", -step))
    return parts


def take_body(core_ref, *refs):
    sources, (to_ref, *held), sems = refs[1:3], refs[3:6], refs[6]
    rows = held[0].shape[0]

    @pl.when(core_ref[0] == 1)
    def _():
        targets = [to_ref.at[pl.ds(at, rows), :] for at in (0, rows)]
        loads, stores = begin(sems, 0, *zip(sources, held)), []
        for i in range(2):
            finish(loads[i : i + 1])
            stores += begin(sems, 2 + i, (held[i], targets[i]))
        finish(stores)


def take(core, kept, *sent):
    got = [lax.ppermute(part, "c", [(0, 1)]) for part in sent]
    anywhere = pl.BlockSpec(memory_space=pl.ANY)
    return pl.pallas_call(
        take_body,
        in_specs=[pl.BlockSpec(memory_space=pltpu.SMEM)] + [anywhere] * 3,
        out_specs=anywhere,
        out_shape=like(*kept.shape),
        input_output_aliases={1: 0},
        scratch_shapes=[pltpu.VMEM(part.shape, part.dtype) for part in got]
        + [pltpu.SemaphoreType.DMA((4,))],
        compiler_params=pltpu.CompilerParams(vmem_limit_bytes=60 * MIB),
        cost_estimate=SMALL,
    )(core, kept, *got)


def owned(mine, axis):
    return lax.psum_scatter(mine, axis, scatter_dimension=0, tiled=True)


def shards(
    tokens,
    seq_lengths,
    key_mask,
    routes,
    cotangent,
    qkv_weight,
    out_weight,
    router_weight,
    norm_gains,
    norm_biases,
    up_train,
    down_train,
    up_frozen,
    down_frozen,
):
    core = lax.axis_index("c")

    place = jnp.stack([lax.axis_index(name) for name in ("x", "yh", "yl")]).astype(jnp.int32)

    block, mine, other = prepare(
        core.reshape(1), qkv_weight, out_weight, router_weight, norm_gains, norm_biases, up_train,
        down_train, up_frozen, down_frozen,
    )
    other = shift(other, "c", 1)
    block, routes, other = lax.optimization_barrier((block, routes, other))
    along_x = spread_x(block)

    both = pack(core.reshape(1), mine, other)
    along_x, both = lax.optimization_barrier((along_x, both))
    rows = spread_y(along_x)
    nat = natural_rows().reshape(1, D)
    g_slots, sid, sidt = route(routes, cotangent)
    near = lax.all_gather(both, "x", tiled=True)

    rows, g_slots, both = lax.optimization_barrier((rows, g_slots, both))
    parts = [rows] + [shift(rows, "z", step) for step in (1, 2, 3)]
    both = shift(both, "yh", 1)
    parts, both, g_slots = lax.optimization_barrier((parts, both, g_slots))
    pieces = []
    for part in parts:
        pieces += [part, shift(part, "c", 1)]
    far = lax.all_gather(both, "x", tiled=True)

    g_rows = to_all(g_slots.reshape(16, CAP, D), PEERS)
    w, h1p, qkv, probs, attnp, x_mid, h2, gate, vec, router, sent = forward(
        seq_lengths[0], nat, key_mask.reshape(1, ROW), tokens, sid, sidt, pieces
    )
    sent, g_rows = lax.optimization_barrier((sent, g_rows))

    arrived = to_all(sent, PEERS)
    out, back, x_rows, d_out, act, d_up = experts(
        place, arrived, g_rows, near, far
    )
    d_back = to_all(back, PEERS)
    up_all = take(core.reshape(1), *up_grad(x_rows, d_up))
    down_all = take(core.reshape(1), *down_grad(d_out, act))
    d_back, out, up_all, down_all = lax.optimization_barrier((d_back, out, up_all, down_all))

    returned = to_all(out, PEERS)
    up_all, down_all = owned(up_all, "x"), owned(down_all, "x")
    d_x_mid, d_attn, first, keep, away = back_one(
        nat, sid, gate, router, vec, d_back, x_mid, cotangent, w, attnp, h2,
        probs, qkv, h1p,
    )
    input_grad, *last = back_two(nat, vec, d_attn, probs, qkv, h1p, first, w, tokens, d_x_mid)
    got = shift(away, "c", 1)
    keep, got, returned = lax.optimization_barrier((keep, got, returned))
    parts_one = along_z(keep, got)
    parts_one[2::2], last, up_all = lax.optimization_barrier((parts_one[2::2], last, up_all))
    up_all = owned(up_all, "yh")
    parts_two = along_z(last[0], shift(last[1], "c", 1))
    parts_two[2], down_all = lax.optimization_barrier((parts_two[2], down_all))
    down_all = owned(down_all, "yh")
    blocks = to_blocks(place, parts_one + parts_two)
    blocks, returned = lax.optimization_barrier((blocks, returned))
    own_qkv, own_out, small = from_blocks(to_all(blocks, FAR))
    grad_up, grad_down = up_all.astype(F32)[None], down_all.astype(F32)[None]
    block_out = merge(sid, returned.reshape(16 * CAP, D), gate, x_mid)
    return (
        block_out,
        input_grad,
        own_qkv,
        own_out,
        small[:, :16],
        small[:, 16:18].T,
        small[:, 18:20].T,
        grad_up,
        grad_down,
    )


def solution(mesh):
    fine = Mesh(mesh.devices.reshape(SIZES), NAMES)
    by_row = P(NAMES, None)
    by_column = P(None, NAMES)
    by_expert = P(NARROW, WIDE, None)
    return jax.shard_map(
        shards,
        mesh=fine,
        in_specs=(by_row, by_row, P(NAMES)) + (by_row,) * 5 + (by_column,) * 2 + (by_expert,) * 4,
        out_specs=(by_row,) * 5 + (by_column,) * 2 + (by_expert,) * 2,
        check_vma=False,
    )
```

```python
import functools

import jax
import jax.numpy as jnp
from jax import lax
from jax.experimental import pallas as pl
from jax.experimental.pallas import tpu as pltpu
from jax.sharding import Mesh
from jax.sharding import PartitionSpec as P

SIZES = (4, 2, 2, 4, 2)
NAMES = ("x", "yh", "c", "z", "yl")
WIDE = ("x", "yh", "c")
NARROW = ("z", "yl")
BF = jnp.bfloat16
F32 = jnp.float32
ROW = 512
D = 768
FF = 3072
CAP = 96
LINE = 592
SOURCES = 4
GELU_ONE = 0.7978845608028654
GELU_CUBE = GELU_ONE * 0.044715
MIB = 1024 * 1024
SMALL = pl.CostEstimate(flops=10**6, bytes_accessed=10**4, transcendentals=0)


def nn(a, b):
    return jnp.dot(a, b, preferred_element_type=F32)


def nt(a, b):
    return lax.dot_general(a, b, (((1,), (1,)), ((), ())), preferred_element_type=F32)


def tn(a, b):
    return lax.dot_general(a, b, (((0,), (0,)), ((), ())), preferred_element_type=F32)


def iota(shape, dim):
    return lax.broadcasted_iota(jnp.int32, shape, dim)


def hot(mask):
    return jnp.where(mask, 1.0, 0.0).astype(BF)


def like(*dims, dtype=BF):
    return jax.ShapeDtypeStruct(dims, dtype)


def tail_of(line):
    high = line.astype(BF).astype(F32)
    row = iota((16, 128), 0)
    return jnp.where(row == 0, high, jnp.where(row == 1, line - high, 0.0)).astype(BF)


def line_of(tail):
    tail = tail.astype(F32)
    return tail[0:1] + tail[1:2]


def begin(sems, first, *pairs):
    copies = [
        pltpu.make_async_copy(source, target, sems.at[first + i])
        for i, (source, target) in enumerate(pairs)
    ]
    for copy in copies:
        copy.start()
    return copies


def finish(copies):
    for copy in copies:
        copy.wait()


def norm(x):
    centered = x - jnp.mean(x, -1, keepdims=True)
    scale = lax.rsqrt(jnp.mean(centered * centered, -1, keepdims=True) + 1e-5)
    return centered * scale, scale


def norm_back(d_out, x_hat, scale, gain):
    t = d_out * gain
    d_in = scale * (
        t - jnp.mean(t, -1, keepdims=True) - x_hat * jnp.mean(t * x_hat, -1, keepdims=True)
    )
    return d_in, jnp.sum(d_out * x_hat, 0, keepdims=True), jnp.sum(d_out, 0, keepdims=True)


def route_body(routes_ref, cot_ref, g_ref, sid_ref, sidt_ref):
    lane = iota((ROW, 128), 1)
    r0, r1 = routes_ref[:, 0:1], routes_ref[:, 1:2]
    either = hot((lane == r0) | (lane == r1))
    earlier = nn(hot(iota((ROW, ROW), 1) < iota((ROW, ROW), 0)), either)
    p0 = jnp.sum(jnp.where(lane == r0, earlier, 0.0), 1, keepdims=True).astype(jnp.int32)
    p1 = jnp.sum(jnp.where(lane == r1, earlier, 0.0), 1, keepdims=True).astype(jnp.int32)
    columns = (
        jnp.where(p0 < CAP, r0 * CAP + p0, -1),
        jnp.where(p1 < CAP, r1 * CAP + p1, -1),
        r0,
    )
    table = jnp.broadcast_to(r1, (ROW, 128))
    for at, column in enumerate(columns):
        table = jnp.where(lane == at, column, table)
    sid_ref[...] = table
    turned = jnp.transpose(table.astype(F32))[0:8].astype(jnp.int32)
    sidt_ref[...] = turned
    for part in range(4):
        slot = iota((4 * CAP, ROW), 0) + part * 4 * CAP
        pick = hot((slot == turned[0:1]) | (slot == turned[1:2]))
        g_ref[part * 4 * CAP : (part + 1) * 4 * CAP, :] = nn(pick, cot_ref[...]).astype(BF)


def route(routes, cotangent):
    return pl.pallas_call(
        route_body,
        out_shape=[like(16 * CAP, D), like(ROW, 128, dtype=jnp.int32), like(8, ROW, dtype=jnp.int32)],
        compiler_params=pltpu.CompilerParams(vmem_limit_bytes=32 * MIB),
        cost_estimate=SMALL,
    )(routes, cotangent)


def forward_body(*refs):
    lens_ref, nat_ref, mask_ref, tok_ref, sid_ref, sidt_ref = refs[:6]
    pieces, refs = refs[6:14], refs[14:]
    w_out, h1p_out, qkv_out, probs_out, attnp_out, xmid_out, h2_out = refs[:7]
    gate_ref, vec_ref, router_ref, sent_ref = refs[7:11]
    w_ref, rest_ref, h1p_ref, qkv_ref, probs_ref, attn, attnp_ref, xmid_ref, h2_ref, bias = refs[11:21]
    sems = refs[21]
    rows = [pl.ds(at * 96, 96) for at in range(8)]
    small = [(piece.at[:, FF:], rest_ref.at[to, :]) for piece, to in zip(pieces, rows)]
    large = [(piece.at[:, :FF], w_ref.at[to, :]) for piece, to in zip(pieces, rows)]
    small, large = begin(sems, 0, *small), begin(sems, 8, *large)
    turn = hot(iota((D, D), 0) == nat_ref[...])
    x = tok_ref[...].astype(F32)
    x_hat = norm(x)[0]
    finish(small)
    rest = nn(turn, rest_ref[...])
    vectors = jnp.transpose(rest)[16:24]
    router_ref[...] = rest.astype(BF)
    vec_ref[...] = vectors
    h1 = (x_hat * vectors[0:1] + vectors[2:3]).astype(BF)
    h1p_ref[...] = nn(h1, turn).astype(BF)
    finish(large)
    away = begin(sems, 0, (w_ref, w_out), (h1p_ref, h1p_out))
    for part in range(3):
        cols = slice(part * D, (part + 1) * D)
        qkv_ref[:, cols] = nn(h1p_ref[...], w_ref[:, cols]).astype(BF)
    away += begin(sems, 2, (qkv_ref, qkv_out))

    end_one = lens_ref[0]
    end_two = end_one + lens_ref[1]

    def segment(place):
        return (place >= end_one).astype(jnp.int32) + (place >= end_two).astype(jnp.int32)

    query, key = iota((ROW, ROW), 0), iota((ROW, ROW), 1)
    same = segment(iota((ROW, 1), 0)) == segment(iota((1, ROW), 1))
    allowed = same & (key <= query) & ((mask_ref[...] == 1) | (key == query))
    bias[...] = jnp.where(allowed, 0.0, -1e30)
    low = iota((1, 128), 1) < 64
    half = ROW // 2
    zero = jnp.zeros((), BF)

    def pair(index, carry):
        at = pl.multiple_of(index * 128, 128)
        q = qkv_ref[:, pl.ds(at, 128)] * jnp.asarray(0.125, BF)
        k = qkv_ref[:, pl.ds(D + at, 128)]
        v = qkv_ref[:, pl.ds(2 * D + at, 128)]
        out = [None, None]
        for head in range(2):
            mine = low if head == 0 else jnp.logical_not(low)
            k_mine, v_mine = jnp.where(mine, k, zero), jnp.where(mine, v, zero)
            for block in range(2):
                count, rows = half * (block + 1), slice(block * half, (block + 1) * half)
                scores = nt(q[rows], k_mine[:count]) + bias[rows, :count]
                e = jnp.exp(scores - jnp.max(scores, 1, keepdims=True))
                probs = (e * (1.0 / jnp.sum(e, 1, keepdims=True))).astype(BF)
                probs_ref[2 * index + head, rows, :count] = probs
                if block == 0:
                    probs_ref[2 * index + head, rows, count:] = jnp.zeros((half, half), BF)
                term = nn(probs, v_mine[:count])
                out[block] = term if head == 0 else out[block] + term
        for block in range(2):
            attn[block * half : (block + 1) * half, pl.ds(at, 128)] = out[block].astype(BF)
        heads = pl.ds(2 * index, 2)
        begin(sems, 8 + index, (probs_ref.at[heads], probs_out.at[heads]))
        return carry

    lax.fori_loop(0, 6, pair, 0)
    for index in range(6):
        heads = pl.ds(2 * index, 2)
        away.append(
            pltpu.make_async_copy(probs_ref.at[heads], probs_out.at[heads], sems.at[8 + index])
        )
    attnp_ref[...] = nn(attn[...], turn).astype(BF)
    x_mid = x + nn(attnp_ref[...], w_ref[:, 3 * D :])
    xmid_ref[...] = x_mid
    h2 = (norm(x_mid)[0] * vectors[1:2] + vectors[3:4]).astype(BF)
    h2_ref[...] = h2
    away += begin(sems, 3, (attnp_ref, attnp_out), (xmid_ref, xmid_out), (h2_ref, h2_out))
    logits = nn(h2, router_ref[...])
    lane = iota((ROW, 128), 1)
    s0, s1, r0, r1 = (sid_ref[:, at : at + 1] for at in range(4))
    c0 = jnp.sum(jnp.where(lane == r0, logits, 0.0), 1, keepdims=True)
    c1 = jnp.sum(jnp.where(lane == r1, logits, 0.0), 1, keepdims=True)
    g0, g1 = 1.0 / (1.0 + jnp.exp(c1 - c0)), 1.0 / (1.0 + jnp.exp(c0 - c1))
    gate_ref[...] = jnp.where(lane == 0, g0, jnp.where(lane == 1, g1, 0.0))
    for part in range(4):
        slot = iota((4 * CAP, ROW), 0) + part * 4 * CAP
        pick = hot((slot == sidt_ref[0:1]) | (slot == sidt_ref[1:2]))
        rows = nn(pick, h2_ref[...]).astype(BF)
        for i in range(4):
            for j in range(6):
                block = rows[i * CAP : (i + 1) * CAP, j * 128 : (j + 1) * 128]
                sent_ref[4 * part + i, j * CAP : (j + 1) * CAP, :] = block
    for expert in range(16):
        slot = lane + expert * CAP
        line = jnp.sum(
            jnp.where(slot == s0, g0, 0.0) + jnp.where(slot == s1, g1, 0.0), 0, keepdims=True
        )
        sent_ref[expert, 6 * CAP : LINE, :] = tail_of(line)
    finish(away)


def forward(lens, nat, mask, tokens, sid, sidt, pieces):
    vmem = pl.BlockSpec(memory_space=pltpu.VMEM)
    anywhere = pl.BlockSpec(memory_space=pl.ANY)
    moved = [
        like(D, FF),
        like(ROW, D),
        like(ROW, 3 * D),
        like(12, ROW, ROW),
        like(ROW, D),
        like(ROW, D, dtype=F32),
        like(ROW, D),
    ]
    held = [like(ROW, 128, dtype=F32), like(8, D, dtype=F32), like(D, 128), like(16, LINE, 128)]
    buffers = [like(D, FF), like(D, 128), *moved[1:4], like(ROW, D), *moved[4:]]
    return pl.pallas_call(
        forward_body,
        in_specs=[pl.BlockSpec(memory_space=pltpu.SMEM)] + [vmem] * 5 + [anywhere] * 8,
        out_specs=[anywhere] * 7 + [vmem] * 4,
        out_shape=moved + held,
        scratch_shapes=[pltpu.VMEM(b.shape, b.dtype) for b in buffers]
        + [pltpu.VMEM((ROW, ROW), F32), pltpu.SemaphoreType.DMA((16,))],
        compiler_params=pltpu.CompilerParams(vmem_limit_bytes=62 * MIB),
        cost_estimate=SMALL,
    )(lens, nat, mask, tokens, sid, sidt, *pieces)


def expert_body(
    place_ref, sent_ref, g_ref, near_in, far_in, out_ref, back_ref, x_ref, dout_ref, act_ref,
    dup_ref, up_ref, down_ref, sems,
):
    def loads():
        for source, y in ((near_in, place_ref[1]), (far_in, 1 - place_ref[1])):
            for x in range(4):
                block = 2 * x + y
                for j in range(4):
                    rows, cols = pl.ds(block * 96, 96), pl.ds(j * D, D)
                    yield source.at[pl.ds(x * D + j * 96, 96), :], up_ref.at[rows, cols]
                rows = pl.ds(block * 384, 384)
                yield source.at[pl.ds(x * D + 384, 384), :], down_ref.at[rows, :]

    @pl.when(pl.program_id(0) == 0)
    def _():
        copies = [
            pltpu.make_async_copy(source, target, sems.at[i])
            for i, (source, target) in enumerate(loads())
        ]
        for copy in copies:
            copy.start()
        for copy in copies:
            copy.wait()

    for s in range(SOURCES):
        first, last = s * CAP, (s + 1) * CAP
        for j in range(6):
            x_ref[first:last, j * 128 : (j + 1) * 128] = sent_ref[s, j * CAP : (j + 1) * CAP, :]
        gate = line_of(sent_ref[s, 6 * CAP : LINE, :])
        column = jnp.transpose(jnp.broadcast_to(gate, (128, 128)))[:CAP, :1]
        dout_ref[first:last, :] = (g_ref[s].astype(F32) * column).astype(BF)
    x, d_out = x_ref[...], dout_ref[...]
    for part in range(FF // 256):
        cols = slice(part * 256, (part + 1) * 256)
        up = nn(x, up_ref[:, cols])
        d_act = nt(d_out, down_ref[cols, :])
        square = up * up
        t = jnp.tanh(up * (GELU_ONE + GELU_CUBE * square))
        a = 0.5 + 0.5 * t
        act_ref[:, cols] = (up * a).astype(BF)
        slope = a + (up * (1.0 - t * t)) * (0.5 * GELU_ONE + 1.5 * GELU_CUBE * square)
        dup_ref[:, cols] = (d_act * slope).astype(BF)
    out = nn(act_ref[...], down_ref[...]).astype(BF)
    back = nt(dup_ref[...], up_ref[...]).astype(BF)
    for s in range(SOURCES):
        out_ref[s] = out[s * CAP : (s + 1) * CAP]
        for j in range(6):
            block = back[s * CAP : (s + 1) * CAP, j * 128 : (j + 1) * 128]
            back_ref[s, j * CAP : (j + 1) * CAP, :] = block
    for s in range(SOURCES):
        d_gate = jnp.sum(out_ref[s].astype(F32) * g_ref[s].astype(F32), -1, keepdims=True)
        d_gate = jnp.broadcast_to(d_gate, (CAP, 128))
        wide = jnp.concatenate([d_gate, jnp.zeros((128 - CAP, 128), F32)], 0)
        back_ref[s, 6 * CAP : LINE, :] = tail_of(jnp.transpose(wide)[0:1])


def experts(place, sent, g, near, far):
    rows = SOURCES * CAP
    anywhere = pl.BlockSpec(memory_space=pl.ANY)
    by_source = pl.BlockSpec((SOURCES, CAP, D), lambda i: (i, 0, 0))
    message = pl.BlockSpec((SOURCES, LINE, 128), lambda i: (i, 0, 0))
    by_rows = lambda width: pl.BlockSpec((rows, width), lambda i: (i, 0))
    return pl.pallas_call(
        expert_body,
        grid=(16 // SOURCES,),
        in_specs=[
            pl.BlockSpec(memory_space=pltpu.SMEM),
            message,
            by_source,
        ]
        + [anywhere] * 2,
        out_specs=[
            by_source, message, by_rows(D), by_rows(D), by_rows(FF), by_rows(FF),
        ],
        out_shape=[
            like(16, CAP, D),
            like(16, LINE, 128),
            like(16 * CAP, D),
            like(16 * CAP, D),
            like(16 * CAP, FF),
            like(16 * CAP, FF),
        ],
        scratch_shapes=[
            pltpu.VMEM((D, FF), BF),
            pltpu.VMEM((FF, D), BF),
            pltpu.SemaphoreType.DMA((40,)),
        ],
        compiler_params=pltpu.CompilerParams(vmem_limit_bytes=62 * MIB),
        cost_estimate=SMALL,
    )(place, sent, g, near, far)


def up_grad_body(x_ref, dup_ref, keep_ref, first_ref, last_ref):
    grad = tn(x_ref[...], dup_ref[...]).astype(BF)
    for block in range(8):
        rows, low = block * 96, (block % 4) * 48
        keep_ref[block * 48 : (block + 1) * 48, :] = grad[rows : rows + 48]
        away_ref = (first_ref, last_ref)[block // 4]
        away_ref[low : low + 48, :] = grad[rows + 48 : rows + 96]


def up_grad(x, d_up):
    columns = lambda rows: pl.BlockSpec((rows, D), lambda i: (0, i))
    return pl.pallas_call(
        up_grad_body,
        grid=(4,),
        in_specs=[pl.BlockSpec((16 * CAP, D), lambda i: (0, 0)), columns(16 * CAP)],
        out_specs=[columns(384), columns(192), columns(192)],
        out_shape=[like(384, FF), like(192, FF), like(192, FF)],
        compiler_params=pltpu.CompilerParams(vmem_limit_bytes=60 * MIB),
        cost_estimate=SMALL,
    )(x, d_up)


def down_grad_body(dout_ref, act_ref, keep_ref, first_ref, last_ref):
    grad = tn(act_ref[...], dout_ref[...]).astype(BF)
    for block in range(2):
        keep_ref[block * 192 : (block + 1) * 192, :] = grad[block * 384 : block * 384 + 192]
    away = jnp.concatenate([grad[192:384], grad[576:768]], 0)
    for part, away_ref in enumerate((first_ref, last_ref)):

        @pl.when(pl.program_id(0) // 2 == part)
        def _():
            away_ref[...] = away


def down_grad(d_out, act):
    rows = lambda index: pl.BlockSpec((384, D), index)
    return pl.pallas_call(
        down_grad_body,
        grid=(4,),
        in_specs=[
            pl.BlockSpec((16 * CAP, D), lambda i: (0, 0)),
            pl.BlockSpec((16 * CAP, D), lambda i: (0, i)),
        ],
        out_specs=[
            rows(lambda i: (i, 0)),
            rows(lambda i: (jnp.minimum(i, 1), 0)),
            rows(lambda i: (jnp.maximum(i - 2, 0), 0)),
        ],
        out_shape=[like(1536, D), like(768, D), like(768, D)],
        compiler_params=pltpu.CompilerParams(vmem_limit_bytes=60 * MIB),
        cost_estimate=SMALL,
    )(d_out, act)


def put_rows(keep_ref, away_ref, cols, values):
    for step in range(4):
        rows = slice(step * 96, (step + 1) * 96)
        keep_ref[rows, cols] = values[step * 192 : step * 192 + 96]
        away_ref[rows, cols] = values[step * 192 + 96 : (step + 1) * 192]


def attention_back(base, pairs, dattn_ref, probs_ref, qkv_ref, d_qkv):
    width = 128 * pairs
    low = iota((1, 128), 1) < 64
    zero = jnp.zeros((), BF)
    half = ROW // 2

    def add(terms, at, term):
        terms[at] = term if terms[at] is None else terms[at] + term

    def pair(index, carry):
        at = pl.multiple_of((base + index) * 128, 128)
        to = pl.multiple_of(index * 128, 128)
        q, k, v = (qkv_ref[:, pl.ds(part * D + at, 128)] for part in range(3))
        d_attn = dattn_ref[:, pl.ds(at, 128)]
        dq, dk, dv = [None, None], [None, None], [None, None]
        for head in range(2):
            mine = low if head == 0 else jnp.logical_not(low)
            q_mine, k_mine, v_mine, d_mine = (jnp.where(mine, t, zero) for t in (q, k, v, d_attn))
            for block in range(2):
                count, rows = half * (block + 1), slice(block * half, (block + 1) * half)
                probs = probs_ref[2 * index + head, rows, :count]
                d_probs = nt(d_mine[rows], v_mine[:count])
                wide = probs.astype(F32)
                weighted = wide * d_probs
                delta = jnp.sum(weighted, 1, keepdims=True)
                d_scores = (weighted - wide * delta).astype(BF)
                add(dq, block, nn(d_scores, k_mine[:count]))
                for other in range(block + 1):
                    keys = slice(other * half, (other + 1) * half)
                    add(dk, other, tn(d_scores[:, keys], q_mine[rows]))
                    add(dv, other, tn(probs[:, keys], d_mine[rows]))
        for block in range(2):
            rows = slice(block * half, (block + 1) * half)
            d_qkv[rows, pl.ds(to, 128)] = (dq[block] * 0.125).astype(BF)
            d_qkv[rows, pl.ds(width + to, 128)] = (dk[block] * 0.125).astype(BF)
            d_qkv[rows, pl.ds(2 * width + to, 128)] = dv[block].astype(BF)
        return carry

    lax.fori_loop(0, pairs, pair, 0)


def back_one_body(
    nat_ref, sid_ref, gate_ref, router_ref, vec_ref, dback_in, xmid_in, cot_in, w_in, attnp_in,
    h2_in, probs_in, qkv_in, h1p_in, dxm_out, dattn_out, dqkv_out, keep_out, away_out,
    dback_ref, xmid_ref, cot_ref, w_ref, attnp_ref, h2_ref, probs_ref, qkv_ref, h1p_ref, dxm_ref,
    dattn_ref, dqkv_ref, keep_ref, away_ref, slots_ref, sems,
):
    sources = (
        dback_in, xmid_in, cot_in, w_in.at[:, 3 * D :], attnp_in, h2_in, qkv_in, probs_in.at[:8], h1p_in,
    )
    targets = (dback_ref, xmid_ref, cot_ref, w_ref, attnp_ref, h2_ref, qkv_ref, probs_ref, h1p_ref)
    pairs = list(zip(sources, targets))
    loads = begin(sems, 0, *pairs[:1])
    turn = hot(iota((D, D), 0) == nat_ref[...])
    lane = iota((ROW, 128), 1)
    s0, s1, r0, r1 = (sid_ref[:, at : at + 1] for at in range(4))
    finish(loads)
    loads += begin(sems, 1, *pairs[1:])
    a0 = a1 = jnp.zeros((ROW, 128), F32)
    for expert in range(16):
        line = line_of(dback_ref[expert, 6 * CAP : LINE, :])
        slot = jnp.where(lane < CAP, lane + expert * CAP, -2)
        a0 = a0 + jnp.where(slot == s0, line, 0.0)
        a1 = a1 + jnp.where(slot == s1, line, 0.0)
    dg0, dg1 = jnp.sum(a0, 1, keepdims=True), jnp.sum(a1, 1, keepdims=True)
    g0, g1 = gate_ref[:, 0:1], gate_ref[:, 1:2]
    both = g0 * dg0 + g1 * dg1
    d_logits = jnp.where(lane == r0, g0 * (dg0 - both), 0.0)
    d_logits = d_logits + jnp.where(lane == r1, g1 * (dg1 - both), 0.0)
    high = d_logits.astype(BF)
    low = (d_logits - high.astype(F32)).astype(BF)
    d_h2 = nt(high, router_ref[...]) + nt(low, router_ref[...])
    for part in range(4):
        for i in range(4):
            for j in range(6):
                block = dback_ref[4 * part + i, j * CAP : (j + 1) * CAP, :]
                slots_ref[i * CAP : (i + 1) * CAP, j * 128 : (j + 1) * 128] = block
        slot = iota((ROW, 4 * CAP), 1) + part * 4 * CAP
        pick = hot((slot == s0) | (slot == s1))
        d_h2 = d_h2 + nn(pick, slots_ref[...])
    finish(loads[1:3])
    x_hat, scale = norm(xmid_ref[...])
    d_in, d_gain, d_bias = norm_back(d_h2, x_hat, scale, vec_ref[1:2])
    d_x_mid = cot_ref[...].astype(F32) + d_in
    dxm_ref[...] = d_x_mid
    d_proj = d_x_mid.astype(BF)
    finish(loads[3:6])
    dattn_ref[...] = nt(nt(d_proj, w_ref[...]).astype(BF), turn).astype(BF)
    leaving = begin(sems, 9, (dxm_ref, dxm_out), (dattn_ref, dattn_out))
    put_rows(keep_ref, away_ref, slice(0, D), tn(attnp_ref[...], d_proj).astype(BF))
    d_router = tn(h2_ref[...], high) + tn(h2_ref[...], low)
    sub = iota((128, D), 0)
    rows = jnp.where(sub == 17, d_gain, 0.0) + jnp.where(sub == 19, d_bias, 0.0)
    small = d_router + jnp.transpose(rows)
    put_rows(keep_ref, away_ref, slice(D, D + 128), tn(turn, small.astype(BF)).astype(BF))
    cols = slice(0, D + 128)
    leaving += begin(
        sems, 11, (keep_ref.at[:, cols], keep_out.at[:, cols]), (away_ref.at[:, cols], away_out.at[:, cols])
    )
    finish(loads[6:8])
    attention_back(0, 4, dattn_ref, probs_ref, qkv_ref, dqkv_ref)
    leaving += begin(sems, 13, (dqkv_ref, dqkv_out))
    finish(loads[8:])
    for part in range(3):
        cols = slice(D + 128 + part * 512, D + 128 + (part + 1) * 512)
        grad = tn(h1p_ref[...], dqkv_ref[:, part * 512 : (part + 1) * 512]).astype(BF)
        put_rows(keep_ref, away_ref, cols, grad)
        leaving += begin(
            sems,
            14 + 2 * part,
            (keep_ref.at[:, cols], keep_out.at[:, cols]),
            (away_ref.at[:, cols], away_out.at[:, cols]),
        )
    finish(leaving)


def back_one(nat, sid, gate, router, vec, d_back, x_mid, cotangent, w, attnp, h2, probs, qkv, h1p):
    vmem = pl.BlockSpec(memory_space=pltpu.VMEM)
    anywhere = pl.BlockSpec(memory_space=pl.ANY)
    ins = [
        like(16, LINE, 128), like(ROW, D, dtype=F32), like(ROW, D), like(D, D), like(ROW, D),
        like(ROW, D), like(8, ROW, ROW), like(ROW, 3 * D), like(ROW, D),
    ]
    outs = [
        like(ROW, D, dtype=F32), like(ROW, D), like(ROW, 1536), like(384, 2432), like(384, 2432),
    ]
    return pl.pallas_call(
        back_one_body,
        in_specs=[vmem] * 5 + [anywhere] * 9,
        out_specs=[anywhere] * 5,
        out_shape=outs,
        scratch_shapes=[pltpu.VMEM(b.shape, b.dtype) for b in ins + outs]
        + [pltpu.VMEM((4 * CAP, D), BF), pltpu.SemaphoreType.DMA((20,))],
        compiler_params=pltpu.CompilerParams(vmem_limit_bytes=62 * MIB),
        cost_estimate=SMALL,
    )(nat, sid, gate, router, vec, d_back, x_mid, cotangent, w, attnp, h2, probs, qkv, h1p)


def back_two_body(
    nat_ref, vec_ref, dattn_in, probs_in, qkv_in, h1p_in, first_in, w_in, tok_in, dxm_in,
    gx_out, keep_out, away_out, dattn_ref, probs_ref, qkv_ref, h1p_ref, first_ref, w_ref, tok_ref,
    dxm_ref, gx_ref, keep_ref, away_ref, second_ref, sems,
):
    sources = (
        dattn_in, qkv_in, probs_in.at[8:], h1p_in, first_in, w_in.at[:, : 3 * D], tok_in, dxm_in,
    )
    targets = (dattn_ref, qkv_ref, probs_ref, h1p_ref, first_ref, w_ref, tok_ref, dxm_ref)
    pairs = list(zip(sources, targets))
    loads = begin(sems, 0, *pairs[:3])
    turn = hot(iota((D, D), 0) == nat_ref[...])
    finish(loads)
    loads += begin(sems, 3, *pairs[3:])
    attention_back(4, 2, dattn_ref, probs_ref, qkv_ref, second_ref)
    finish(loads[3:6])
    d_h1p = jnp.zeros((ROW, D), F32)
    for part in range(3):
        middle = part * D + 512
        d_second = second_ref[:, part * 256 : (part + 1) * 256]
        grad = tn(h1p_ref[...], d_second).astype(BF)
        put_rows(keep_ref, away_ref, slice(part * 256, (part + 1) * 256), grad)
        d_h1p = d_h1p + nt(first_ref[:, part * 512 : (part + 1) * 512], w_ref[:, part * D : middle])
        d_h1p = d_h1p + nt(d_second, w_ref[:, middle : (part + 1) * D])
    cols = slice(0, D)
    leaving = begin(
        sems, 8, (keep_ref.at[:, cols], keep_out.at[:, cols]), (away_ref.at[:, cols], away_out.at[:, cols])
    )
    finish(loads[6:])
    d_h1 = nt(d_h1p.astype(BF), turn)
    x_hat, scale = norm(tok_ref[...].astype(F32))
    d_in, d_gain, d_bias = norm_back(d_h1, x_hat, scale, vec_ref[0:1])
    gx_ref[...] = dxm_ref[...] + d_in
    leaving += begin(sems, 10, (gx_ref, gx_out))
    sub = iota((128, D), 0)
    rows = jnp.where(sub == 16, d_gain, 0.0) + jnp.where(sub == 18, d_bias, 0.0)
    small = tn(turn, jnp.transpose(rows).astype(BF)).astype(BF)
    cols = slice(D, D + 128)
    put_rows(keep_ref, away_ref, cols, small)
    leaving += begin(
        sems, 11, (keep_ref.at[:, cols], keep_out.at[:, cols]), (away_ref.at[:, cols], away_out.at[:, cols])
    )
    finish(leaving)


def back_two(nat, vec, d_attn, probs, qkv, h1p, first, w, tokens, d_x_mid):
    vmem = pl.BlockSpec(memory_space=pltpu.VMEM)
    anywhere = pl.BlockSpec(memory_space=pl.ANY)
    ins = [
        like(ROW, D), like(4, ROW, ROW), like(ROW, 3 * D), like(ROW, D), like(ROW, 1536),
        like(D, 3 * D), like(ROW, D), like(ROW, D, dtype=F32),
    ]
    outs = [like(ROW, D, dtype=F32), like(384, 896), like(384, 896)]
    return pl.pallas_call(
        back_two_body,
        in_specs=[vmem] * 2 + [anywhere] * 8,
        out_specs=[anywhere] * 3,
        out_shape=outs,
        scratch_shapes=[pltpu.VMEM(b.shape, b.dtype) for b in ins + outs]
        + [pltpu.VMEM((ROW, D), BF), pltpu.SemaphoreType.DMA((13,))],
        compiler_params=pltpu.CompilerParams(vmem_limit_bytes=62 * MIB),
        cost_estimate=SMALL,
    )(nat, vec, d_attn, probs, qkv, h1p, first, w, tokens, d_x_mid)


def merge_body(sid_ref, ret_ref, gate_ref, xmid_ref, out_ref):
    s0, s1 = sid_ref[:, 0:1], sid_ref[:, 1:2]
    y0 = y1 = jnp.zeros((ROW, D), F32)
    for part in range(4):
        slot = iota((ROW, 4 * CAP), 1) + part * 4 * CAP
        values = ret_ref[part * 4 * CAP : (part + 1) * 4 * CAP, :]
        y0 = y0 + nn(hot(slot == s0), values)
        y1 = y1 + nn(hot(slot == s1), values)
    out_ref[...] = (xmid_ref[...] + (gate_ref[:, 0:1] * y0 + gate_ref[:, 1:2] * y1)).astype(BF)


def merge(sid, returned, gate, x_mid):
    return pl.pallas_call(
        merge_body,
        out_shape=like(ROW, D),
        compiler_params=pltpu.CompilerParams(vmem_limit_bytes=40 * MIB),
        cost_estimate=SMALL,
    )(sid, returned, gate, x_mid)


def to_blocks_body(place_ref, *refs):
    count = (len(refs) - 3) // 2
    held = refs[count + 1 : 2 * count + 1]
    out_ref, total, sems = refs[count], refs[-2], refs[-1]
    sources = [ref.at[pl.ds(0, 96), :] for ref in refs[:count]]
    loads = begin(sems, 0, *zip(sources, held))
    col = 0
    total[96:104, :] = jnp.zeros((8, total.shape[1]), F32)
    for group in range(count // 5):
        mine = slice(5 * group, 5 * group + 5)
        finish(loads[mine])
        value = held[5 * group][...].astype(F32)
        for part in held[mine][1:]:
            value = value + part[...].astype(F32)
        total[0:96, col : col + value.shape[1]] = value
        col += value.shape[1]
    x, y = place_ref[0], 2 * place_ref[1] + place_ref[2]
    for k in range(16):
        to = lax.rem(x - k % 4 + 4, 4) * 4 + lax.rem(y - k // 4 + 4, 4)
        out_ref[to] = total[6 * k : 6 * k + 8, :].astype(BF)


def to_blocks(place, parts):
    width = sum(part.shape[1] for part in parts[::5])
    return pl.pallas_call(
        to_blocks_body,
        in_specs=[pl.BlockSpec(memory_space=pltpu.SMEM)]
        + [pl.BlockSpec(memory_space=pl.ANY)] * len(parts),
        out_shape=like(16, 8, width),
        scratch_shapes=[pltpu.VMEM((96, part.shape[1]), BF) for part in parts]
        + [pltpu.VMEM((104, width), F32), pltpu.SemaphoreType.DMA((len(parts),))],
        compiler_params=pltpu.CompilerParams(vmem_limit_bytes=60 * MIB),
        cost_estimate=SMALL,
    )(place, *parts)


def from_blocks_body(in_ref, qkv_ref, out_ref, small_ref):
    total = in_ref[0].astype(F32)
    for k in range(1, 16):
        total = total + in_ref[k].astype(F32)
    out_ref[...] = total[:6, :D]
    for part in range(3):
        qkv_ref[:, part * D : part * D + 512] = total[:6, 896 + part * 512 : 1408 + part * 512]
        qkv_ref[:, part * D + 512 : (part + 1) * D] = total[:6, 2432 + part * 256 : 2688 + part * 256]
    small_ref[...] = total[:6, D : D + 128] + total[:6, 3200:3328]


def from_blocks(blocks):
    return pl.pallas_call(
        from_blocks_body,
        out_shape=[like(6, 3 * D, dtype=F32), like(6, D, dtype=F32), like(6, 128, dtype=F32)],
        compiler_params=pltpu.CompilerParams(vmem_limit_bytes=16 * MIB),
        cost_estimate=SMALL,
    )(blocks)


def prepare_body(core_ref, *refs):
    sources, (block_ref, mine_ref, other_ref) = refs[:9], refs[9:12]
    held, turned, sems = refs[12:21], refs[21], refs[22]
    loads = begin(sems, 0, *zip(sources, held))
    qkv_ref, out_ref, router_ref, gains_ref, biases_ref, up_t, down_t, up_f, down_f = held
    finish(loads[:5])
    block_ref[...] = jnp.zeros(block_ref.shape, BF)
    block_ref[0:6, : 3 * D] = qkv_ref[...].astype(BF)
    block_ref[0:6, 3 * D : FF] = out_ref[...].astype(BF)
    turned[...] = jnp.zeros((128, 128), F32)
    turned[16:18, 0:6] = gains_ref[...]
    turned[18:20, 0:6] = biases_ref[...]
    vectors = jnp.transpose(turned[...])[0:8]
    turned[0:6, 0:16] = router_ref[...]
    keep = iota((8, 128), 1) < 16
    small = jnp.where(keep, turned[0:8, :], vectors)
    small = jnp.where(iota((8, 128), 0) < 6, small, 0.0)
    block_ref[:, FF:] = small.astype(BF)
    trained = core_ref[0] == 0
    finish(loads[5:])
    for j in range(4):
        cols, rows = slice(j * D, (j + 1) * D), slice(j * 48, (j + 1) * 48)
        low, fixed = up_t[0, :, cols].astype(BF), up_f[0, :, cols]
        mine_ref[rows, :] = jnp.where(trained, low, fixed)
        other_ref[rows, :] = jnp.where(trained, fixed, low)
    low = down_t[0].astype(BF)
    mine_ref[192:, :] = jnp.where(trained, low, down_f[0])
    other_ref[192:, :] = jnp.where(trained, down_f[0], low)


def prepare(core, *arrays):
    anywhere = pl.BlockSpec(memory_space=pl.ANY)
    return pl.pallas_call(
        prepare_body,
        in_specs=[pl.BlockSpec(memory_space=pltpu.SMEM)] + [anywhere] * 9,
        out_shape=[like(8, FF + 128), like(384, D), like(384, D)],
        scratch_shapes=[pltpu.VMEM(array.shape, array.dtype) for array in arrays]
        + [pltpu.VMEM((128, 128), F32), pltpu.SemaphoreType.DMA((9,))],
        compiler_params=pltpu.CompilerParams(vmem_limit_bytes=60 * MIB),
        cost_estimate=SMALL,
    )(core, *arrays)


def pack_body(core_ref, mine_in, got_in, to_ref, sems):
    pairs = []
    for source, core in ((mine_in, core_ref[0]), (got_in, 1 - core_ref[0])):
        for j in range(4):
            rows = pl.ds(j * 96 + core * 48, 48)
            pairs.append((source.at[pl.ds(j * 48, 48), :], to_ref.at[rows, :]))
        pairs.append((source.at[pl.ds(192, 192), :], to_ref.at[pl.ds(384 + core * 192, 192), :]))
    finish(begin(sems, 0, *pairs))


def pack(core, mine, got):
    anywhere = pl.BlockSpec(memory_space=pl.ANY)
    return pl.pallas_call(
        pack_body,
        in_specs=[pl.BlockSpec(memory_space=pltpu.SMEM)] + [anywhere] * 2,
        out_shape=like(D, D),
        scratch_shapes=[pltpu.SemaphoreType.DMA((10,))],
        compiler_params=pltpu.CompilerParams(vmem_limit_bytes=16 * MIB),
        cost_estimate=SMALL,
    )(core, mine, got)


def shift(value, axis, by):
    count = lax.axis_size(axis)
    return lax.ppermute(value, axis, [(i, (i + by) % count) for i in range(count)])


def ordered(mine, other, index):
    first = jnp.where(index == 0, mine, other)
    second = jnp.where(index == 0, other, mine)
    return first, second


FAR = ("x", "yh", "yl")
PEERS = ("c", "z", "yl")


def to_all(rows, names):
    return lax.all_to_all(rows, names, split_axis=0, concat_axis=0, tiled=True)


def spread_x(block):
    return jnp.stack([block] + [shift(block, "x", step) for step in (1, 2, 3)])


def spread_y(along_x):
    near = [along_x] + [shift(along_x, ("yh", "yl"), step) for step in (1, 2, 3)]
    return jnp.stack(near)[:, :, :6].reshape(96, along_x.shape[2])


def natural_rows():
    x, c, z = (lax.axis_index(name) for name in ("x", "c", "z"))
    y = lax.axis_index("yh") * 2 + lax.axis_index("yl")
    row = jnp.arange(768)
    step, other, i = row // 192, (row // 96) % 2, row % 96
    core, deep = (c + other) % 2, (z - step) % 4
    high, long = (y - i // 24) % 4, (x - (i // 6) % 4) % 4
    device = ((long * 2 + high // 2) * 2 + core) * 8 + deep * 2 + high % 2
    return (device * 6 + i % 6).astype(jnp.int32)


def along_z(keep, got):
    parts = [keep, got]
    for step in (1, 2, 3):
        rows = slice(step * 96, (step + 1) * 96)
        both = keep[rows].astype(F32) + got[rows].astype(F32)
        parts.append(shift(both.astype(BF), "z", -step))
    return parts


def take_body(core_ref, *refs):
    sources, (to_ref, *held), sems = refs[1:3], refs[3:6], refs[6]
    rows = held[0].shape[0]

    @pl.when(core_ref[0] == 1)
    def _():
        targets = [to_ref.at[pl.ds(at, rows), :] for at in (0, rows)]
        loads, stores = begin(sems, 0, *zip(sources, held)), []
        for i in range(2):
            finish(loads[i : i + 1])
            stores += begin(sems, 2 + i, (held[i], targets[i]))
        finish(stores)


def take(core, kept, *sent):
    got = [lax.ppermute(part, "c", [(0, 1)]) for part in sent]
    anywhere = pl.BlockSpec(memory_space=pl.ANY)
    return pl.pallas_call(
        take_body,
        in_specs=[pl.BlockSpec(memory_space=pltpu.SMEM)] + [anywhere] * 3,
        out_specs=anywhere,
        out_shape=like(*kept.shape),
        input_output_aliases={1: 0},
        scratch_shapes=[pltpu.VMEM(part.shape, part.dtype) for part in got]
        + [pltpu.SemaphoreType.DMA((4,))],
        compiler_params=pltpu.CompilerParams(vmem_limit_bytes=62 * MIB),
        cost_estimate=SMALL,
    )(core, kept, *got)


def over_y(mine):
    y = lax.axis_index("yh")
    parts = mine.reshape(2, mine.shape[0] // 2, mine.shape[1])
    kept, sent = (lax.dynamic_index_in_dim(parts, at, 0, False) for at in (y, 1 - y))
    return kept.astype(F32) + shift(sent, "yh", 1).astype(F32)


def owned(mine, axis):
    return lax.psum_scatter(mine, axis, scatter_dimension=0, tiled=True)


def shards(
    tokens,
    seq_lengths,
    key_mask,
    routes,
    cotangent,
    qkv_weight,
    out_weight,
    router_weight,
    norm_gains,
    norm_biases,
    up_train,
    down_train,
    up_frozen,
    down_frozen,
):
    core = lax.axis_index("c")

    place = jnp.stack([lax.axis_index(name) for name in ("x", "yh", "yl")]).astype(jnp.int32)

    block, mine, other = prepare(
        core.reshape(1), qkv_weight, out_weight, router_weight, norm_gains, norm_biases, up_train,
        down_train, up_frozen, down_frozen,
    )
    other = shift(other, "c", 1)
    block, routes, other = lax.optimization_barrier((block, routes, other))
    along_x = spread_x(block)

    both = pack(core.reshape(1), mine, other)
    along_x, both = lax.optimization_barrier((along_x, both))
    rows = spread_y(along_x)
    nat = natural_rows().reshape(1, D)
    g_slots, sid, sidt = route(routes, cotangent)
    near = lax.all_gather(both, "x", tiled=True)

    rows, g_slots, both = lax.optimization_barrier((rows, g_slots, both))
    parts = [rows] + [shift(rows, "z", step) for step in (1, 2, 3)]
    both = shift(both, "yh", 1)
    parts, both, g_slots = lax.optimization_barrier((parts, both, g_slots))
    pieces = []
    for part in parts:
        pieces += [part, shift(part, "c", 1)]
    far = lax.all_gather(both, "x", tiled=True)

    g_rows = to_all(g_slots.reshape(16, CAP, D), PEERS)
    w, h1p, qkv, probs, attnp, x_mid, h2, gate, vec, router, sent = forward(
        seq_lengths[0], nat, key_mask.reshape(1, ROW), tokens, sid, sidt, pieces
    )
    sent, g_rows = lax.optimization_barrier((sent, g_rows))

    arrived = to_all(sent, PEERS)
    out, back, x_rows, d_out, act, d_up = experts(
        place, arrived, g_rows, near, far
    )
    d_back = to_all(back, PEERS)
    up_all = take(core.reshape(1), *up_grad(x_rows, d_up))
    down_parts = down_grad(d_out, act)
    d_back, out, up_all, down_parts = lax.optimization_barrier((d_back, out, up_all, down_parts))

    returned = to_all(out, PEERS)
    up_all, down_all = owned(up_all, "x"), take(core.reshape(1), *down_parts)
    d_x_mid, d_attn, first, keep, away = back_one(
        nat, sid, gate, router, vec, d_back, x_mid, cotangent, w, attnp, h2,
        probs, qkv, h1p,
    )
    input_grad, *last = back_two(nat, vec, d_attn, probs, qkv, h1p, first, w, tokens, d_x_mid)
    got = shift(away, "c", 1)
    keep, got, returned, down_all = lax.optimization_barrier((keep, got, returned, down_all))
    down_all = owned(down_all, "x")
    parts_one = along_z(keep, got)
    parts_one[2::2], last, up_all = lax.optimization_barrier((parts_one[2::2], last, up_all))
    up_all = over_y(up_all)
    parts_two = along_z(last[0], shift(last[1], "c", 1))
    parts_two, down_all = lax.optimization_barrier((parts_two, down_all))
    down_all = owned(down_all, "yh")
    blocks = to_blocks(place, parts_one + parts_two)
    blocks, returned = lax.optimization_barrier((blocks, returned))
    blocks, down_all = lax.optimization_barrier((to_all(blocks, FAR), down_all))
    own_qkv, own_out, small = from_blocks(blocks)
    grad_up, grad_down = up_all.astype(F32)[None], down_all.astype(F32)[None]
    block_out = merge(sid, returned.reshape(16 * CAP, D), gate, x_mid)
    return (
        block_out,
        input_grad,
        own_qkv,
        own_out,
        small[:, :16],
        small[:, 16:18].T,
        small[:, 18:20].T,
        grad_up,
        grad_down,
    )


def solution(mesh):
    fine = Mesh(mesh.devices.reshape(SIZES), NAMES)
    by_row = P(NAMES, None)
    by_column = P(None, NAMES)
    by_expert = P(NARROW, WIDE, None)
    return jax.shard_map(
        shards,
        mesh=fine,
        in_specs=(by_row, by_row, P(NAMES)) + (by_row,) * 5 + (by_column,) * 2 + (by_expert,) * 4,
        out_specs=(by_row,) * 5 + (by_column,) * 2 + (by_expert,) * 2,
        check_vma=False,
    )
```

```python
import functools

import jax
import jax.numpy as jnp
from jax import lax
from jax.experimental import pallas as pl
from jax.experimental.pallas import tpu as pltpu
from jax.sharding import Mesh
from jax.sharding import PartitionSpec as P

SIZES = (4, 2, 2, 4, 2)
NAMES = ("x", "yh", "c", "z", "yl")
WIDE = ("x", "yh", "c")
NARROW = ("z", "yl")
BF = jnp.bfloat16
F32 = jnp.float32
ROW = 512
D = 768
FF = 3072
CAP = 96
LINE = 592
SOURCES = 4
GELU_ONE = 0.7978845608028654
GELU_CUBE = GELU_ONE * 0.044715
MIB = 1024 * 1024
SMALL = pl.CostEstimate(flops=10**6, bytes_accessed=10**4, transcendentals=0)


def nn(a, b):
    return jnp.dot(a, b, preferred_element_type=F32)


def nt(a, b):
    return lax.dot_general(a, b, (((1,), (1,)), ((), ())), preferred_element_type=F32)


def tn(a, b):
    return lax.dot_general(a, b, (((0,), (0,)), ((), ())), preferred_element_type=F32)


def iota(shape, dim):
    return lax.broadcasted_iota(jnp.int32, shape, dim)


def hot(mask):
    return jnp.where(mask, 1.0, 0.0).astype(BF)


def like(*dims, dtype=BF):
    return jax.ShapeDtypeStruct(dims, dtype)


def tail_of(line):
    high = line.astype(BF).astype(F32)
    row = iota((16, 128), 0)
    return jnp.where(row == 0, high, jnp.where(row == 1, line - high, 0.0)).astype(BF)


def line_of(tail):
    tail = tail.astype(F32)
    return tail[0:1] + tail[1:2]


def begin(sems, first, *pairs):
    copies = [
        pltpu.make_async_copy(source, target, sems.at[first + i])
        for i, (source, target) in enumerate(pairs)
    ]
    for copy in copies:
        copy.start()
    return copies


def finish(copies):
    for copy in copies:
        copy.wait()


def norm(x):
    centered = x - jnp.mean(x, -1, keepdims=True)
    scale = lax.rsqrt(jnp.mean(centered * centered, -1, keepdims=True) + 1e-5)
    return centered * scale, scale


def norm_back(d_out, x_hat, scale, gain):
    t = d_out * gain
    d_in = scale * (
        t - jnp.mean(t, -1, keepdims=True) - x_hat * jnp.mean(t * x_hat, -1, keepdims=True)
    )
    return d_in, jnp.sum(d_out * x_hat, 0, keepdims=True), jnp.sum(d_out, 0, keepdims=True)


def route_body(routes_ref, cot_ref, g_ref, sid_ref, sidt_ref):
    lane = iota((ROW, 128), 1)
    r0, r1 = routes_ref[:, 0:1], routes_ref[:, 1:2]
    either = hot((lane == r0) | (lane == r1))
    earlier = nn(hot(iota((ROW, ROW), 1) < iota((ROW, ROW), 0)), either)
    p0 = jnp.sum(jnp.where(lane == r0, earlier, 0.0), 1, keepdims=True).astype(jnp.int32)
    p1 = jnp.sum(jnp.where(lane == r1, earlier, 0.0), 1, keepdims=True).astype(jnp.int32)
    columns = (
        jnp.where(p0 < CAP, r0 * CAP + p0, -1),
        jnp.where(p1 < CAP, r1 * CAP + p1, -1),
        r0,
    )
    table = jnp.broadcast_to(r1, (ROW, 128))
    for at, column in enumerate(columns):
        table = jnp.where(lane == at, column, table)
    sid_ref[...] = table
    turned = jnp.transpose(table.astype(F32))[0:8].astype(jnp.int32)
    sidt_ref[...] = turned
    for part in range(4):
        slot = iota((4 * CAP, ROW), 0) + part * 4 * CAP
        pick = hot((slot == turned[0:1]) | (slot == turned[1:2]))
        g_ref[part * 4 * CAP : (part + 1) * 4 * CAP, :] = nn(pick, cot_ref[...]).astype(BF)


def route(routes, cotangent):
    return pl.pallas_call(
        route_body,
        out_shape=[like(16 * CAP, D), like(ROW, 128, dtype=jnp.int32), like(8, ROW, dtype=jnp.int32)],
        compiler_params=pltpu.CompilerParams(vmem_limit_bytes=32 * MIB),
        cost_estimate=SMALL,
    )(routes, cotangent)


def forward_body(*refs):
    lens_ref, nat_ref, mask_ref, tok_ref, sid_ref, sidt_ref = refs[:6]
    pieces, refs = refs[6:14], refs[14:]
    w_out, h1p_out, qkv_out, probs_out, attnp_out, xmid_out, h2_out = refs[:7]
    gate_ref, vec_ref, router_ref, sent_ref = refs[7:11]
    w_ref, rest_ref, h1p_ref, qkv_ref, probs_ref, attn, attnp_ref, xmid_ref, h2_ref, bias = refs[11:21]
    sems = refs[21]
    rows = [pl.ds(at * 96, 96) for at in range(8)]
    small = [(piece.at[:, FF:], rest_ref.at[to, :]) for piece, to in zip(pieces, rows)]
    large = [(piece.at[:, :FF], w_ref.at[to, :]) for piece, to in zip(pieces, rows)]
    small, large = begin(sems, 0, *small), begin(sems, 8, *large)
    turn = hot(iota((D, D), 0) == nat_ref[...])
    x = tok_ref[...].astype(F32)
    x_hat = norm(x)[0]
    finish(small)
    rest = nn(turn, rest_ref[...])
    vectors = jnp.transpose(rest)[16:24]
    router_ref[...] = rest.astype(BF)
    vec_ref[...] = vectors
    h1 = (x_hat * vectors[0:1] + vectors[2:3]).astype(BF)
    h1p_ref[...] = nn(h1, turn).astype(BF)
    finish(large)
    away = begin(sems, 0, (w_ref, w_out), (h1p_ref, h1p_out))
    for part in range(3):
        cols = slice(part * D, (part + 1) * D)
        qkv_ref[:, cols] = nn(h1p_ref[...], w_ref[:, cols]).astype(BF)
    away += begin(sems, 2, (qkv_ref, qkv_out))

    end_one = lens_ref[0]
    end_two = end_one + lens_ref[1]

    def segment(place):
        return (place >= end_one).astype(jnp.int32) + (place >= end_two).astype(jnp.int32)

    query, key = iota((ROW, ROW), 0), iota((ROW, ROW), 1)
    same = segment(iota((ROW, 1), 0)) == segment(iota((1, ROW), 1))
    allowed = same & (key <= query) & ((mask_ref[...] == 1) | (key == query))
    bias[...] = jnp.where(allowed, 0.0, -1e30)
    low = iota((1, 128), 1) < 64
    half = ROW // 2
    zero = jnp.zeros((), BF)

    def pair(index, carry):
        at = pl.multiple_of(index * 128, 128)
        q = qkv_ref[:, pl.ds(at, 128)] * jnp.asarray(0.125, BF)
        k = qkv_ref[:, pl.ds(D + at, 128)]
        v = qkv_ref[:, pl.ds(2 * D + at, 128)]
        out = [None, None]
        for head in range(2):
            mine = low if head == 0 else jnp.logical_not(low)
            k_mine, v_mine = jnp.where(mine, k, zero), jnp.where(mine, v, zero)
            for block in range(2):
                count, rows = half * (block + 1), slice(block * half, (block + 1) * half)
                scores = nt(q[rows], k_mine[:count]) + bias[rows, :count]
                e = jnp.exp(scores - jnp.max(scores, 1, keepdims=True))
                probs = (e * (1.0 / jnp.sum(e, 1, keepdims=True))).astype(BF)
                probs_ref[2 * index + head, rows, :count] = probs
                if block == 0:
                    probs_ref[2 * index + head, rows, count:] = jnp.zeros((half, half), BF)
                term = nn(probs, v_mine[:count])
                out[block] = term if head == 0 else out[block] + term
        for block in range(2):
            attn[block * half : (block + 1) * half, pl.ds(at, 128)] = out[block].astype(BF)
        heads = pl.ds(2 * index, 2)
        begin(sems, 8 + index, (probs_ref.at[heads], probs_out.at[heads]))
        return carry

    lax.fori_loop(0, 6, pair, 0)
    for index in range(6):
        heads = pl.ds(2 * index, 2)
        away.append(
            pltpu.make_async_copy(probs_ref.at[heads], probs_out.at[heads], sems.at[8 + index])
        )
    attnp_ref[...] = nn(attn[...], turn).astype(BF)
    x_mid = x + nn(attnp_ref[...], w_ref[:, 3 * D :])
    xmid_ref[...] = x_mid
    h2 = (norm(x_mid)[0] * vectors[1:2] + vectors[3:4]).astype(BF)
    h2_ref[...] = h2
    away += begin(sems, 3, (attnp_ref, attnp_out), (xmid_ref, xmid_out), (h2_ref, h2_out))
    logits = nn(h2, router_ref[...])
    lane = iota((ROW, 128), 1)
    s0, s1, r0, r1 = (sid_ref[:, at : at + 1] for at in range(4))
    c0 = jnp.sum(jnp.where(lane == r0, logits, 0.0), 1, keepdims=True)
    c1 = jnp.sum(jnp.where(lane == r1, logits, 0.0), 1, keepdims=True)
    g0, g1 = 1.0 / (1.0 + jnp.exp(c1 - c0)), 1.0 / (1.0 + jnp.exp(c0 - c1))
    gate_ref[...] = jnp.where(lane == 0, g0, jnp.where(lane == 1, g1, 0.0))
    for part in range(4):
        slot = iota((4 * CAP, ROW), 0) + part * 4 * CAP
        pick = hot((slot == sidt_ref[0:1]) | (slot == sidt_ref[1:2]))
        rows = nn(pick, h2_ref[...]).astype(BF)
        for i in range(4):
            for j in range(6):
                block = rows[i * CAP : (i + 1) * CAP, j * 128 : (j + 1) * 128]
                sent_ref[4 * part + i, j * CAP : (j + 1) * CAP, :] = block
    for expert in range(16):
        slot = lane + expert * CAP
        line = jnp.sum(
            jnp.where(slot == s0, g0, 0.0) + jnp.where(slot == s1, g1, 0.0), 0, keepdims=True
        )
        sent_ref[expert, 6 * CAP : LINE, :] = tail_of(line)
    finish(away)


def forward(lens, nat, mask, tokens, sid, sidt, pieces):
    vmem = pl.BlockSpec(memory_space=pltpu.VMEM)
    anywhere = pl.BlockSpec(memory_space=pl.ANY)
    moved = [
        like(D, FF),
        like(ROW, D),
        like(ROW, 3 * D),
        like(12, ROW, ROW),
        like(ROW, D),
        like(ROW, D, dtype=F32),
        like(ROW, D),
    ]
    held = [like(ROW, 128, dtype=F32), like(8, D, dtype=F32), like(D, 128), like(16, LINE, 128)]
    buffers = [like(D, FF), like(D, 128), *moved[1:4], like(ROW, D), *moved[4:]]
    return pl.pallas_call(
        forward_body,
        in_specs=[pl.BlockSpec(memory_space=pltpu.SMEM)] + [vmem] * 5 + [anywhere] * 8,
        out_specs=[anywhere] * 7 + [vmem] * 4,
        out_shape=moved + held,
        scratch_shapes=[pltpu.VMEM(b.shape, b.dtype) for b in buffers]
        + [pltpu.VMEM((ROW, ROW), F32), pltpu.SemaphoreType.DMA((16,))],
        compiler_params=pltpu.CompilerParams(vmem_limit_bytes=62 * MIB),
        cost_estimate=SMALL,
    )(lens, nat, mask, tokens, sid, sidt, *pieces)


def expert_body(
    place_ref, sent_ref, g_ref, near_in, far_in, out_ref, back_ref, x_ref, dout_ref, act_ref,
    dup_ref, up_ref, down_ref, sems,
):
    def loads():
        for source, y in ((near_in, place_ref[1]), (far_in, 1 - place_ref[1])):
            for x in range(4):
                block = 2 * x + y
                for j in range(4):
                    rows, cols = pl.ds(block * 96, 96), pl.ds(j * D, D)
                    yield source.at[pl.ds(x * D + j * 96, 96), :], up_ref.at[rows, cols]
                rows = pl.ds(block * 384, 384)
                yield source.at[pl.ds(x * D + 384, 384), :], down_ref.at[rows, :]

    @pl.when(pl.program_id(0) == 0)
    def _():
        copies = [
            pltpu.make_async_copy(source, target, sems.at[i])
            for i, (source, target) in enumerate(loads())
        ]
        for copy in copies:
            copy.start()
        for copy in copies:
            copy.wait()

    for s in range(SOURCES):
        first, last = s * CAP, (s + 1) * CAP
        for j in range(6):
            x_ref[first:last, j * 128 : (j + 1) * 128] = sent_ref[s, j * CAP : (j + 1) * CAP, :]
        gate = line_of(sent_ref[s, 6 * CAP : LINE, :])
        column = jnp.transpose(jnp.broadcast_to(gate, (128, 128)))[:CAP, :1]
        dout_ref[first:last, :] = (g_ref[s].astype(F32) * column).astype(BF)
    x, d_out = x_ref[...], dout_ref[...]
    for part in range(FF // 256):
        cols = slice(part * 256, (part + 1) * 256)
        up = nn(x, up_ref[:, cols])
        d_act = nt(d_out, down_ref[cols, :])
        square = up * up
        t = jnp.tanh(up * (GELU_ONE + GELU_CUBE * square))
        a = 0.5 + 0.5 * t
        act_ref[:, cols] = (up * a).astype(BF)
        slope = a + (up * (1.0 - t * t)) * (0.5 * GELU_ONE + 1.5 * GELU_CUBE * square)
        dup_ref[:, cols] = (d_act * slope).astype(BF)
    out = nn(act_ref[...], down_ref[...]).astype(BF)
    back = nt(dup_ref[...], up_ref[...]).astype(BF)
    for s in range(SOURCES):
        out_ref[s] = out[s * CAP : (s + 1) * CAP]
        for j in range(6):
            block = back[s * CAP : (s + 1) * CAP, j * 128 : (j + 1) * 128]
            back_ref[s, j * CAP : (j + 1) * CAP, :] = block
    for s in range(SOURCES):
        d_gate = jnp.sum(out_ref[s].astype(F32) * g_ref[s].astype(F32), -1, keepdims=True)
        d_gate = jnp.broadcast_to(d_gate, (CAP, 128))
        wide = jnp.concatenate([d_gate, jnp.zeros((128 - CAP, 128), F32)], 0)
        back_ref[s, 6 * CAP : LINE, :] = tail_of(jnp.transpose(wide)[0:1])


def experts(place, sent, g, near, far):
    rows = SOURCES * CAP
    anywhere = pl.BlockSpec(memory_space=pl.ANY)
    by_source = pl.BlockSpec((SOURCES, CAP, D), lambda i: (i, 0, 0))
    message = pl.BlockSpec((SOURCES, LINE, 128), lambda i: (i, 0, 0))
    by_rows = lambda width: pl.BlockSpec((rows, width), lambda i: (i, 0))
    return pl.pallas_call(
        expert_body,
        grid=(16 // SOURCES,),
        in_specs=[
            pl.BlockSpec(memory_space=pltpu.SMEM),
            message,
            by_source,
        ]
        + [anywhere] * 2,
        out_specs=[
            by_source, message, by_rows(D), by_rows(D), by_rows(FF), by_rows(FF),
        ],
        out_shape=[
            like(16, CAP, D),
            like(16, LINE, 128),
            like(16 * CAP, D),
            like(16 * CAP, D),
            like(16 * CAP, FF),
            like(16 * CAP, FF),
        ],
        scratch_shapes=[
            pltpu.VMEM((D, FF), BF),
            pltpu.VMEM((FF, D), BF),
            pltpu.SemaphoreType.DMA((40,)),
        ],
        compiler_params=pltpu.CompilerParams(vmem_limit_bytes=62 * MIB),
        cost_estimate=SMALL,
    )(place, sent, g, near, far)


def up_grad_body(x_ref, dup_ref, keep_ref, first_ref, last_ref):
    grad = tn(x_ref[...], dup_ref[...]).astype(BF)
    for block in range(8):
        rows, low = block * 96, (block % 4) * 48
        keep_ref[block * 48 : (block + 1) * 48, :] = grad[rows : rows + 48]
        away_ref = (first_ref, last_ref)[block // 4]
        away_ref[low : low + 48, :] = grad[rows + 48 : rows + 96]


def up_grad(x, d_up):
    columns = lambda rows: pl.BlockSpec((rows, D), lambda i: (0, i))
    return pl.pallas_call(
        up_grad_body,
        grid=(4,),
        in_specs=[pl.BlockSpec((16 * CAP, D), lambda i: (0, 0)), columns(16 * CAP)],
        out_specs=[columns(384), columns(192), columns(192)],
        out_shape=[like(384, FF), like(192, FF), like(192, FF)],
        compiler_params=pltpu.CompilerParams(vmem_limit_bytes=60 * MIB),
        cost_estimate=SMALL,
    )(x, d_up)


def down_grad_body(dout_ref, act_ref, keep_ref, first_ref, last_ref):
    grad = tn(act_ref[...], dout_ref[...]).astype(BF)
    for block in range(2):
        keep_ref[block * 192 : (block + 1) * 192, :] = grad[block * 384 : block * 384 + 192]
    away = jnp.concatenate([grad[192:384], grad[576:768]], 0)
    for part, away_ref in enumerate((first_ref, last_ref)):

        @pl.when(pl.program_id(0) // 2 == part)
        def _():
            away_ref[...] = away


def down_grad(d_out, act):
    rows = lambda index: pl.BlockSpec((384, D), index)
    return pl.pallas_call(
        down_grad_body,
        grid=(4,),
        in_specs=[
            pl.BlockSpec((16 * CAP, D), lambda i: (0, 0)),
            pl.BlockSpec((16 * CAP, D), lambda i: (0, i)),
        ],
        out_specs=[
            rows(lambda i: (i, 0)),
            rows(lambda i: (jnp.minimum(i, 1), 0)),
            rows(lambda i: (jnp.maximum(i - 2, 0), 0)),
        ],
        out_shape=[like(1536, D), like(768, D), like(768, D)],
        compiler_params=pltpu.CompilerParams(vmem_limit_bytes=60 * MIB),
        cost_estimate=SMALL,
    )(d_out, act)


def put_rows(keep_ref, away_ref, cols, values):
    for step in range(4):
        rows = slice(step * 96, (step + 1) * 96)
        keep_ref[rows, cols] = values[step * 192 : step * 192 + 96]
        away_ref[rows, cols] = values[step * 192 + 96 : (step + 1) * 192]


def attention_back(base, pairs, dattn_ref, probs_ref, qkv_ref, d_qkv):
    width = 128 * pairs
    low = iota((1, 128), 1) < 64
    zero = jnp.zeros((), BF)
    half = ROW // 2

    def add(terms, at, term):
        terms[at] = term if terms[at] is None else terms[at] + term

    def pair(index, carry):
        at = pl.multiple_of((base + index) * 128, 128)
        to = pl.multiple_of(index * 128, 128)
        q, k, v = (qkv_ref[:, pl.ds(part * D + at, 128)] for part in range(3))
        d_attn = dattn_ref[:, pl.ds(at, 128)]
        dq, dk, dv = [None, None], [None, None], [None, None]
        for head in range(2):
            mine = low if head == 0 else jnp.logical_not(low)
            q_mine, k_mine, v_mine, d_mine = (jnp.where(mine, t, zero) for t in (q, k, v, d_attn))
            for block in range(2):
                count, rows = half * (block + 1), slice(block * half, (block + 1) * half)
                probs = probs_ref[2 * index + head, rows, :count]
                d_probs = nt(d_mine[rows], v_mine[:count])
                wide = probs.astype(F32)
                weighted = wide * d_probs
                delta = jnp.sum(weighted, 1, keepdims=True)
                d_scores = (weighted - wide * delta).astype(BF)
                add(dq, block, nn(d_scores, k_mine[:count]))
                for other in range(block + 1):
                    keys = slice(other * half, (other + 1) * half)
                    add(dk, other, tn(d_scores[:, keys], q_mine[rows]))
                    add(dv, other, tn(probs[:, keys], d_mine[rows]))
        for block in range(2):
            rows = slice(block * half, (block + 1) * half)
            d_qkv[rows, pl.ds(to, 128)] = (dq[block] * 0.125).astype(BF)
            d_qkv[rows, pl.ds(width + to, 128)] = (dk[block] * 0.125).astype(BF)
            d_qkv[rows, pl.ds(2 * width + to, 128)] = dv[block].astype(BF)
        return carry

    lax.fori_loop(0, pairs, pair, 0)


def back_one_body(
    nat_ref, sid_ref, gate_ref, router_ref, vec_ref, dback_in, xmid_in, cot_in, w_in, attnp_in,
    h2_in, probs_in, qkv_in, h1p_in, dxm_out, dattn_out, dqkv_out, keep_out, away_out,
    dback_ref, xmid_ref, cot_ref, w_ref, attnp_ref, h2_ref, probs_ref, qkv_ref, h1p_ref, dxm_ref,
    dattn_ref, dqkv_ref, keep_ref, away_ref, slots_ref, columns_ref, sems,
):
    sources = (
        dback_in, xmid_in, cot_in, w_in.at[:, 3 * D :], attnp_in, h2_in, qkv_in, probs_in.at[:8], h1p_in,
    )
    targets = (dback_ref, xmid_ref, cot_ref, w_ref, attnp_ref, h2_ref, qkv_ref, probs_ref, h1p_ref)
    pairs = list(zip(sources, targets))
    loads = begin(sems, 0, *pairs[:1])
    turn = hot(iota((D, D), 0) == nat_ref[...])
    lane = iota((ROW, 128), 1)
    s0, s1, r0, r1 = (sid_ref[:, at : at + 1] for at in range(4))
    finish(loads)
    loads += begin(sems, 1, *pairs[1:])
    dg0 = dg1 = jnp.zeros((ROW, 128), F32)
    d_h2 = jnp.zeros((ROW, D), F32)
    columns_ref[...] = jnp.zeros((4 * CAP, 128), BF)
    for part in range(4):
        for i in range(4):
            message = dback_ref.at[4 * part + i]
            for j in range(6):
                block = message[j * CAP : (j + 1) * CAP, :]
                slots_ref[i * CAP : (i + 1) * CAP, j * 128 : (j + 1) * 128] = block
            terms = jnp.transpose(message[6 * CAP : LINE, :].astype(F32))
            columns_ref[i * CAP : (i + 1) * CAP, 0:16] = terms[:CAP].astype(BF)
        slot = iota((ROW, 4 * CAP), 1) + part * 4 * CAP
        first, second = hot(slot == s0), hot(slot == s1)
        dg0 = dg0 + nn(first, columns_ref[...])
        dg1 = dg1 + nn(second, columns_ref[...])
        d_h2 = d_h2 + nn(first + second, slots_ref[...])
    dg0, dg1 = dg0[:, 0:1] + dg0[:, 1:2], dg1[:, 0:1] + dg1[:, 1:2]
    g0, g1 = gate_ref[:, 0:1], gate_ref[:, 1:2]
    both = g0 * dg0 + g1 * dg1
    d_logits = jnp.where(lane == r0, g0 * (dg0 - both), 0.0)
    d_logits = d_logits + jnp.where(lane == r1, g1 * (dg1 - both), 0.0)
    high = d_logits.astype(BF)
    low = (d_logits - high.astype(F32)).astype(BF)
    d_h2 = d_h2 + nt(high, router_ref[...]) + nt(low, router_ref[...])
    finish(loads[1:3])
    x_hat, scale = norm(xmid_ref[...])
    d_in, d_gain, d_bias = norm_back(d_h2, x_hat, scale, vec_ref[1:2])
    d_x_mid = cot_ref[...].astype(F32) + d_in
    dxm_ref[...] = d_x_mid
    d_proj = d_x_mid.astype(BF)
    finish(loads[3:6])
    dattn_ref[...] = nt(nt(d_proj, w_ref[...]).astype(BF), turn).astype(BF)
    leaving = begin(sems, 9, (dxm_ref, dxm_out), (dattn_ref, dattn_out))
    put_rows(keep_ref, away_ref, slice(0, D), tn(attnp_ref[...], d_proj).astype(BF))
    d_router = tn(h2_ref[...], jnp.concatenate([high, low], 1))
    d_router = d_router[:, :128] + d_router[:, 128:]
    sub = iota((128, D), 0)
    rows = jnp.where(sub == 17, d_gain, 0.0) + jnp.where(sub == 19, d_bias, 0.0)
    small = d_router + jnp.transpose(rows)
    put_rows(keep_ref, away_ref, slice(D, D + 128), tn(turn, small.astype(BF)).astype(BF))
    cols = slice(0, D + 128)
    leaving += begin(
        sems, 11, (keep_ref.at[:, cols], keep_out.at[:, cols]), (away_ref.at[:, cols], away_out.at[:, cols])
    )
    finish(loads[6:8])
    attention_back(0, 4, dattn_ref, probs_ref, qkv_ref, dqkv_ref)
    leaving += begin(sems, 13, (dqkv_ref, dqkv_out))
    finish(loads[8:])
    for part in range(3):
        cols = slice(D + 128 + part * 512, D + 128 + (part + 1) * 512)
        grad = tn(h1p_ref[...], dqkv_ref[:, part * 512 : (part + 1) * 512]).astype(BF)
        put_rows(keep_ref, away_ref, cols, grad)
        leaving += begin(
            sems,
            14 + 2 * part,
            (keep_ref.at[:, cols], keep_out.at[:, cols]),
            (away_ref.at[:, cols], away_out.at[:, cols]),
        )
    finish(leaving)


def back_one(nat, sid, gate, router, vec, d_back, x_mid, cotangent, w, attnp, h2, probs, qkv, h1p):
    vmem = pl.BlockSpec(memory_space=pltpu.VMEM)
    anywhere = pl.BlockSpec(memory_space=pl.ANY)
    ins = [
        like(16, LINE, 128), like(ROW, D, dtype=F32), like(ROW, D), like(D, D), like(ROW, D),
        like(ROW, D), like(8, ROW, ROW), like(ROW, 3 * D), like(ROW, D),
    ]
    outs = [
        like(ROW, D, dtype=F32), like(ROW, D), like(ROW, 1536), like(384, 2432), like(384, 2432),
    ]
    return pl.pallas_call(
        back_one_body,
        in_specs=[vmem] * 5 + [anywhere] * 9,
        out_specs=[anywhere] * 5,
        out_shape=outs,
        scratch_shapes=[pltpu.VMEM(b.shape, b.dtype) for b in ins + outs]
        + [pltpu.VMEM((4 * CAP, D), BF), pltpu.VMEM((4 * CAP, 128), BF)]
        + [pltpu.SemaphoreType.DMA((20,))],
        compiler_params=pltpu.CompilerParams(vmem_limit_bytes=62 * MIB),
        cost_estimate=SMALL,
    )(nat, sid, gate, router, vec, d_back, x_mid, cotangent, w, attnp, h2, probs, qkv, h1p)


def back_two_body(
    nat_ref, vec_ref, dattn_in, probs_in, qkv_in, h1p_in, first_in, w_in, tok_in, dxm_in,
    gx_out, keep_out, away_out, dattn_ref, probs_ref, qkv_ref, h1p_ref, first_ref, w_ref, tok_ref,
    dxm_ref, gx_ref, keep_ref, away_ref, second_ref, sems,
):
    sources = (
        dattn_in, qkv_in, probs_in.at[8:], h1p_in, first_in, w_in.at[:, : 3 * D], tok_in, dxm_in,
    )
    targets = (dattn_ref, qkv_ref, probs_ref, h1p_ref, first_ref, w_ref, tok_ref, dxm_ref)
    pairs = list(zip(sources, targets))
    loads = begin(sems, 0, *pairs[:3])
    turn = hot(iota((D, D), 0) == nat_ref[...])
    finish(loads)
    loads += begin(sems, 3, *pairs[3:])
    attention_back(4, 2, dattn_ref, probs_ref, qkv_ref, second_ref)
    finish(loads[3:6])
    d_h1p = jnp.zeros((ROW, D), F32)
    for part in range(3):
        middle = part * D + 512
        d_second = second_ref[:, part * 256 : (part + 1) * 256]
        grad = tn(h1p_ref[...], d_second).astype(BF)
        put_rows(keep_ref, away_ref, slice(part * 256, (part + 1) * 256), grad)
        d_h1p = d_h1p + nt(first_ref[:, part * 512 : (part + 1) * 512], w_ref[:, part * D : middle])
        d_h1p = d_h1p + nt(d_second, w_ref[:, middle : (part + 1) * D])
    cols = slice(0, D)
    leaving = begin(
        sems, 8, (keep_ref.at[:, cols], keep_out.at[:, cols]), (away_ref.at[:, cols], away_out.at[:, cols])
    )
    finish(loads[6:])
    d_h1 = nt(d_h1p.astype(BF), turn)
    x_hat, scale = norm(tok_ref[...].astype(F32))
    d_in, d_gain, d_bias = norm_back(d_h1, x_hat, scale, vec_ref[0:1])
    gx_ref[...] = dxm_ref[...] + d_in
    leaving += begin(sems, 10, (gx_ref, gx_out))
    sub = iota((128, D), 0)
    rows = jnp.where(sub == 16, d_gain, 0.0) + jnp.where(sub == 18, d_bias, 0.0)
    small = tn(turn, jnp.transpose(rows).astype(BF)).astype(BF)
    cols = slice(D, D + 128)
    put_rows(keep_ref, away_ref, cols, small)
    leaving += begin(
        sems, 11, (keep_ref.at[:, cols], keep_out.at[:, cols]), (away_ref.at[:, cols], away_out.at[:, cols])
    )
    finish(leaving)


def back_two(nat, vec, d_attn, probs, qkv, h1p, first, w, tokens, d_x_mid):
    vmem = pl.BlockSpec(memory_space=pltpu.VMEM)
    anywhere = pl.BlockSpec(memory_space=pl.ANY)
    ins = [
        like(ROW, D), like(4, ROW, ROW), like(ROW, 3 * D), like(ROW, D), like(ROW, 1536),
        like(D, 3 * D), like(ROW, D), like(ROW, D, dtype=F32),
    ]
    outs = [like(ROW, D, dtype=F32), like(384, 896), like(384, 896)]
    return pl.pallas_call(
        back_two_body,
        in_specs=[vmem] * 2 + [anywhere] * 8,
        out_specs=[anywhere] * 3,
        out_shape=outs,
        scratch_shapes=[pltpu.VMEM(b.shape, b.dtype) for b in ins + outs]
        + [pltpu.VMEM((ROW, D), BF), pltpu.SemaphoreType.DMA((13,))],
        compiler_params=pltpu.CompilerParams(vmem_limit_bytes=62 * MIB),
        cost_estimate=SMALL,
    )(nat, vec, d_attn, probs, qkv, h1p, first, w, tokens, d_x_mid)


def merge_body(sid_ref, ret_ref, gate_ref, xmid_ref, out_ref):
    s0, s1 = sid_ref[:, 0:1], sid_ref[:, 1:2]
    y0 = y1 = jnp.zeros((ROW, D), F32)
    for part in range(4):
        slot = iota((ROW, 4 * CAP), 1) + part * 4 * CAP
        values = ret_ref[part * 4 * CAP : (part + 1) * 4 * CAP, :]
        y0 = y0 + nn(hot(slot == s0), values)
        y1 = y1 + nn(hot(slot == s1), values)
    out_ref[...] = (xmid_ref[...] + (gate_ref[:, 0:1] * y0 + gate_ref[:, 1:2] * y1)).astype(BF)


def merge(sid, returned, gate, x_mid):
    return pl.pallas_call(
        merge_body,
        out_shape=like(ROW, D),
        compiler_params=pltpu.CompilerParams(vmem_limit_bytes=40 * MIB),
        cost_estimate=SMALL,
    )(sid, returned, gate, x_mid)


def to_blocks_body(offsets, place_ref, *refs):
    count = len(offsets)
    held = refs[count + 1 : 2 * count + 1]
    out_ref, total, sems = refs[count], refs[-2], refs[-1]
    sources = [ref.at[pl.ds(0, 96), :] for ref in refs[:count]]
    loads = begin(sems, 0, *zip(sources, held))
    total[...] = jnp.zeros(total.shape, F32)
    for load, part, offset in zip(loads, held, offsets):
        finish([load])
        total[0:96, offset : offset + part.shape[1]] += part[...].astype(F32)
    x, y = place_ref[0], 2 * place_ref[1] + place_ref[2]
    for k in range(16):
        to = lax.rem(x - k % 4 + 4, 4) * 4 + lax.rem(y - k // 4 + 4, 4)
        out_ref[to] = total[6 * k : 6 * k + 8, :].astype(BF)


def to_blocks(place, groups):
    offsets, parts = zip(*groups)
    width = max(offset + part.shape[1] for offset, part in groups)
    return pl.pallas_call(
        functools.partial(to_blocks_body, offsets),
        in_specs=[pl.BlockSpec(memory_space=pltpu.SMEM)]
        + [pl.BlockSpec(memory_space=pl.ANY)] * len(parts),
        out_shape=like(16, 8, width),
        scratch_shapes=[pltpu.VMEM((96, part.shape[1]), BF) for part in parts]
        + [pltpu.VMEM((104, width), F32), pltpu.SemaphoreType.DMA((len(parts),))],
        compiler_params=pltpu.CompilerParams(vmem_limit_bytes=60 * MIB),
        cost_estimate=SMALL,
    )(place, *parts)


def from_blocks_body(in_ref, qkv_ref, out_ref, small_ref):
    total = in_ref[0].astype(F32)
    for k in range(1, 16):
        total = total + in_ref[k].astype(F32)
    out_ref[...] = total[:6, :D]
    for part in range(3):
        qkv_ref[:, part * D : part * D + 512] = total[:6, 896 + part * 512 : 1408 + part * 512]
        qkv_ref[:, part * D + 512 : (part + 1) * D] = total[:6, 2432 + part * 256 : 2688 + part * 256]
    small_ref[...] = total[:6, D : D + 128] + total[:6, 3200:3328]


def from_blocks(blocks):
    return pl.pallas_call(
        from_blocks_body,
        out_shape=[like(6, 3 * D, dtype=F32), like(6, D, dtype=F32), like(6, 128, dtype=F32)],
        compiler_params=pltpu.CompilerParams(vmem_limit_bytes=16 * MIB),
        cost_estimate=SMALL,
    )(blocks)


def prepare_body(core_ref, *refs):
    sources, (block_ref, mine_ref, other_ref) = refs[:9], refs[9:12]
    held, turned, sems = refs[12:21], refs[21], refs[22]
    loads = begin(sems, 0, *zip(sources, held))
    qkv_ref, out_ref, router_ref, gains_ref, biases_ref, up_t, down_t, up_f, down_f = held
    finish(loads[:5])
    block_ref[...] = jnp.zeros(block_ref.shape, BF)
    block_ref[0:6, : 3 * D] = qkv_ref[...].astype(BF)
    block_ref[0:6, 3 * D : FF] = out_ref[...].astype(BF)
    turned[...] = jnp.zeros((128, 128), F32)
    turned[16:18, 0:6] = gains_ref[...]
    turned[18:20, 0:6] = biases_ref[...]
    vectors = jnp.transpose(turned[...])[0:8]
    turned[0:6, 0:16] = router_ref[...]
    keep = iota((8, 128), 1) < 16
    small = jnp.where(keep, turned[0:8, :], vectors)
    small = jnp.where(iota((8, 128), 0) < 6, small, 0.0)
    block_ref[:, FF:] = small.astype(BF)
    trained = core_ref[0] == 0
    finish(loads[5:])
    for j in range(4):
        cols, rows = slice(j * D, (j + 1) * D), slice(j * 48, (j + 1) * 48)
        low, fixed = up_t[0, :, cols].astype(BF), up_f[0, :, cols]
        mine_ref[rows, :] = jnp.where(trained, low, fixed)
        other_ref[rows, :] = jnp.where(trained, fixed, low)
    low = down_t[0].astype(BF)
    mine_ref[192:, :] = jnp.where(trained, low, down_f[0])
    other_ref[192:, :] = jnp.where(trained, down_f[0], low)


def prepare(core, *arrays):
    anywhere = pl.BlockSpec(memory_space=pl.ANY)
    return pl.pallas_call(
        prepare_body,
        in_specs=[pl.BlockSpec(memory_space=pltpu.SMEM)] + [anywhere] * 9,
        out_shape=[like(8, FF + 128), like(384, D), like(384, D)],
        scratch_shapes=[pltpu.VMEM(array.shape, array.dtype) for array in arrays]
        + [pltpu.VMEM((128, 128), F32), pltpu.SemaphoreType.DMA((9,))],
        compiler_params=pltpu.CompilerParams(vmem_limit_bytes=60 * MIB),
        cost_estimate=SMALL,
    )(core, *arrays)


def pack_body(core_ref, mine_in, got_in, to_ref, sems):
    pairs = []
    for source, core in ((mine_in, core_ref[0]), (got_in, 1 - core_ref[0])):
        for j in range(4):
            rows = pl.ds(j * 96 + core * 48, 48)
            pairs.append((source.at[pl.ds(j * 48, 48), :], to_ref.at[rows, :]))
        pairs.append((source.at[pl.ds(192, 192), :], to_ref.at[pl.ds(384 + core * 192, 192), :]))
    finish(begin(sems, 0, *pairs))


def pack(core, mine, got):
    anywhere = pl.BlockSpec(memory_space=pl.ANY)
    return pl.pallas_call(
        pack_body,
        in_specs=[pl.BlockSpec(memory_space=pltpu.SMEM)] + [anywhere] * 2,
        out_shape=like(D, D),
        scratch_shapes=[pltpu.SemaphoreType.DMA((10,))],
        compiler_params=pltpu.CompilerParams(vmem_limit_bytes=16 * MIB),
        cost_estimate=SMALL,
    )(core, mine, got)


def shift(value, axis, by):
    count = lax.axis_size(axis)
    return lax.ppermute(value, axis, [(i, (i + by) % count) for i in range(count)])


def ordered(mine, other, index):
    first = jnp.where(index == 0, mine, other)
    second = jnp.where(index == 0, other, mine)
    return first, second


FAR = ("x", "yh", "yl")
PEERS = ("c", "z", "yl")


def to_all(rows, names):
    return lax.all_to_all(rows, names, split_axis=0, concat_axis=0, tiled=True)


def spread_x(block):
    return jnp.stack([block] + [shift(block, "x", step) for step in (1, 2, 3)])


def spread_y(along_x):
    near = [along_x] + [shift(along_x, ("yh", "yl"), step) for step in (1, 2, 3)]
    return jnp.stack(near)[:, :, :6].reshape(96, along_x.shape[2])


def natural_rows():
    x, c, z = (lax.axis_index(name) for name in ("x", "c", "z"))
    y = lax.axis_index("yh") * 2 + lax.axis_index("yl")
    row = jnp.arange(768)
    step, other, i = row // 192, (row // 96) % 2, row % 96
    core, deep = (c + other) % 2, (z - step) % 4
    high, long = (y - i // 24) % 4, (x - (i // 6) % 4) % 4
    device = ((long * 2 + high // 2) * 2 + core) * 8 + deep * 2 + high % 2
    return (device * 6 + i % 6).astype(jnp.int32)


def step_of(keep, got, step):
    rows = slice(step * 96, (step + 1) * 96)
    return (keep[rows].astype(F32) + got[rows].astype(F32)).astype(BF)


def along_z(keep, got):
    return [shift(step_of(keep, got, step), "z", -step) for step in (1, 2, 3)]


def take_body(core_ref, *refs):
    sources, (to_ref, *held), sems = refs[1:3], refs[3:6], refs[6]
    rows = held[0].shape[0]

    @pl.when(core_ref[0] == 1)
    def _():
        targets = [to_ref.at[pl.ds(at, rows), :] for at in (0, rows)]
        loads, stores = begin(sems, 0, *zip(sources, held)), []
        for i in range(2):
            finish(loads[i : i + 1])
            stores += begin(sems, 2 + i, (held[i], targets[i]))
        finish(stores)


def take(core, kept, *sent):
    got = [lax.ppermute(part, "c", [(0, 1)]) for part in sent]
    anywhere = pl.BlockSpec(memory_space=pl.ANY)
    return pl.pallas_call(
        take_body,
        in_specs=[pl.BlockSpec(memory_space=pltpu.SMEM)] + [anywhere] * 3,
        out_specs=anywhere,
        out_shape=like(*kept.shape),
        input_output_aliases={1: 0},
        scratch_shapes=[pltpu.VMEM(part.shape, part.dtype) for part in got]
        + [pltpu.SemaphoreType.DMA((4,))],
        compiler_params=pltpu.CompilerParams(vmem_limit_bytes=62 * MIB),
        cost_estimate=SMALL,
    )(core, kept, *got)


def over_y(mine):
    y = lax.axis_index("yh")
    parts = mine.reshape(2, mine.shape[0] // 2, mine.shape[1])
    kept, sent = (lax.dynamic_index_in_dim(parts, at, 0, False) for at in (y, 1 - y))
    return kept.astype(F32) + shift(sent, "yh", 1).astype(F32)


def owned(mine, axis):
    return lax.psum_scatter(mine, axis, scatter_dimension=0, tiled=True)


def shards(
    tokens,
    seq_lengths,
    key_mask,
    routes,
    cotangent,
    qkv_weight,
    out_weight,
    router_weight,
    norm_gains,
    norm_biases,
    up_train,
    down_train,
    up_frozen,
    down_frozen,
):
    core = lax.axis_index("c")

    place = jnp.stack([lax.axis_index(name) for name in ("x", "yh", "yl")]).astype(jnp.int32)

    block, mine, other = prepare(
        core.reshape(1), qkv_weight, out_weight, router_weight, norm_gains, norm_biases, up_train,
        down_train, up_frozen, down_frozen,
    )
    other = shift(other, "c", 1)
    block, routes, other = lax.optimization_barrier((block, routes, other))
    along_x = spread_x(block)

    both = pack(core.reshape(1), mine, other)
    along_x, both = lax.optimization_barrier((along_x, both))
    rows = spread_y(along_x)
    nat = natural_rows().reshape(1, D)
    g_slots, sid, sidt = route(routes, cotangent)
    near = lax.all_gather(both, "x", tiled=True)

    rows, g_slots, both = lax.optimization_barrier((rows, g_slots, both))
    parts = [rows] + [shift(rows, "z", step) for step in (1, 2, 3)]
    both = shift(both, "yh", 1)
    parts, both, g_slots = lax.optimization_barrier((parts, both, g_slots))
    pieces = []
    for part in parts:
        pieces += [part, shift(part, "c", 1)]
    far = lax.all_gather(both, "x", tiled=True)

    g_rows = to_all(g_slots.reshape(16, CAP, D), PEERS)
    w, h1p, qkv, probs, attnp, x_mid, h2, gate, vec, router, sent = forward(
        seq_lengths[0], nat, key_mask.reshape(1, ROW), tokens, sid, sidt, pieces
    )
    sent, g_rows = lax.optimization_barrier((sent, g_rows))

    arrived = to_all(sent, PEERS)
    out, back, x_rows, d_out, act, d_up = experts(
        place, arrived, g_rows, near, far
    )
    d_back = to_all(back, PEERS)
    up_all = take(core.reshape(1), *up_grad(x_rows, d_up))
    down_parts = down_grad(d_out, act)
    d_back, out, up_all, down_parts = lax.optimization_barrier((d_back, out, up_all, down_parts))

    returned = to_all(out, PEERS)
    up_all, down_all = owned(up_all, "x"), take(core.reshape(1), *down_parts)
    d_x_mid, d_attn, first, keep, away = back_one(
        nat, sid, gate, router, vec, d_back, x_mid, cotangent, w, attnp, h2,
        probs, qkv, h1p,
    )
    input_grad, *last = back_two(nat, vec, d_attn, probs, qkv, h1p, first, w, tokens, d_x_mid)
    got = shift(away, "c", 1)
    keep, got, returned, down_all = lax.optimization_barrier((keep, got, returned, down_all))
    down_all = owned(down_all, "x")
    one, two, three = (step_of(keep, got, step) for step in (1, 2, 3))
    one, three = shift(one, "z", -1), shift(three, "z", -3)
    two = [shift(half, "z", -2) for half in (two[:, :1280], two[:, 1280:])]
    one, three, two[0], last, up_all = lax.optimization_barrier((one, three, two[0], last, up_all))
    groups = [(0, keep), (0, got), (0, one), (0, three), (0, two[0]), (1280, two[1])]
    up_all = over_y(up_all)
    keep, got = last[0], shift(last[1], "c", 1)
    groups += [(2432, part) for part in (keep, got, *along_z(keep, got))]
    offsets, parts = zip(*groups)
    parts, down_all, up_all = lax.optimization_barrier((parts, down_all, up_all))
    down_all = owned(down_all, "yh")
    blocks = to_blocks(place, list(zip(offsets, parts)))
    blocks, returned = lax.optimization_barrier((blocks, returned))
    blocks, down_all = lax.optimization_barrier((to_all(blocks, FAR), down_all))
    own_qkv, own_out, small = from_blocks(blocks)
    grad_up, grad_down = up_all.astype(F32)[None], down_all.astype(F32)[None]
    block_out = merge(sid, returned.reshape(16 * CAP, D), gate, x_mid)
    return (
        block_out,
        input_grad,
        own_qkv,
        own_out,
        small[:, :16],
        small[:, 16:18].T,
        small[:, 18:20].T,
        grad_up,
        grad_down,
    )


def solution(mesh):
    fine = Mesh(mesh.devices.reshape(SIZES), NAMES)
    by_row = P(NAMES, None)
    by_column = P(None, NAMES)
    by_expert = P(NARROW, WIDE, None)
    return jax.shard_map(
        shards,
        mesh=fine,
        in_specs=(by_row, by_row, P(NAMES)) + (by_row,) * 5 + (by_column,) * 2 + (by_expert,) * 4,
        out_specs=(by_row,) * 5 + (by_column,) * 2 + (by_expert,) * 2,
        check_vma=False,
    )
```

```python
import functools

import jax
import jax.numpy as jnp
from jax import lax
from jax.experimental import pallas as pl
from jax.experimental.pallas import tpu as pltpu
from jax.sharding import Mesh
from jax.sharding import PartitionSpec as P

SIZES = (4, 2, 2, 4, 2)
NAMES = ("x", "yh", "c", "z", "yl")
WIDE = ("x", "yh", "c")
NARROW = ("z", "yl")
BF = jnp.bfloat16
F32 = jnp.float32
ROW = 512
D = 768
FF = 3072
CAP = 96
LINE = 592
SOURCES = 4
GELU_ONE = 0.7978845608028654
GELU_CUBE = GELU_ONE * 0.044715
MIB = 1024 * 1024
SMALL = pl.CostEstimate(flops=10**6, bytes_accessed=10**4, transcendentals=0)


def nn(a, b):
    return jnp.dot(a, b, preferred_element_type=F32)


def nt(a, b):
    return lax.dot_general(a, b, (((1,), (1,)), ((), ())), preferred_element_type=F32)


def tn(a, b):
    return lax.dot_general(a, b, (((0,), (0,)), ((), ())), preferred_element_type=F32)


def iota(shape, dim):
    return lax.broadcasted_iota(jnp.int32, shape, dim)


def hot(mask):
    return jnp.where(mask, 1.0, 0.0).astype(BF)


def like(*dims, dtype=BF):
    return jax.ShapeDtypeStruct(dims, dtype)


def tail_of(line):
    high = line.astype(BF).astype(F32)
    row = iota((16, 128), 0)
    return jnp.where(row == 0, high, jnp.where(row == 1, line - high, 0.0)).astype(BF)


def line_of(tail):
    tail = tail.astype(F32)
    return tail[0:1] + tail[1:2]


def begin(sems, first, *pairs):
    copies = [
        pltpu.make_async_copy(source, target, sems.at[first + i])
        for i, (source, target) in enumerate(pairs)
    ]
    for copy in copies:
        copy.start()
    return copies


def finish(copies):
    for copy in copies:
        copy.wait()


def norm(x):
    centered = x - jnp.mean(x, -1, keepdims=True)
    scale = lax.rsqrt(jnp.mean(centered * centered, -1, keepdims=True) + 1e-5)
    return centered * scale, scale


def norm_back(d_out, x_hat, scale, gain):
    t = d_out * gain
    d_in = scale * (
        t - jnp.mean(t, -1, keepdims=True) - x_hat * jnp.mean(t * x_hat, -1, keepdims=True)
    )
    return d_in, jnp.sum(d_out * x_hat, 0, keepdims=True), jnp.sum(d_out, 0, keepdims=True)


def route_body(routes_ref, cot_ref, g_ref, sid_ref, sidt_ref):
    lane = iota((ROW, 128), 1)
    r0, r1 = routes_ref[:, 0:1], routes_ref[:, 1:2]
    either = hot((lane == r0) | (lane == r1))
    earlier = nn(hot(iota((ROW, ROW), 1) < iota((ROW, ROW), 0)), either)
    p0 = jnp.sum(jnp.where(lane == r0, earlier, 0.0), 1, keepdims=True).astype(jnp.int32)
    p1 = jnp.sum(jnp.where(lane == r1, earlier, 0.0), 1, keepdims=True).astype(jnp.int32)
    columns = (
        jnp.where(p0 < CAP, r0 * CAP + p0, -1),
        jnp.where(p1 < CAP, r1 * CAP + p1, -1),
        r0,
    )
    table = jnp.broadcast_to(r1, (ROW, 128))
    for at, column in enumerate(columns):
        table = jnp.where(lane == at, column, table)
    sid_ref[...] = table
    turned = jnp.transpose(table.astype(F32))[0:8].astype(jnp.int32)
    sidt_ref[...] = turned
    for part in range(4):
        slot = iota((4 * CAP, ROW), 0) + part * 4 * CAP
        pick = hot((slot == turned[0:1]) | (slot == turned[1:2]))
        g_ref[part * 4 * CAP : (part + 1) * 4 * CAP, :] = nn(pick, cot_ref[...]).astype(BF)


def route(routes, cotangent):
    return pl.pallas_call(
        route_body,
        out_shape=[like(16 * CAP, D), like(ROW, 128, dtype=jnp.int32), like(8, ROW, dtype=jnp.int32)],
        compiler_params=pltpu.CompilerParams(vmem_limit_bytes=32 * MIB),
        cost_estimate=SMALL,
    )(routes, cotangent)


def forward_body(*refs):
    lens_ref, nat_ref, mask_ref, tok_ref, sid_ref, sidt_ref = refs[:6]
    pieces, refs = refs[6:14], refs[14:]
    w_out, h1p_out, qkv_out, probs_out, attnp_out, xmid_out, h2_out, back_out = refs[:8]
    gate_ref, vec_ref, router_ref, sent_ref = refs[8:12]
    w_ref, rest_ref, h1p_ref, qkv_ref, probs_ref, attn, attnp_ref, xmid_ref, h2_ref = refs[12:21]
    back_ref, bias, nat_w, sems = refs[21:]
    rows = [pl.ds(at * 96, 96) for at in range(8)]
    small = [(piece.at[:, FF:], rest_ref.at[to, :]) for piece, to in zip(pieces, rows)]
    large = [(piece.at[:, :FF], w_ref.at[to, :]) for piece, to in zip(pieces, rows)]
    small, large = begin(sems, 0, *small), begin(sems, 8, *large)
    turn = hot(iota((D, D), 0) == nat_ref[...])
    x = tok_ref[...].astype(F32)
    x_hat = norm(x)[0]
    finish(small)
    rest = nn(turn, rest_ref[...])
    vectors = jnp.transpose(rest)[16:24]
    router_ref[...] = rest.astype(BF)
    vec_ref[...] = vectors
    h1 = (x_hat * vectors[0:1] + vectors[2:3]).astype(BF)
    h1p_ref[...] = nn(h1, turn).astype(BF)
    back_ref[...] = jnp.transpose(turn)
    finish(large)
    for part in range(4):
        cols = slice(part * D, (part + 1) * D)
        nat_w[:, cols] = nn(turn, w_ref[:, cols]).astype(BF)
        if part < 3:
            qkv_ref[:, cols] = nn(h1, nat_w[:, cols]).astype(BF)
    away = begin(
        sems, 0, (nat_w, w_out), (h1p_ref, h1p_out), (qkv_ref, qkv_out), (back_ref, back_out)
    )

    end_one = lens_ref[0]
    end_two = end_one + lens_ref[1]

    def segment(place):
        return (place >= end_one).astype(jnp.int32) + (place >= end_two).astype(jnp.int32)

    query, key = iota((ROW, ROW), 0), iota((ROW, ROW), 1)
    same = segment(iota((ROW, 1), 0)) == segment(iota((1, ROW), 1))
    allowed = same & (key <= query) & ((mask_ref[...] == 1) | (key == query))
    bias[...] = jnp.where(allowed, 0.0, -1e30)
    low = iota((1, 128), 1) < 64
    half = ROW // 2
    zero = jnp.zeros((), BF)

    def pair(index, carry):
        at = pl.multiple_of(index * 128, 128)
        q = qkv_ref[:, pl.ds(at, 128)] * jnp.asarray(0.125, BF)
        k = qkv_ref[:, pl.ds(D + at, 128)]
        v = qkv_ref[:, pl.ds(2 * D + at, 128)]
        out = [None, None]
        for head in range(2):
            mine = low if head == 0 else jnp.logical_not(low)
            k_mine, v_mine = jnp.where(mine, k, zero), jnp.where(mine, v, zero)
            for block in range(2):
                count, rows = half * (block + 1), slice(block * half, (block + 1) * half)
                scores = nt(q[rows], k_mine[:count]) + bias[rows, :count]
                e = jnp.exp(scores - jnp.max(scores, 1, keepdims=True))
                probs = (e * (1.0 / jnp.sum(e, 1, keepdims=True))).astype(BF)
                probs_ref[2 * index + head, rows, :count] = probs
                if block == 0:
                    probs_ref[2 * index + head, rows, count:] = jnp.zeros((half, half), BF)
                term = nn(probs, v_mine[:count])
                out[block] = term if head == 0 else out[block] + term
        for block in range(2):
            attn[block * half : (block + 1) * half, pl.ds(at, 128)] = out[block].astype(BF)
        heads = pl.ds(2 * index, 2)
        begin(sems, 8 + index, (probs_ref.at[heads], probs_out.at[heads]))
        return carry

    lax.fori_loop(0, 6, pair, 0)
    for index in range(6):
        heads = pl.ds(2 * index, 2)
        away.append(
            pltpu.make_async_copy(probs_ref.at[heads], probs_out.at[heads], sems.at[8 + index])
        )
    attnp_ref[...] = nn(attn[...], turn).astype(BF)
    x_mid = x + nn(attn[...], nat_w[:, 3 * D :])
    xmid_ref[...] = x_mid
    h2 = (norm(x_mid)[0] * vectors[1:2] + vectors[3:4]).astype(BF)
    h2_ref[...] = h2
    away += begin(sems, 4, (attnp_ref, attnp_out), (xmid_ref, xmid_out), (h2_ref, h2_out))
    logits = nn(h2, router_ref[...])
    lane = iota((ROW, 128), 1)
    s0, s1, r0, r1 = (sid_ref[:, at : at + 1] for at in range(4))
    c0 = jnp.sum(jnp.where(lane == r0, logits, 0.0), 1, keepdims=True)
    c1 = jnp.sum(jnp.where(lane == r1, logits, 0.0), 1, keepdims=True)
    g0, g1 = 1.0 / (1.0 + jnp.exp(c1 - c0)), 1.0 / (1.0 + jnp.exp(c0 - c1))
    gate_ref[...] = jnp.where(lane == 0, g0, jnp.where(lane == 1, g1, 0.0))
    for part in range(4):
        slot = iota((4 * CAP, ROW), 0) + part * 4 * CAP
        pick = hot((slot == sidt_ref[0:1]) | (slot == sidt_ref[1:2]))
        rows = nn(pick, h2_ref[...]).astype(BF)
        for i in range(4):
            for j in range(6):
                block = rows[i * CAP : (i + 1) * CAP, j * 128 : (j + 1) * 128]
                sent_ref[4 * part + i, j * CAP : (j + 1) * CAP, :] = block
    for expert in range(16):
        slot = lane + expert * CAP
        line = jnp.sum(
            jnp.where(slot == s0, g0, 0.0) + jnp.where(slot == s1, g1, 0.0), 0, keepdims=True
        )
        sent_ref[expert, 6 * CAP : LINE, :] = tail_of(line)
    finish(away)


def forward(lens, nat, mask, tokens, sid, sidt, pieces):
    vmem = pl.BlockSpec(memory_space=pltpu.VMEM)
    anywhere = pl.BlockSpec(memory_space=pl.ANY)
    moved = [
        like(D, FF),
        like(ROW, D),
        like(ROW, 3 * D),
        like(12, ROW, ROW),
        like(ROW, D),
        like(ROW, D, dtype=F32),
        like(ROW, D),
        like(D, D),
    ]
    held = [like(ROW, 128, dtype=F32), like(8, D, dtype=F32), like(D, 128), like(16, LINE, 128)]
    buffers = [like(D, FF), like(D, 128), *moved[1:4], like(ROW, D), *moved[4:]]
    return pl.pallas_call(
        forward_body,
        in_specs=[pl.BlockSpec(memory_space=pltpu.SMEM)] + [vmem] * 5 + [anywhere] * 8,
        out_specs=[anywhere] * 8 + [vmem] * 4,
        out_shape=moved + held,
        scratch_shapes=[pltpu.VMEM(b.shape, b.dtype) for b in buffers]
        + [pltpu.VMEM((ROW, ROW), F32), pltpu.VMEM((D, FF), BF), pltpu.SemaphoreType.DMA((16,))],
        compiler_params=pltpu.CompilerParams(vmem_limit_bytes=62 * MIB),
        cost_estimate=SMALL,
    )(lens, nat, mask, tokens, sid, sidt, *pieces)


def expert_body(
    place_ref, sent_ref, g_ref, near_in, far_in, out_ref, back_ref, x_ref, dout_ref, act_ref,
    dup_ref, up_ref, down_ref, sems,
):
    def loads():
        for source, y in ((near_in, place_ref[1]), (far_in, 1 - place_ref[1])):
            for x in range(4):
                block = 2 * x + y
                for j in range(4):
                    rows, cols = pl.ds(block * 96, 96), pl.ds(j * D, D)
                    yield source.at[pl.ds(x * D + j * 96, 96), :], up_ref.at[rows, cols]
                rows = pl.ds(block * 384, 384)
                yield source.at[pl.ds(x * D + 384, 384), :], down_ref.at[rows, :]

    @pl.when(pl.program_id(0) == 0)
    def _():
        copies = [
            pltpu.make_async_copy(source, target, sems.at[i])
            for i, (source, target) in enumerate(loads())
        ]
        for copy in copies:
            copy.start()
        for copy in copies:
            copy.wait()

    for s in range(SOURCES):
        first, last = s * CAP, (s + 1) * CAP
        for j in range(6):
            x_ref[first:last, j * 128 : (j + 1) * 128] = sent_ref[s, j * CAP : (j + 1) * CAP, :]
        gate = line_of(sent_ref[s, 6 * CAP : LINE, :])
        column = jnp.transpose(jnp.broadcast_to(gate, (128, 128)))[:CAP, :1]
        dout_ref[first:last, :] = (g_ref[s].astype(F32) * column).astype(BF)
    x, d_out = x_ref[...], dout_ref[...]
    for part in range(FF // 256):
        cols = slice(part * 256, (part + 1) * 256)
        up = nn(x, up_ref[:, cols])
        d_act = nt(d_out, down_ref[cols, :])
        square = up * up
        t = jnp.tanh(up * (GELU_ONE + GELU_CUBE * square))
        a = 0.5 + 0.5 * t
        act_ref[:, cols] = (up * a).astype(BF)
        slope = a + (up * (1.0 - t * t)) * (0.5 * GELU_ONE + 1.5 * GELU_CUBE * square)
        dup_ref[:, cols] = (d_act * slope).astype(BF)
    out = nn(act_ref[...], down_ref[...]).astype(BF)
    back = nt(dup_ref[...], up_ref[...]).astype(BF)
    for s in range(SOURCES):
        out_ref[s] = out[s * CAP : (s + 1) * CAP]
        for j in range(6):
            block = back[s * CAP : (s + 1) * CAP, j * 128 : (j + 1) * 128]
            back_ref[s, j * CAP : (j + 1) * CAP, :] = block
    for s in range(SOURCES):
        d_gate = jnp.sum(out_ref[s].astype(F32) * g_ref[s].astype(F32), -1, keepdims=True)
        d_gate = jnp.broadcast_to(d_gate, (CAP, 128))
        wide = jnp.concatenate([d_gate, jnp.zeros((128 - CAP, 128), F32)], 0)
        back_ref[s, 6 * CAP : LINE, :] = tail_of(jnp.transpose(wide)[0:1])


def experts(place, sent, g, near, far):
    rows = SOURCES * CAP
    anywhere = pl.BlockSpec(memory_space=pl.ANY)
    by_source = pl.BlockSpec((SOURCES, CAP, D), lambda i: (i, 0, 0))
    message = pl.BlockSpec((SOURCES, LINE, 128), lambda i: (i, 0, 0))
    by_rows = lambda width: pl.BlockSpec((rows, width), lambda i: (i, 0))
    return pl.pallas_call(
        expert_body,
        grid=(16 // SOURCES,),
        in_specs=[
            pl.BlockSpec(memory_space=pltpu.SMEM),
            message,
            by_source,
        ]
        + [anywhere] * 2,
        out_specs=[
            by_source, message, by_rows(D), by_rows(D), by_rows(FF), by_rows(FF),
        ],
        out_shape=[
            like(16, CAP, D),
            like(16, LINE, 128),
            like(16 * CAP, D),
            like(16 * CAP, D),
            like(16 * CAP, FF),
            like(16 * CAP, FF),
        ],
        scratch_shapes=[
            pltpu.VMEM((D, FF), BF),
            pltpu.VMEM((FF, D), BF),
            pltpu.SemaphoreType.DMA((40,)),
        ],
        compiler_params=pltpu.CompilerParams(vmem_limit_bytes=62 * MIB),
        cost_estimate=SMALL,
    )(place, sent, g, near, far)


def up_grad_body(x_ref, dup_ref, keep_ref, first_ref, last_ref):
    grad = tn(x_ref[...], dup_ref[...]).astype(BF)
    for block in range(8):
        rows, low = block * 96, (block % 4) * 48
        keep_ref[block * 48 : (block + 1) * 48, :] = grad[rows : rows + 48]
        away_ref = (first_ref, last_ref)[block // 4]
        away_ref[low : low + 48, :] = grad[rows + 48 : rows + 96]


def up_grad(x, d_up):
    columns = lambda rows: pl.BlockSpec((rows, D), lambda i: (0, i))
    return pl.pallas_call(
        up_grad_body,
        grid=(4,),
        in_specs=[pl.BlockSpec((16 * CAP, D), lambda i: (0, 0)), columns(16 * CAP)],
        out_specs=[columns(384), columns(192), columns(192)],
        out_shape=[like(384, FF), like(192, FF), like(192, FF)],
        compiler_params=pltpu.CompilerParams(vmem_limit_bytes=60 * MIB),
        cost_estimate=SMALL,
    )(x, d_up)


def down_grad_body(dout_ref, act_ref, keep_ref, first_ref, last_ref):
    grad = tn(act_ref[...], dout_ref[...]).astype(BF)
    for block in range(2):
        keep_ref[block * 192 : (block + 1) * 192, :] = grad[block * 384 : block * 384 + 192]
    away = jnp.concatenate([grad[192:384], grad[576:768]], 0)
    for part, away_ref in enumerate((first_ref, last_ref)):

        @pl.when(pl.program_id(0) // 2 == part)
        def _():
            away_ref[...] = away


def down_grad(d_out, act):
    rows = lambda index: pl.BlockSpec((384, D), index)
    return pl.pallas_call(
        down_grad_body,
        grid=(4,),
        in_specs=[
            pl.BlockSpec((16 * CAP, D), lambda i: (0, 0)),
            pl.BlockSpec((16 * CAP, D), lambda i: (0, i)),
        ],
        out_specs=[
            rows(lambda i: (i, 0)),
            rows(lambda i: (jnp.minimum(i, 1), 0)),
            rows(lambda i: (jnp.maximum(i - 2, 0), 0)),
        ],
        out_shape=[like(1536, D), like(768, D), like(768, D)],
        compiler_params=pltpu.CompilerParams(vmem_limit_bytes=60 * MIB),
        cost_estimate=SMALL,
    )(d_out, act)


def put_rows(keep_ref, away_ref, cols, values):
    for step in range(4):
        rows = slice(step * 96, (step + 1) * 96)
        keep_ref[rows, cols] = values[step * 192 : step * 192 + 96]
        away_ref[rows, cols] = values[step * 192 + 96 : (step + 1) * 192]


def attention_back(base, pairs, dattn_ref, probs_ref, qkv_ref, d_qkv):
    width = 128 * pairs
    low = iota((1, 128), 1) < 64
    zero = jnp.zeros((), BF)
    half = ROW // 2

    def add(terms, at, term):
        terms[at] = term if terms[at] is None else terms[at] + term

    def pair(index, carry):
        at = pl.multiple_of((base + index) * 128, 128)
        to = pl.multiple_of(index * 128, 128)
        q, k, v = (qkv_ref[:, pl.ds(part * D + at, 128)] for part in range(3))
        d_attn = dattn_ref[:, pl.ds(at, 128)]
        dq, dk, dv = [None, None], [None, None], [None, None]
        for head in range(2):
            mine = low if head == 0 else jnp.logical_not(low)
            q_mine, k_mine, v_mine, d_mine = (jnp.where(mine, t, zero) for t in (q, k, v, d_attn))
            for block in range(2):
                count, rows = half * (block + 1), slice(block * half, (block + 1) * half)
                probs = probs_ref[2 * index + head, rows, :count]
                d_probs = nt(d_mine[rows], v_mine[:count])
                wide = probs.astype(F32)
                weighted = wide * d_probs
                delta = jnp.sum(weighted, 1, keepdims=True)
                d_scores = (weighted - wide * delta).astype(BF)
                add(dq, block, nn(d_scores, k_mine[:count]))
                for other in range(block + 1):
                    keys = slice(other * half, (other + 1) * half)
                    add(dk, other, tn(d_scores[:, keys], q_mine[rows]))
                    add(dv, other, tn(probs[:, keys], d_mine[rows]))
        for block in range(2):
            rows = slice(block * half, (block + 1) * half)
            d_qkv[rows, pl.ds(to, 128)] = (dq[block] * 0.125).astype(BF)
            d_qkv[rows, pl.ds(width + to, 128)] = (dk[block] * 0.125).astype(BF)
            d_qkv[rows, pl.ds(2 * width + to, 128)] = dv[block].astype(BF)
        return carry

    lax.fori_loop(0, pairs, pair, 0, unroll=2)


def back_one_body(
    sid_ref, gate_ref, router_ref, vec_ref, dback_in, xmid_in, cot_in, w_in, attnp_in,
    h2_in, probs_in, qkv_in, h1p_in, turn_in, dxm_out, dattn_out, dqkv_out, keep_out, away_out,
    dback_ref, xmid_ref, cot_ref, w_ref, attnp_ref, h2_ref, probs_ref, qkv_ref, h1p_ref, turn_ref, dxm_ref,
    dattn_ref, dqkv_ref, keep_ref, away_ref, slots_ref, columns_ref, sems,
):
    sources = (
        dback_in, xmid_in, cot_in, w_in.at[:, 3 * D :], attnp_in, h2_in, turn_in, qkv_in, probs_in.at[:8],
        h1p_in,
    )
    targets = (
        dback_ref, xmid_ref, cot_ref, w_ref, attnp_ref, h2_ref, turn_ref, qkv_ref, probs_ref, h1p_ref,
    )
    pairs = list(zip(sources, targets))
    loads = begin(sems, 0, *pairs[:1])
    lane = iota((ROW, 128), 1)
    s0, s1, r0, r1 = (sid_ref[:, at : at + 1] for at in range(4))
    finish(loads)
    loads += begin(sems, 1, *pairs[1:])
    dg0 = dg1 = jnp.zeros((ROW, 128), F32)
    d_h2 = jnp.zeros((ROW, D), F32)
    columns_ref[...] = jnp.zeros((4 * CAP, 128), BF)
    for part in range(4):
        for i in range(4):
            message = dback_ref.at[4 * part + i]
            for j in range(6):
                block = message[j * CAP : (j + 1) * CAP, :]
                slots_ref[i * CAP : (i + 1) * CAP, j * 128 : (j + 1) * 128] = block
            terms = jnp.transpose(message[6 * CAP : LINE, :].astype(F32))
            columns_ref[i * CAP : (i + 1) * CAP, 0:16] = terms[:CAP].astype(BF)
        slot = iota((ROW, 4 * CAP), 1) + part * 4 * CAP
        first, second = hot(slot == s0), hot(slot == s1)
        dg0 = dg0 + nn(first, columns_ref[...])
        dg1 = dg1 + nn(second, columns_ref[...])
        d_h2 = d_h2 + nn(first + second, slots_ref[...])
    dg0, dg1 = dg0[:, 0:1] + dg0[:, 1:2], dg1[:, 0:1] + dg1[:, 1:2]
    g0, g1 = gate_ref[:, 0:1], gate_ref[:, 1:2]
    both = g0 * dg0 + g1 * dg1
    d_logits = jnp.where(lane == r0, g0 * (dg0 - both), 0.0)
    d_logits = d_logits + jnp.where(lane == r1, g1 * (dg1 - both), 0.0)
    high = d_logits.astype(BF)
    low = (d_logits - high.astype(F32)).astype(BF)
    d_h2 = d_h2 + nt(high, router_ref[...]) + nt(low, router_ref[...])
    finish(loads[1:3])
    x_hat, scale = norm(xmid_ref[...])
    d_in, d_gain, d_bias = norm_back(d_h2, x_hat, scale, vec_ref[1:2])
    d_x_mid = cot_ref[...].astype(F32) + d_in
    dxm_ref[...] = d_x_mid
    d_proj = d_x_mid.astype(BF)
    finish(loads[3:7])
    dattn_ref[...] = nt(d_proj, w_ref[...]).astype(BF)
    leaving = begin(sems, 10, (dxm_ref, dxm_out), (dattn_ref, dattn_out))
    put_rows(keep_ref, away_ref, slice(0, D), tn(attnp_ref[...], d_proj).astype(BF))
    d_router = tn(h2_ref[...], jnp.concatenate([high, low], 1))
    d_router = d_router[:, :128] + d_router[:, 128:]
    sub = iota((128, D), 0)
    rows = jnp.where(sub == 17, d_gain, 0.0) + jnp.where(sub == 19, d_bias, 0.0)
    small = d_router + jnp.transpose(rows)
    put_rows(keep_ref, away_ref, slice(D, D + 128), nn(turn_ref[...], small.astype(BF)).astype(BF))
    cols = slice(0, D + 128)
    leaving += begin(
        sems, 12, (keep_ref.at[:, cols], keep_out.at[:, cols]), (away_ref.at[:, cols], away_out.at[:, cols])
    )
    finish(loads[7:9])
    attention_back(0, 4, dattn_ref, probs_ref, qkv_ref, dqkv_ref)
    leaving += begin(sems, 14, (dqkv_ref, dqkv_out))
    finish(loads[9:])
    for part in range(3):
        cols = slice(D + 128 + part * 512, D + 128 + (part + 1) * 512)
        grad = tn(h1p_ref[...], dqkv_ref[:, part * 512 : (part + 1) * 512]).astype(BF)
        put_rows(keep_ref, away_ref, cols, grad)
        leaving += begin(
            sems,
            15 + 2 * part,
            (keep_ref.at[:, cols], keep_out.at[:, cols]),
            (away_ref.at[:, cols], away_out.at[:, cols]),
        )
    finish(leaving)


def back_one(
    sid, gate, router, vec, d_back, x_mid, cotangent, w, attnp, h2, probs, qkv, h1p, turn
):
    vmem = pl.BlockSpec(memory_space=pltpu.VMEM)
    anywhere = pl.BlockSpec(memory_space=pl.ANY)
    ins = [
        like(16, LINE, 128), like(ROW, D, dtype=F32), like(ROW, D), like(D, D), like(ROW, D),
        like(ROW, D), like(8, ROW, ROW), like(ROW, 3 * D), like(ROW, D), like(D, D),
    ]
    outs = [
        like(ROW, D, dtype=F32), like(ROW, D), like(ROW, 1536), like(384, 2432), like(384, 2432),
    ]
    return pl.pallas_call(
        back_one_body,
        in_specs=[vmem] * 4 + [anywhere] * 10,
        out_specs=[anywhere] * 5,
        out_shape=outs,
        scratch_shapes=[pltpu.VMEM(b.shape, b.dtype) for b in ins + outs]
        + [pltpu.VMEM((4 * CAP, D), BF), pltpu.VMEM((4 * CAP, 128), BF)]
        + [pltpu.SemaphoreType.DMA((21,))],
        compiler_params=pltpu.CompilerParams(vmem_limit_bytes=62 * MIB),
        cost_estimate=SMALL,
    )(sid, gate, router, vec, d_back, x_mid, cotangent, w, attnp, h2, probs, qkv, h1p, turn)


def back_two_body(
    vec_ref, dattn_in, probs_in, qkv_in, h1p_in, first_in, w_in, tok_in, dxm_in, turn_in,
    gx_out, keep_out, away_out, dattn_ref, probs_ref, qkv_ref, h1p_ref, first_ref, w_ref, tok_ref,
    dxm_ref, turn_ref, gx_ref, keep_ref, away_ref, second_ref, sems,
):
    sources = (
        dattn_in, qkv_in, probs_in.at[8:], h1p_in, first_in, w_in.at[:, : 3 * D], tok_in, dxm_in,
        turn_in,
    )
    targets = (dattn_ref, qkv_ref, probs_ref, h1p_ref, first_ref, w_ref, tok_ref, dxm_ref, turn_ref)
    pairs = list(zip(sources, targets))
    loads = begin(sems, 0, *pairs[:3])
    finish(loads)
    loads += begin(sems, 3, *pairs[3:])
    attention_back(4, 2, dattn_ref, probs_ref, qkv_ref, second_ref)
    finish(loads[3:6])
    d_h1 = jnp.zeros((ROW, D), F32)
    for part in range(3):
        middle = part * D + 512
        d_second = second_ref[:, part * 256 : (part + 1) * 256]
        grad = tn(h1p_ref[...], d_second).astype(BF)
        put_rows(keep_ref, away_ref, slice(part * 256, (part + 1) * 256), grad)
        d_h1 = d_h1 + nt(first_ref[:, part * 512 : (part + 1) * 512], w_ref[:, part * D : middle])
        d_h1 = d_h1 + nt(d_second, w_ref[:, middle : (part + 1) * D])
    cols = slice(0, D)
    leaving = begin(
        sems, 9, (keep_ref.at[:, cols], keep_out.at[:, cols]), (away_ref.at[:, cols], away_out.at[:, cols])
    )
    finish(loads[6:])
    x_hat, scale = norm(tok_ref[...].astype(F32))
    d_in, d_gain, d_bias = norm_back(d_h1, x_hat, scale, vec_ref[0:1])
    gx_ref[...] = dxm_ref[...] + d_in
    leaving += begin(sems, 11, (gx_ref, gx_out))
    sub = iota((128, D), 0)
    rows = jnp.where(sub == 16, d_gain, 0.0) + jnp.where(sub == 18, d_bias, 0.0)
    small = nn(turn_ref[...], jnp.transpose(rows).astype(BF)).astype(BF)
    cols = slice(D, D + 128)
    put_rows(keep_ref, away_ref, cols, small)
    leaving += begin(
        sems, 12, (keep_ref.at[:, cols], keep_out.at[:, cols]), (away_ref.at[:, cols], away_out.at[:, cols])
    )
    finish(leaving)


def back_two(vec, d_attn, probs, qkv, h1p, first, w, tokens, d_x_mid, turn):
    vmem = pl.BlockSpec(memory_space=pltpu.VMEM)
    anywhere = pl.BlockSpec(memory_space=pl.ANY)
    ins = [
        like(ROW, D), like(4, ROW, ROW), like(ROW, 3 * D), like(ROW, D), like(ROW, 1536),
        like(D, 3 * D), like(ROW, D), like(ROW, D, dtype=F32), like(D, D),
    ]
    outs = [like(ROW, D, dtype=F32), like(384, 896), like(384, 896)]
    return pl.pallas_call(
        back_two_body,
        in_specs=[vmem] + [anywhere] * 9,
        out_specs=[anywhere] * 3,
        out_shape=outs,
        scratch_shapes=[pltpu.VMEM(b.shape, b.dtype) for b in ins + outs]
        + [pltpu.VMEM((ROW, D), BF), pltpu.SemaphoreType.DMA((14,))],
        compiler_params=pltpu.CompilerParams(vmem_limit_bytes=62 * MIB),
        cost_estimate=SMALL,
    )(vec, d_attn, probs, qkv, h1p, first, w, tokens, d_x_mid, turn)


def merge_body(sid_ref, ret_ref, gate_ref, xmid_ref, out_ref):
    s0, s1 = sid_ref[:, 0:1], sid_ref[:, 1:2]
    y0 = y1 = jnp.zeros((ROW, D), F32)
    for part in range(4):
        slot = iota((ROW, 4 * CAP), 1) + part * 4 * CAP
        values = ret_ref[part * 4 * CAP : (part + 1) * 4 * CAP, :]
        y0 = y0 + nn(hot(slot == s0), values)
        y1 = y1 + nn(hot(slot == s1), values)
    out_ref[...] = (xmid_ref[...] + (gate_ref[:, 0:1] * y0 + gate_ref[:, 1:2] * y1)).astype(BF)


def merge(sid, returned, gate, x_mid):
    return pl.pallas_call(
        merge_body,
        out_shape=like(ROW, D),
        compiler_params=pltpu.CompilerParams(vmem_limit_bytes=40 * MIB),
        cost_estimate=SMALL,
    )(sid, returned, gate, x_mid)


def to_blocks_body(offsets, place_ref, *refs):
    count = len(offsets)
    held = refs[count + 1 : 2 * count + 1]
    out_ref, total, sems = refs[count], refs[-2], refs[-1]
    sources = [ref.at[pl.ds(0, 96), :] for ref in refs[:count]]
    loads = begin(sems, 0, *zip(sources, held))
    total[...] = jnp.zeros(total.shape, F32)
    for load, part, offset in zip(loads, held, offsets):
        finish([load])
        total[0:96, offset : offset + part.shape[1]] += part[...].astype(F32)
    x, y = place_ref[0], 2 * place_ref[1] + place_ref[2]
    for k in range(16):
        to = lax.rem(x - k % 4 + 4, 4) * 4 + lax.rem(y - k // 4 + 4, 4)
        out_ref[to] = total[6 * k : 6 * k + 8, :].astype(BF)


def to_blocks(place, groups):
    offsets, parts = zip(*groups)
    width = max(offset + part.shape[1] for offset, part in groups)
    return pl.pallas_call(
        functools.partial(to_blocks_body, offsets),
        in_specs=[pl.BlockSpec(memory_space=pltpu.SMEM)]
        + [pl.BlockSpec(memory_space=pl.ANY)] * len(parts),
        out_shape=like(16, 8, width),
        scratch_shapes=[pltpu.VMEM((96, part.shape[1]), BF) for part in parts]
        + [pltpu.VMEM((104, width), F32), pltpu.SemaphoreType.DMA((len(parts),))],
        compiler_params=pltpu.CompilerParams(vmem_limit_bytes=60 * MIB),
        cost_estimate=SMALL,
    )(place, *parts)


def from_blocks_body(in_ref, qkv_ref, out_ref, small_ref):
    total = in_ref[0].astype(F32)
    for k in range(1, 16):
        total = total + in_ref[k].astype(F32)
    out_ref[...] = total[:6, :D]
    for part in range(3):
        qkv_ref[:, part * D : part * D + 512] = total[:6, 896 + part * 512 : 1408 + part * 512]
        qkv_ref[:, part * D + 512 : (part + 1) * D] = total[:6, 2432 + part * 256 : 2688 + part * 256]
    small_ref[...] = total[:6, D : D + 128] + total[:6, 3200:3328]


def from_blocks(blocks):
    return pl.pallas_call(
        from_blocks_body,
        out_shape=[like(6, 3 * D, dtype=F32), like(6, D, dtype=F32), like(6, 128, dtype=F32)],
        compiler_params=pltpu.CompilerParams(vmem_limit_bytes=16 * MIB),
        cost_estimate=SMALL,
    )(blocks)


def prepare_body(core_ref, *refs):
    sources, (block_ref, mine_ref, other_ref) = refs[:9], refs[9:12]
    held, turned, sems = refs[12:21], refs[21], refs[22]
    loads = begin(sems, 0, *zip(sources, held))
    qkv_ref, out_ref, router_ref, gains_ref, biases_ref, up_t, down_t, up_f, down_f = held
    finish(loads[:5])
    block_ref[...] = jnp.zeros(block_ref.shape, BF)
    block_ref[0:6, : 3 * D] = qkv_ref[...].astype(BF)
    block_ref[0:6, 3 * D : FF] = out_ref[...].astype(BF)
    turned[...] = jnp.zeros((128, 128), F32)
    turned[16:18, 0:6] = gains_ref[...]
    turned[18:20, 0:6] = biases_ref[...]
    vectors = jnp.transpose(turned[...])[0:8]
    turned[0:6, 0:16] = router_ref[...]
    keep = iota((8, 128), 1) < 16
    small = jnp.where(keep, turned[0:8, :], vectors)
    small = jnp.where(iota((8, 128), 0) < 6, small, 0.0)
    block_ref[:, FF:] = small.astype(BF)
    trained = core_ref[0] == 0
    finish(loads[5:])
    for j in range(4):
        cols, rows = slice(j * D, (j + 1) * D), slice(j * 48, (j + 1) * 48)
        low, fixed = up_t[0, :, cols].astype(BF), up_f[0, :, cols]
        mine_ref[rows, :] = jnp.where(trained, low, fixed)
        other_ref[rows, :] = jnp.where(trained, fixed, low)
    low = down_t[0].astype(BF)
    mine_ref[192:, :] = jnp.where(trained, low, down_f[0])
    other_ref[192:, :] = jnp.where(trained, down_f[0], low)


def prepare(core, *arrays):
    anywhere = pl.BlockSpec(memory_space=pl.ANY)
    return pl.pallas_call(
        prepare_body,
        in_specs=[pl.BlockSpec(memory_space=pltpu.SMEM)] + [anywhere] * 9,
        out_shape=[like(8, FF + 128), like(384, D), like(384, D)],
        scratch_shapes=[pltpu.VMEM(array.shape, array.dtype) for array in arrays]
        + [pltpu.VMEM((128, 128), F32), pltpu.SemaphoreType.DMA((9,))],
        compiler_params=pltpu.CompilerParams(vmem_limit_bytes=60 * MIB),
        cost_estimate=SMALL,
    )(core, *arrays)


def pack_body(core_ref, mine_in, got_in, to_ref, sems):
    pairs = []
    for source, core in ((mine_in, core_ref[0]), (got_in, 1 - core_ref[0])):
        for j in range(4):
            rows = pl.ds(j * 96 + core * 48, 48)
            pairs.append((source.at[pl.ds(j * 48, 48), :], to_ref.at[rows, :]))
        pairs.append((source.at[pl.ds(192, 192), :], to_ref.at[pl.ds(384 + core * 192, 192), :]))
    finish(begin(sems, 0, *pairs))


def pack(core, mine, got):
    anywhere = pl.BlockSpec(memory_space=pl.ANY)
    return pl.pallas_call(
        pack_body,
        in_specs=[pl.BlockSpec(memory_space=pltpu.SMEM)] + [anywhere] * 2,
        out_shape=like(D, D),
        scratch_shapes=[pltpu.SemaphoreType.DMA((10,))],
        compiler_params=pltpu.CompilerParams(vmem_limit_bytes=16 * MIB),
        cost_estimate=SMALL,
    )(core, mine, got)


def shift(value, axis, by):
    count = lax.axis_size(axis)
    return lax.ppermute(value, axis, [(i, (i + by) % count) for i in range(count)])


def ordered(mine, other, index):
    first = jnp.where(index == 0, mine, other)
    second = jnp.where(index == 0, other, mine)
    return first, second


FAR = ("x", "yh", "yl")
PEERS = ("c", "z", "yl")


def to_all(rows, names):
    return lax.all_to_all(rows, names, split_axis=0, concat_axis=0, tiled=True)


def spread_x(block):
    return jnp.stack([block] + [shift(block, "x", step) for step in (1, 2, 3)])


def spread_y(along_x):
    near = [along_x] + [shift(along_x, ("yh", "yl"), step) for step in (1, 2, 3)]
    return jnp.stack(near)[:, :, :6].reshape(96, along_x.shape[2])


def natural_rows():
    x, c, z = (lax.axis_index(name) for name in ("x", "c", "z"))
    y = lax.axis_index("yh") * 2 + lax.axis_index("yl")
    row = jnp.arange(768)
    step, other, i = row // 192, (row // 96) % 2, row % 96
    core, deep = (c + other) % 2, (z - step) % 4
    high, long = (y - i // 24) % 4, (x - (i // 6) % 4) % 4
    device = ((long * 2 + high // 2) * 2 + core) * 8 + deep * 2 + high % 2
    return (device * 6 + i % 6).astype(jnp.int32)


def step_of(keep, got, step):
    rows = slice(step * 96, (step + 1) * 96)
    return (keep[rows].astype(F32) + got[rows].astype(F32)).astype(BF)


def along_z(keep, got):
    return [shift(step_of(keep, got, step), "z", -step) for step in (1, 2, 3)]


def take_body(core_ref, *refs):
    sources, (to_ref, *held), sems = refs[1:3], refs[3:6], refs[6]
    rows = held[0].shape[0]

    @pl.when(core_ref[0] == 1)
    def _():
        targets = [to_ref.at[pl.ds(at, rows), :] for at in (0, rows)]
        loads, stores = begin(sems, 0, *zip(sources, held)), []
        for i in range(2):
            finish(loads[i : i + 1])
            stores += begin(sems, 2 + i, (held[i], targets[i]))
        finish(stores)


def take(core, kept, *sent):
    got = [lax.ppermute(part, "c", [(0, 1)]) for part in sent]
    anywhere = pl.BlockSpec(memory_space=pl.ANY)
    return pl.pallas_call(
        take_body,
        in_specs=[pl.BlockSpec(memory_space=pltpu.SMEM)] + [anywhere] * 3,
        out_specs=anywhere,
        out_shape=like(*kept.shape),
        input_output_aliases={1: 0},
        scratch_shapes=[pltpu.VMEM(part.shape, part.dtype) for part in got]
        + [pltpu.SemaphoreType.DMA((4,))],
        compiler_params=pltpu.CompilerParams(vmem_limit_bytes=62 * MIB),
        cost_estimate=SMALL,
    )(core, kept, *got)


def over_y(mine):
    y = lax.axis_index("yh")
    parts = mine.reshape(2, mine.shape[0] // 2, mine.shape[1])
    kept, sent = (lax.dynamic_index_in_dim(parts, at, 0, False) for at in (y, 1 - y))
    return kept.astype(F32) + shift(sent, "yh", 1).astype(F32)


def owned(mine, axis):
    return lax.psum_scatter(mine, axis, scatter_dimension=0, tiled=True)


def shards(
    tokens,
    seq_lengths,
    key_mask,
    routes,
    cotangent,
    qkv_weight,
    out_weight,
    router_weight,
    norm_gains,
    norm_biases,
    up_train,
    down_train,
    up_frozen,
    down_frozen,
):
    core = lax.axis_index("c")

    place = jnp.stack([lax.axis_index(name) for name in ("x", "yh", "yl")]).astype(jnp.int32)

    block, mine, other = prepare(
        core.reshape(1), qkv_weight, out_weight, router_weight, norm_gains, norm_biases, up_train,
        down_train, up_frozen, down_frozen,
    )
    other = shift(other, "c", 1)
    block, routes, other = lax.optimization_barrier((block, routes, other))
    along_x = spread_x(block)

    both = pack(core.reshape(1), mine, other)
    along_x, both = lax.optimization_barrier((along_x, both))
    rows = spread_y(along_x)
    nat = natural_rows().reshape(1, D)
    g_slots, sid, sidt = route(routes, cotangent)
    near = lax.all_gather(both, "x", tiled=True)

    rows, g_slots, both = lax.optimization_barrier((rows, g_slots, both))
    parts = [rows] + [shift(rows, "z", step) for step in (1, 2, 3)]
    both = shift(both, "yh", 1)
    parts, both, g_slots = lax.optimization_barrier((parts, both, g_slots))
    pieces = []
    for part in parts:
        pieces += [part, shift(part, "c", 1)]
    far = lax.all_gather(both, "x", tiled=True)

    g_rows = to_all(g_slots.reshape(16, CAP, D), PEERS)
    w, h1p, qkv, probs, attnp, x_mid, h2, turn, gate, vec, router, sent = forward(
        seq_lengths[0], nat, key_mask.reshape(1, ROW), tokens, sid, sidt, pieces
    )
    sent, g_rows = lax.optimization_barrier((sent, g_rows))

    arrived = to_all(sent, PEERS)
    out, back, x_rows, d_out, act, d_up = experts(
        place, arrived, g_rows, near, far
    )
    d_back = to_all(back, PEERS)
    up_all = take(core.reshape(1), *up_grad(x_rows, d_up))
    down_parts = down_grad(d_out, act)
    d_back, out, up_all, down_parts = lax.optimization_barrier((d_back, out, up_all, down_parts))

    returned = to_all(out, PEERS)
    up_all, down_all = owned(up_all, "x"), take(core.reshape(1), *down_parts)
    d_x_mid, d_attn, first, keep, away = back_one(
        sid, gate, router, vec, d_back, x_mid, cotangent, w, attnp, h2, probs, qkv, h1p, turn
    )
    input_grad, *last = back_two(vec, d_attn, probs, qkv, h1p, first, w, tokens, d_x_mid, turn)
    got = shift(away, "c", 1)
    keep, got, returned, down_all = lax.optimization_barrier((keep, got, returned, down_all))
    down_all = owned(down_all, "x")
    one, two, three = (step_of(keep, got, step) for step in (1, 2, 3))
    one, three = shift(one, "z", -1), shift(three, "z", -3)
    two = [shift(half, "z", -2) for half in (two[:, :1280], two[:, 1280:])]
    one, three, two[0], last, up_all = lax.optimization_barrier((one, three, two[0], last, up_all))
    groups = [(0, keep), (0, got), (0, one), (0, three), (0, two[0]), (1280, two[1])]
    up_all = over_y(up_all)
    keep, got = last[0], shift(last[1], "c", 1)
    groups += [(2432, part) for part in (keep, got, *along_z(keep, got))]
    offsets, parts = zip(*groups)
    parts, down_all, up_all = lax.optimization_barrier((parts, down_all, up_all))
    down_all = owned(down_all, "yh")
    blocks = to_blocks(place, list(zip(offsets, parts)))
    blocks, returned = lax.optimization_barrier((blocks, returned))
    grad_down = down_all.astype(F32)[None]
    blocks, grad_down = lax.optimization_barrier((to_all(blocks, FAR), grad_down))
    own_qkv, own_out, small = from_blocks(blocks)
    grad_up = up_all.astype(F32)[None]
    block_out = merge(sid, returned.reshape(16 * CAP, D), gate, x_mid)
    return (
        block_out,
        input_grad,
        own_qkv,
        own_out,
        small[:, :16],
        small[:, 16:18].T,
        small[:, 18:20].T,
        grad_up,
        grad_down,
    )


def solution(mesh):
    fine = Mesh(mesh.devices.reshape(SIZES), NAMES)
    by_row = P(NAMES, None)
    by_column = P(None, NAMES)
    by_expert = P(NARROW, WIDE, None)
    return jax.shard_map(
        shards,
        mesh=fine,
        in_specs=(by_row, by_row, P(NAMES)) + (by_row,) * 5 + (by_column,) * 2 + (by_expert,) * 4,
        out_specs=(by_row,) * 5 + (by_column,) * 2 + (by_expert,) * 2,
        check_vma=False,
    )
```

```python
import functools

import jax
import jax.numpy as jnp
from jax import lax
from jax.experimental import pallas as pl
from jax.experimental.pallas import tpu as pltpu
from jax.sharding import Mesh
from jax.sharding import PartitionSpec as P

SIZES = (4, 2, 2, 4, 2)
NAMES = ("x", "yh", "c", "z", "yl")
WIDE = ("x", "yh", "c")
NARROW = ("z", "yl")
BF = jnp.bfloat16
F32 = jnp.float32
ROW = 512
D = 768
FF = 3072
CAP = 96
LINE = 592
SOURCES = 4
GELU_ONE = 0.7978845608028654
GELU_CUBE = GELU_ONE * 0.044715
MIB = 1024 * 1024
SMALL = pl.CostEstimate(flops=10**6, bytes_accessed=10**4, transcendentals=0)


def nn(a, b):
    return jnp.dot(a, b, preferred_element_type=F32)


def nt(a, b):
    return lax.dot_general(a, b, (((1,), (1,)), ((), ())), preferred_element_type=F32)


def tn(a, b):
    return lax.dot_general(a, b, (((0,), (0,)), ((), ())), preferred_element_type=F32)


def iota(shape, dim):
    return lax.broadcasted_iota(jnp.int32, shape, dim)


def hot(mask):
    return jnp.where(mask, 1.0, 0.0).astype(BF)


def like(*dims, dtype=BF):
    return jax.ShapeDtypeStruct(dims, dtype)


def tail_of(line):
    high = line.astype(BF).astype(F32)
    row = iota((16, 128), 0)
    return jnp.where(row == 0, high, jnp.where(row == 1, line - high, 0.0)).astype(BF)


def line_of(tail):
    tail = tail.astype(F32)
    return tail[0:1] + tail[1:2]


def begin(sems, first, *pairs):
    copies = [
        pltpu.make_async_copy(source, target, sems.at[first + i])
        for i, (source, target) in enumerate(pairs)
    ]
    for copy in copies:
        copy.start()
    return copies


def finish(copies):
    for copy in copies:
        copy.wait()


def norm(x):
    centered = x - jnp.mean(x, -1, keepdims=True)
    scale = lax.rsqrt(jnp.mean(centered * centered, -1, keepdims=True) + 1e-5)
    return centered * scale, scale


def norm_back(d_out, x_hat, scale, gain):
    t = d_out * gain
    d_in = scale * (
        t - jnp.mean(t, -1, keepdims=True) - x_hat * jnp.mean(t * x_hat, -1, keepdims=True)
    )
    return d_in, jnp.sum(d_out * x_hat, 0, keepdims=True), jnp.sum(d_out, 0, keepdims=True)


def route_body(routes_ref, cot_ref, g_ref, sid_ref, sidt_ref):
    lane = iota((ROW, 128), 1)
    r0, r1 = routes_ref[:, 0:1], routes_ref[:, 1:2]
    either = hot((lane == r0) | (lane == r1))
    earlier = nn(hot(iota((ROW, ROW), 1) < iota((ROW, ROW), 0)), either)
    p0 = jnp.sum(jnp.where(lane == r0, earlier, 0.0), 1, keepdims=True).astype(jnp.int32)
    p1 = jnp.sum(jnp.where(lane == r1, earlier, 0.0), 1, keepdims=True).astype(jnp.int32)
    columns = (
        jnp.where(p0 < CAP, r0 * CAP + p0, -1),
        jnp.where(p1 < CAP, r1 * CAP + p1, -1),
        r0,
    )
    table = jnp.broadcast_to(r1, (ROW, 128))
    for at, column in enumerate(columns):
        table = jnp.where(lane == at, column, table)
    sid_ref[...] = table
    turned = jnp.transpose(table.astype(F32))[0:8].astype(jnp.int32)
    sidt_ref[...] = turned
    for part in range(4):
        slot = iota((4 * CAP, ROW), 0) + part * 4 * CAP
        pick = hot((slot == turned[0:1]) | (slot == turned[1:2]))
        g_ref[part * 4 * CAP : (part + 1) * 4 * CAP, :] = nn(pick, cot_ref[...]).astype(BF)


def route(routes, cotangent):
    return pl.pallas_call(
        route_body,
        out_shape=[like(16 * CAP, D), like(ROW, 128, dtype=jnp.int32), like(8, ROW, dtype=jnp.int32)],
        compiler_params=pltpu.CompilerParams(vmem_limit_bytes=32 * MIB),
        cost_estimate=SMALL,
    )(routes, cotangent)


def forward_body(*refs):
    lens_ref, nat_ref, mask_ref, tok_ref, sid_ref, sidt_ref = refs[:6]
    pieces, refs = refs[6:14], refs[14:]
    w_out, h1p_out, qkv_out, probs_out, attnp_out, xmid_out, h2_out, back_out = refs[:8]
    gate_ref, vec_ref, router_ref, sent_ref = refs[8:12]
    w_ref, rest_ref, h1p_ref, qkv_ref, probs_ref, attn, attnp_ref, xmid_ref, h2_ref = refs[12:21]
    back_ref, bias, nat_w, sems = refs[21:]
    rows = [pl.ds(at * 96, 96) for at in range(8)]
    small = [(piece.at[:, FF:], rest_ref.at[to, :]) for piece, to in zip(pieces, rows)]
    large = [(piece.at[:, :FF], w_ref.at[to, :]) for piece, to in zip(pieces, rows)]
    small, large = begin(sems, 0, *small), begin(sems, 8, *large)
    turn = hot(iota((D, D), 0) == nat_ref[...])
    x = tok_ref[...].astype(F32)
    x_hat = norm(x)[0]
    finish(small)
    rest = nn(turn, rest_ref[...])
    vectors = jnp.transpose(rest)[16:24]
    router_ref[...] = rest.astype(BF)
    vec_ref[...] = vectors
    h1 = (x_hat * vectors[0:1] + vectors[2:3]).astype(BF)
    h1p_ref[...] = nn(h1, turn).astype(BF)
    back_ref[...] = jnp.transpose(turn)
    finish(large)
    for part in range(4):
        cols = slice(part * D, (part + 1) * D)
        nat_w[:, cols] = nn(turn, w_ref[:, cols]).astype(BF)
        if part < 3:
            qkv_ref[:, cols] = nn(h1, nat_w[:, cols]).astype(BF)
    away = begin(
        sems, 0, (nat_w, w_out), (h1p_ref, h1p_out), (qkv_ref, qkv_out), (back_ref, back_out)
    )

    end_one = lens_ref[0]
    end_two = end_one + lens_ref[1]

    def segment(place):
        return (place >= end_one).astype(jnp.int32) + (place >= end_two).astype(jnp.int32)

    query, key = iota((ROW, ROW), 0), iota((ROW, ROW), 1)
    same = segment(iota((ROW, 1), 0)) == segment(iota((1, ROW), 1))
    allowed = same & (key <= query) & ((mask_ref[...] == 1) | (key == query))
    bias[...] = jnp.where(allowed, 0.0, -1e30)
    low = iota((1, 128), 1) < 64
    half = ROW // 2
    zero = jnp.zeros((), BF)

    def pair(index, carry):
        at = pl.multiple_of(index * 128, 128)
        q = qkv_ref[:, pl.ds(at, 128)] * jnp.asarray(0.125, BF)
        k = qkv_ref[:, pl.ds(D + at, 128)]
        v = qkv_ref[:, pl.ds(2 * D + at, 128)]
        out = [None, None]
        for head in range(2):
            mine = low if head == 0 else jnp.logical_not(low)
            k_mine, v_mine = jnp.where(mine, k, zero), jnp.where(mine, v, zero)
            for block in range(2):
                count, rows = half * (block + 1), slice(block * half, (block + 1) * half)
                scores = nt(q[rows], k_mine[:count]) + bias[rows, :count]
                e = jnp.exp(scores - jnp.max(scores, 1, keepdims=True))
                probs = (e * (1.0 / jnp.sum(e, 1, keepdims=True))).astype(BF)
                probs_ref[2 * index + head, rows, :count] = probs
                if block == 0:
                    probs_ref[2 * index + head, rows, count:] = jnp.zeros((half, half), BF)
                term = nn(probs, v_mine[:count])
                out[block] = term if head == 0 else out[block] + term
        for block in range(2):
            attn[block * half : (block + 1) * half, pl.ds(at, 128)] = out[block].astype(BF)
        heads = pl.ds(2 * index, 2)
        begin(sems, 8 + index, (probs_ref.at[heads], probs_out.at[heads]))
        return carry

    lax.fori_loop(0, 6, pair, 0)
    for index in range(6):
        heads = pl.ds(2 * index, 2)
        away.append(
            pltpu.make_async_copy(probs_ref.at[heads], probs_out.at[heads], sems.at[8 + index])
        )
    attnp_ref[...] = nn(attn[...], turn).astype(BF)
    x_mid = x + nn(attn[...], nat_w[:, 3 * D :])
    xmid_ref[...] = x_mid
    h2 = (norm(x_mid)[0] * vectors[1:2] + vectors[3:4]).astype(BF)
    h2_ref[...] = h2
    away += begin(sems, 4, (attnp_ref, attnp_out), (xmid_ref, xmid_out), (h2_ref, h2_out))
    logits = nn(h2, router_ref[...])
    lane = iota((ROW, 128), 1)
    s0, s1, r0, r1 = (sid_ref[:, at : at + 1] for at in range(4))
    c0 = jnp.sum(jnp.where(lane == r0, logits, 0.0), 1, keepdims=True)
    c1 = jnp.sum(jnp.where(lane == r1, logits, 0.0), 1, keepdims=True)
    g0, g1 = 1.0 / (1.0 + jnp.exp(c1 - c0)), 1.0 / (1.0 + jnp.exp(c0 - c1))
    gate_ref[...] = jnp.where(lane == 0, g0, jnp.where(lane == 1, g1, 0.0))
    for part in range(4):
        slot = iota((4 * CAP, ROW), 0) + part * 4 * CAP
        pick = hot((slot == sidt_ref[0:1]) | (slot == sidt_ref[1:2]))
        rows = nn(pick, h2_ref[...]).astype(BF)
        for i in range(4):
            for j in range(6):
                block = rows[i * CAP : (i + 1) * CAP, j * 128 : (j + 1) * 128]
                sent_ref[4 * part + i, j * CAP : (j + 1) * CAP, :] = block
    for expert in range(16):
        slot = lane + expert * CAP
        line = jnp.sum(
            jnp.where(slot == s0, g0, 0.0) + jnp.where(slot == s1, g1, 0.0), 0, keepdims=True
        )
        sent_ref[expert, 6 * CAP : LINE, :] = tail_of(line)
    finish(away)


def forward(lens, nat, mask, tokens, sid, sidt, pieces):
    vmem = pl.BlockSpec(memory_space=pltpu.VMEM)
    anywhere = pl.BlockSpec(memory_space=pl.ANY)
    moved = [
        like(D, FF),
        like(ROW, D),
        like(ROW, 3 * D),
        like(12, ROW, ROW),
        like(ROW, D),
        like(ROW, D, dtype=F32),
        like(ROW, D),
        like(D, D),
    ]
    held = [like(ROW, 128, dtype=F32), like(8, D, dtype=F32), like(D, 128), like(16, LINE, 128)]
    buffers = [like(D, FF), like(D, 128), *moved[1:4], like(ROW, D), *moved[4:]]
    return pl.pallas_call(
        forward_body,
        in_specs=[pl.BlockSpec(memory_space=pltpu.SMEM)] + [vmem] * 5 + [anywhere] * 8,
        out_specs=[anywhere] * 8 + [vmem] * 4,
        out_shape=moved + held,
        scratch_shapes=[pltpu.VMEM(b.shape, b.dtype) for b in buffers]
        + [pltpu.VMEM((ROW, ROW), F32), pltpu.VMEM((D, FF), BF), pltpu.SemaphoreType.DMA((16,))],
        compiler_params=pltpu.CompilerParams(vmem_limit_bytes=62 * MIB),
        cost_estimate=SMALL,
    )(lens, nat, mask, tokens, sid, sidt, *pieces)


def expert_body(
    place_ref, sent_ref, g_ref, near_in, far_in, out_ref, back_ref, x_ref, dout_ref, act_ref,
    dup_ref, up_ref, down_ref, sems,
):
    def loads():
        for source, y in ((near_in, place_ref[1]), (far_in, 1 - place_ref[1])):
            for x in range(4):
                block = 2 * x + y
                for j in range(4):
                    rows, cols = pl.ds(block * 96, 96), pl.ds(j * D, D)
                    yield source.at[pl.ds(x * D + j * 96, 96), :], up_ref.at[rows, cols]
                rows = pl.ds(block * 384, 384)
                yield source.at[pl.ds(x * D + 384, 384), :], down_ref.at[rows, :]

    @pl.when(pl.program_id(0) == 0)
    def _():
        copies = [
            pltpu.make_async_copy(source, target, sems.at[i])
            for i, (source, target) in enumerate(loads())
        ]
        for copy in copies:
            copy.start()
        for copy in copies:
            copy.wait()

    for s in range(SOURCES):
        first, last = s * CAP, (s + 1) * CAP
        for j in range(6):
            x_ref[first:last, j * 128 : (j + 1) * 128] = sent_ref[s, j * CAP : (j + 1) * CAP, :]
        gate = line_of(sent_ref[s, 6 * CAP : LINE, :])
        column = jnp.transpose(jnp.broadcast_to(gate, (128, 128)))[:CAP, :1]
        dout_ref[first:last, :] = (g_ref[s].astype(F32) * column).astype(BF)
    x, d_out = x_ref[...], dout_ref[...]
    for part in range(FF // 256):
        cols = slice(part * 256, (part + 1) * 256)
        up = nn(x, up_ref[:, cols])
        d_act = nt(d_out, down_ref[cols, :])
        square = up * up
        t = jnp.tanh(up * (GELU_ONE + GELU_CUBE * square))
        a = 0.5 + 0.5 * t
        act_ref[:, cols] = (up * a).astype(BF)
        slope = a + (up * (1.0 - t * t)) * (0.5 * GELU_ONE + 1.5 * GELU_CUBE * square)
        dup_ref[:, cols] = (d_act * slope).astype(BF)
    out = nn(act_ref[...], down_ref[...]).astype(BF)
    back = nt(dup_ref[...], up_ref[...]).astype(BF)
    for s in range(SOURCES):
        out_ref[s] = out[s * CAP : (s + 1) * CAP]
        for j in range(6):
            block = back[s * CAP : (s + 1) * CAP, j * 128 : (j + 1) * 128]
            back_ref[s, j * CAP : (j + 1) * CAP, :] = block
    for s in range(SOURCES):
        d_gate = jnp.sum(out_ref[s].astype(F32) * g_ref[s].astype(F32), -1, keepdims=True)
        d_gate = jnp.broadcast_to(d_gate, (CAP, 128))
        wide = jnp.concatenate([d_gate, jnp.zeros((128 - CAP, 128), F32)], 0)
        back_ref[s, 6 * CAP : LINE, :] = tail_of(jnp.transpose(wide)[0:1])


def experts(place, sent, g, near, far):
    rows = SOURCES * CAP
    anywhere = pl.BlockSpec(memory_space=pl.ANY)
    by_source = pl.BlockSpec((SOURCES, CAP, D), lambda i: (i, 0, 0))
    message = pl.BlockSpec((SOURCES, LINE, 128), lambda i: (i, 0, 0))
    by_rows = lambda width: pl.BlockSpec((rows, width), lambda i: (i, 0))
    return pl.pallas_call(
        expert_body,
        grid=(16 // SOURCES,),
        in_specs=[
            pl.BlockSpec(memory_space=pltpu.SMEM),
            message,
            by_source,
        ]
        + [anywhere] * 2,
        out_specs=[
            by_source, message, by_rows(D), by_rows(D), by_rows(FF), by_rows(FF),
        ],
        out_shape=[
            like(16, CAP, D),
            like(16, LINE, 128),
            like(16 * CAP, D),
            like(16 * CAP, D),
            like(16 * CAP, FF),
            like(16 * CAP, FF),
        ],
        scratch_shapes=[
            pltpu.VMEM((D, FF), BF),
            pltpu.VMEM((FF, D), BF),
            pltpu.SemaphoreType.DMA((40,)),
        ],
        compiler_params=pltpu.CompilerParams(vmem_limit_bytes=62 * MIB),
        cost_estimate=SMALL,
    )(place, sent, g, near, far)


def up_grad_body(x_ref, dup_ref, keep_ref, first_ref, last_ref):
    grad = tn(x_ref[...], dup_ref[...]).astype(BF)
    for block in range(8):
        rows, low = block * 96, (block % 4) * 48
        keep_ref[block * 48 : (block + 1) * 48, :] = grad[rows : rows + 48]
        away_ref = (first_ref, last_ref)[block // 4]
        away_ref[low : low + 48, :] = grad[rows + 48 : rows + 96]


def up_grad(x, d_up):
    columns = lambda rows: pl.BlockSpec((rows, D), lambda i: (0, i))
    return pl.pallas_call(
        up_grad_body,
        grid=(4,),
        in_specs=[pl.BlockSpec((16 * CAP, D), lambda i: (0, 0)), columns(16 * CAP)],
        out_specs=[columns(384), columns(192), columns(192)],
        out_shape=[like(384, FF), like(192, FF), like(192, FF)],
        compiler_params=pltpu.CompilerParams(vmem_limit_bytes=60 * MIB),
        cost_estimate=SMALL,
    )(x, d_up)


def down_grad_body(dout_ref, act_ref, keep_ref, first_ref, last_ref):
    grad = tn(act_ref[...], dout_ref[...]).astype(BF)
    for block in range(2):
        keep_ref[block * 192 : (block + 1) * 192, :] = grad[block * 384 : block * 384 + 192]
    away = jnp.concatenate([grad[192:384], grad[576:768]], 0)
    for part, away_ref in enumerate((first_ref, last_ref)):

        @pl.when(pl.program_id(0) // 2 == part)
        def _():
            away_ref[...] = away


def down_grad(d_out, act):
    rows = lambda index: pl.BlockSpec((384, D), index)
    return pl.pallas_call(
        down_grad_body,
        grid=(4,),
        in_specs=[
            pl.BlockSpec((16 * CAP, D), lambda i: (0, 0)),
            pl.BlockSpec((16 * CAP, D), lambda i: (0, i)),
        ],
        out_specs=[
            rows(lambda i: (i, 0)),
            rows(lambda i: (jnp.minimum(i, 1), 0)),
            rows(lambda i: (jnp.maximum(i - 2, 0), 0)),
        ],
        out_shape=[like(1536, D), like(768, D), like(768, D)],
        compiler_params=pltpu.CompilerParams(vmem_limit_bytes=60 * MIB),
        cost_estimate=SMALL,
    )(d_out, act)


def put_rows(keep_ref, away_ref, cols, values):
    for step in range(4):
        rows = slice(step * 96, (step + 1) * 96)
        keep_ref[rows, cols] = values[step * 192 : step * 192 + 96]
        away_ref[rows, cols] = values[step * 192 + 96 : (step + 1) * 192]


def attention_back(base, pairs, dattn_ref, probs_ref, qkv_ref, d_qkv):
    width = 128 * pairs
    low = iota((1, 128), 1) < 64
    zero = jnp.zeros((), BF)
    half = ROW // 2

    def add(terms, at, term):
        terms[at] = term if terms[at] is None else terms[at] + term

    def pair(index, carry):
        at = pl.multiple_of((base + index) * 128, 128)
        to = pl.multiple_of(index * 128, 128)
        q, k, v = (qkv_ref[:, pl.ds(part * D + at, 128)] for part in range(3))
        d_attn = dattn_ref[:, pl.ds(at, 128)]
        dq, dk, dv = [None, None], [None, None], [None, None]
        for head in range(2):
            mine = low if head == 0 else jnp.logical_not(low)
            q_mine, k_mine, v_mine, d_mine = (jnp.where(mine, t, zero) for t in (q, k, v, d_attn))
            for block in range(2):
                count, rows = half * (block + 1), slice(block * half, (block + 1) * half)
                probs = probs_ref[2 * index + head, rows, :count]
                d_probs = nt(d_mine[rows], v_mine[:count])
                wide = probs.astype(F32)
                weighted = wide * d_probs
                delta = jnp.sum(weighted, 1, keepdims=True)
                d_scores = (weighted - wide * delta).astype(BF)
                add(dq, block, nn(d_scores, k_mine[:count]))
                for other in range(block + 1):
                    keys = slice(other * half, (other + 1) * half)
                    add(dk, other, tn(d_scores[:, keys], q_mine[rows]))
                    add(dv, other, tn(probs[:, keys], d_mine[rows]))
        for block in range(2):
            rows = slice(block * half, (block + 1) * half)
            d_qkv[rows, pl.ds(to, 128)] = (dq[block] * 0.125).astype(BF)
            d_qkv[rows, pl.ds(width + to, 128)] = (dk[block] * 0.125).astype(BF)
            d_qkv[rows, pl.ds(2 * width + to, 128)] = dv[block].astype(BF)
        return carry

    lax.fori_loop(0, pairs, pair, 0, unroll=2)


def back_one_body(
    sid_ref, gate_ref, router_ref, vec_ref, dback_in, xmid_in, cot_in, w_in, attnp_in,
    h2_in, probs_in, qkv_in, h1p_in, turn_in, dxm_out, dattn_out, dqkv_out, keep_out, away_out,
    dback_ref, xmid_ref, cot_ref, w_ref, attnp_ref, h2_ref, probs_ref, qkv_ref, h1p_ref, turn_ref, dxm_ref,
    dattn_ref, dqkv_ref, keep_ref, away_ref, slots_ref, columns_ref, sems,
):
    sources = (
        dback_in, xmid_in, cot_in, w_in.at[:, 3 * D :], attnp_in, h2_in, turn_in, qkv_in, probs_in.at[:8],
        h1p_in,
    )
    targets = (
        dback_ref, xmid_ref, cot_ref, w_ref, attnp_ref, h2_ref, turn_ref, qkv_ref, probs_ref, h1p_ref,
    )
    pairs = list(zip(sources, targets))
    loads = begin(sems, 0, *pairs[:1])
    lane = iota((ROW, 128), 1)
    s0, s1, r0, r1 = (sid_ref[:, at : at + 1] for at in range(4))
    finish(loads)
    loads += begin(sems, 1, *pairs[1:])
    dg0 = dg1 = jnp.zeros((ROW, 128), F32)
    d_h2 = jnp.zeros((ROW, D), F32)
    columns_ref[...] = jnp.zeros((4 * CAP, 128), BF)
    for part in range(4):
        for i in range(4):
            message = dback_ref.at[4 * part + i]
            for j in range(6):
                block = message[j * CAP : (j + 1) * CAP, :]
                slots_ref[i * CAP : (i + 1) * CAP, j * 128 : (j + 1) * 128] = block
            terms = jnp.transpose(message[6 * CAP : LINE, :].astype(F32))
            columns_ref[i * CAP : (i + 1) * CAP, 0:16] = terms[:CAP].astype(BF)
        slot = iota((ROW, 4 * CAP), 1) + part * 4 * CAP
        first, second = hot(slot == s0), hot(slot == s1)
        dg0 = dg0 + nn(first, columns_ref[...])
        dg1 = dg1 + nn(second, columns_ref[...])
        d_h2 = d_h2 + nn(first + second, slots_ref[...])
    dg0, dg1 = dg0[:, 0:1] + dg0[:, 1:2], dg1[:, 0:1] + dg1[:, 1:2]
    g0, g1 = gate_ref[:, 0:1], gate_ref[:, 1:2]
    both = g0 * dg0 + g1 * dg1
    d_logits = jnp.where(lane == r0, g0 * (dg0 - both), 0.0)
    d_logits = d_logits + jnp.where(lane == r1, g1 * (dg1 - both), 0.0)
    high = d_logits.astype(BF)
    low = (d_logits - high.astype(F32)).astype(BF)
    d_h2 = d_h2 + nt(high, router_ref[...]) + nt(low, router_ref[...])
    finish(loads[1:3])
    x_hat, scale = norm(xmid_ref[...])
    d_in, d_gain, d_bias = norm_back(d_h2, x_hat, scale, vec_ref[1:2])
    d_x_mid = cot_ref[...].astype(F32) + d_in
    dxm_ref[...] = d_x_mid
    d_proj = d_x_mid.astype(BF)
    finish(loads[3:7])
    dattn_ref[...] = nt(d_proj, w_ref[...]).astype(BF)
    leaving = begin(sems, 10, (dxm_ref, dxm_out), (dattn_ref, dattn_out))
    put_rows(keep_ref, away_ref, slice(0, D), tn(attnp_ref[...], d_proj).astype(BF))
    d_router = tn(h2_ref[...], jnp.concatenate([high, low], 1))
    d_router = d_router[:, :128] + d_router[:, 128:]
    sub = iota((128, D), 0)
    rows = jnp.where(sub == 17, d_gain, 0.0) + jnp.where(sub == 19, d_bias, 0.0)
    small = d_router + jnp.transpose(rows)
    put_rows(keep_ref, away_ref, slice(D, D + 128), nn(turn_ref[...], small.astype(BF)).astype(BF))
    cols = slice(0, D + 128)
    leaving += begin(
        sems, 12, (keep_ref.at[:, cols], keep_out.at[:, cols]), (away_ref.at[:, cols], away_out.at[:, cols])
    )
    finish(loads[7:9])
    attention_back(0, 4, dattn_ref, probs_ref, qkv_ref, dqkv_ref)
    leaving += begin(sems, 14, (dqkv_ref, dqkv_out))
    finish(loads[9:])
    for part in range(3):
        cols = slice(D + 128 + part * 512, D + 128 + (part + 1) * 512)
        grad = tn(h1p_ref[...], dqkv_ref[:, part * 512 : (part + 1) * 512]).astype(BF)
        put_rows(keep_ref, away_ref, cols, grad)
        leaving += begin(
            sems,
            15 + 2 * part,
            (keep_ref.at[:, cols], keep_out.at[:, cols]),
            (away_ref.at[:, cols], away_out.at[:, cols]),
        )
    finish(leaving)


def back_one(
    sid, gate, router, vec, d_back, x_mid, cotangent, w, attnp, h2, probs, qkv, h1p, turn
):
    vmem = pl.BlockSpec(memory_space=pltpu.VMEM)
    anywhere = pl.BlockSpec(memory_space=pl.ANY)
    ins = [
        like(16, LINE, 128), like(ROW, D, dtype=F32), like(ROW, D), like(D, D), like(ROW, D),
        like(ROW, D), like(8, ROW, ROW), like(ROW, 3 * D), like(ROW, D), like(D, D),
    ]
    outs = [
        like(ROW, D, dtype=F32), like(ROW, D), like(ROW, 1536), like(384, 2432), like(384, 2432),
    ]
    return pl.pallas_call(
        back_one_body,
        in_specs=[vmem] * 4 + [anywhere] * 10,
        out_specs=[anywhere] * 5,
        out_shape=outs,
        scratch_shapes=[pltpu.VMEM(b.shape, b.dtype) for b in ins + outs]
        + [pltpu.VMEM((4 * CAP, D), BF), pltpu.VMEM((4 * CAP, 128), BF)]
        + [pltpu.SemaphoreType.DMA((21,))],
        compiler_params=pltpu.CompilerParams(vmem_limit_bytes=62 * MIB),
        cost_estimate=SMALL,
    )(sid, gate, router, vec, d_back, x_mid, cotangent, w, attnp, h2, probs, qkv, h1p, turn)


def back_two_body(
    vec_ref, dattn_in, probs_in, qkv_in, h1p_in, first_in, w_in, tok_in, dxm_in, turn_in,
    gx_out, keep_out, away_out, dattn_ref, probs_ref, qkv_ref, h1p_ref, first_ref, w_ref, tok_ref,
    dxm_ref, turn_ref, gx_ref, keep_ref, away_ref, second_ref, sems,
):
    sources = (
        dattn_in, qkv_in, probs_in.at[8:], h1p_in, first_in, w_in.at[:, : 3 * D], tok_in, dxm_in,
        turn_in,
    )
    targets = (dattn_ref, qkv_ref, probs_ref, h1p_ref, first_ref, w_ref, tok_ref, dxm_ref, turn_ref)
    pairs = list(zip(sources, targets))
    loads = begin(sems, 0, *pairs[:3])
    finish(loads)
    loads += begin(sems, 3, *pairs[3:])
    attention_back(4, 2, dattn_ref, probs_ref, qkv_ref, second_ref)
    finish(loads[3:6])
    d_h1 = jnp.zeros((ROW, D), F32)
    for part in range(3):
        middle = part * D + 512
        d_second = second_ref[:, part * 256 : (part + 1) * 256]
        grad = tn(h1p_ref[...], d_second).astype(BF)
        put_rows(keep_ref, away_ref, slice(part * 256, (part + 1) * 256), grad)
        d_h1 = d_h1 + nt(first_ref[:, part * 512 : (part + 1) * 512], w_ref[:, part * D : middle])
        d_h1 = d_h1 + nt(d_second, w_ref[:, middle : (part + 1) * D])
    cols = slice(0, D)
    leaving = begin(
        sems, 9, (keep_ref.at[:, cols], keep_out.at[:, cols]), (away_ref.at[:, cols], away_out.at[:, cols])
    )
    finish(loads[6:])
    x_hat, scale = norm(tok_ref[...].astype(F32))
    d_in, d_gain, d_bias = norm_back(d_h1, x_hat, scale, vec_ref[0:1])
    gx_ref[...] = dxm_ref[...] + d_in
    leaving += begin(sems, 11, (gx_ref, gx_out))
    sub = iota((128, D), 0)
    rows = jnp.where(sub == 16, d_gain, 0.0) + jnp.where(sub == 18, d_bias, 0.0)
    small = nn(turn_ref[...], jnp.transpose(rows).astype(BF)).astype(BF)
    cols = slice(D, D + 128)
    put_rows(keep_ref, away_ref, cols, small)
    leaving += begin(
        sems, 12, (keep_ref.at[:, cols], keep_out.at[:, cols]), (away_ref.at[:, cols], away_out.at[:, cols])
    )
    finish(leaving)


def back_two(vec, d_attn, probs, qkv, h1p, first, w, tokens, d_x_mid, turn):
    vmem = pl.BlockSpec(memory_space=pltpu.VMEM)
    anywhere = pl.BlockSpec(memory_space=pl.ANY)
    ins = [
        like(ROW, D), like(4, ROW, ROW), like(ROW, 3 * D), like(ROW, D), like(ROW, 1536),
        like(D, 3 * D), like(ROW, D), like(ROW, D, dtype=F32), like(D, D),
    ]
    outs = [like(ROW, D, dtype=F32), like(384, 896), like(384, 896)]
    return pl.pallas_call(
        back_two_body,
        in_specs=[vmem] + [anywhere] * 9,
        out_specs=[anywhere] * 3,
        out_shape=outs,
        scratch_shapes=[pltpu.VMEM(b.shape, b.dtype) for b in ins + outs]
        + [pltpu.VMEM((ROW, D), BF), pltpu.SemaphoreType.DMA((14,))],
        compiler_params=pltpu.CompilerParams(vmem_limit_bytes=62 * MIB),
        cost_estimate=SMALL,
    )(vec, d_attn, probs, qkv, h1p, first, w, tokens, d_x_mid, turn)


def merge_body(sid_ref, ret_ref, gate_ref, xmid_ref, out_ref):
    s0, s1 = sid_ref[:, 0:1], sid_ref[:, 1:2]
    y0 = y1 = jnp.zeros((ROW, D), F32)
    for part in range(4):
        slot = iota((ROW, 4 * CAP), 1) + part * 4 * CAP
        values = ret_ref[part * 4 * CAP : (part + 1) * 4 * CAP, :]
        y0 = y0 + nn(hot(slot == s0), values)
        y1 = y1 + nn(hot(slot == s1), values)
    out_ref[...] = (xmid_ref[...] + (gate_ref[:, 0:1] * y0 + gate_ref[:, 1:2] * y1)).astype(BF)


def merge(sid, returned, gate, x_mid):
    return pl.pallas_call(
        merge_body,
        out_shape=like(ROW, D),
        compiler_params=pltpu.CompilerParams(vmem_limit_bytes=40 * MIB),
        cost_estimate=SMALL,
    )(sid, returned, gate, x_mid)


def to_blocks_body(offsets, place_ref, *refs):
    count = len(offsets)
    held = refs[count + 1 : 2 * count + 1]
    out_ref, total, sems = refs[count], refs[-2], refs[-1]
    sources = [ref.at[pl.ds(0, 96), :] for ref in refs[:count]]
    loads = begin(sems, 0, *zip(sources, held))
    total[...] = jnp.zeros(total.shape, F32)
    for load, part, offset in zip(loads, held, offsets):
        finish([load])
        total[0:96, offset : offset + part.shape[1]] += part[...].astype(F32)
    x, y = place_ref[0], 2 * place_ref[1] + place_ref[2]
    for k in range(16):
        to = lax.rem(x - k % 4 + 4, 4) * 4 + lax.rem(y - k // 4 + 4, 4)
        out_ref[to] = total[6 * k : 6 * k + 8, :].astype(BF)


def to_blocks(place, groups):
    offsets, parts = zip(*groups)
    width = max(offset + part.shape[1] for offset, part in groups)
    return pl.pallas_call(
        functools.partial(to_blocks_body, offsets),
        in_specs=[pl.BlockSpec(memory_space=pltpu.SMEM)]
        + [pl.BlockSpec(memory_space=pl.ANY)] * len(parts),
        out_shape=like(16, 8, width),
        scratch_shapes=[pltpu.VMEM((96, part.shape[1]), BF) for part in parts]
        + [pltpu.VMEM((104, width), F32), pltpu.SemaphoreType.DMA((len(parts),))],
        compiler_params=pltpu.CompilerParams(vmem_limit_bytes=60 * MIB),
        cost_estimate=SMALL,
    )(place, *parts)


def from_blocks_body(in_ref, qkv_ref, out_ref, small_ref):
    total = in_ref[0].astype(F32)
    for k in range(1, 16):
        total = total + in_ref[k].astype(F32)
    out_ref[...] = total[:6, :D]
    for part in range(3):
        qkv_ref[:, part * D : part * D + 512] = total[:6, 896 + part * 512 : 1408 + part * 512]
        qkv_ref[:, part * D + 512 : (part + 1) * D] = total[:6, 2432 + part * 256 : 2688 + part * 256]
    small_ref[...] = total[:6, D : D + 128] + total[:6, 3200:3328]


def from_blocks(blocks):
    return pl.pallas_call(
        from_blocks_body,
        out_shape=[like(6, 3 * D, dtype=F32), like(6, D, dtype=F32), like(6, 128, dtype=F32)],
        compiler_params=pltpu.CompilerParams(vmem_limit_bytes=16 * MIB),
        cost_estimate=SMALL,
    )(blocks)


def prepare_body(core_ref, *refs):
    sources, (block_ref, mine_ref, other_ref) = refs[:9], refs[9:12]
    held, turned, wide, sems = refs[12:21], *refs[21:]
    loads = begin(sems, 0, *zip(sources, held))
    qkv_ref, out_ref, router_ref, gains_ref, biases_ref, up_t, down_t, up_f, down_f = held
    finish(loads[:5])
    wide[...] = jnp.zeros(wide.shape, F32)
    wide[0:6, : 3 * D] = qkv_ref[...]
    wide[0:6, 3 * D : FF] = out_ref[...]
    turned[...] = jnp.zeros((128, 128), F32)
    turned[16:18, 0:6] = gains_ref[...]
    turned[18:20, 0:6] = biases_ref[...]
    vectors = jnp.transpose(turned[...])[0:8]
    turned[0:6, 0:16] = router_ref[...]
    keep = iota((8, 128), 1) < 16
    small = jnp.where(keep, turned[0:8, :], vectors)
    small = jnp.where(iota((8, 128), 0) < 6, small, 0.0)
    wide[:, FF:] = small
    block_ref[...] = wide[...].astype(BF)
    trained = core_ref[0] == 0
    finish(loads[5:])
    for j in range(4):
        cols, rows = slice(j * D, (j + 1) * D), slice(j * 48, (j + 1) * 48)
        low, fixed = up_t[0, :, cols].astype(BF), up_f[0, :, cols]
        mine_ref[rows, :] = jnp.where(trained, low, fixed)
        other_ref[rows, :] = jnp.where(trained, fixed, low)
    low = down_t[0].astype(BF)
    mine_ref[192:, :] = jnp.where(trained, low, down_f[0])
    other_ref[192:, :] = jnp.where(trained, down_f[0], low)


def prepare(core, *arrays):
    anywhere = pl.BlockSpec(memory_space=pl.ANY)
    return pl.pallas_call(
        prepare_body,
        in_specs=[pl.BlockSpec(memory_space=pltpu.SMEM)] + [anywhere] * 9,
        out_shape=[like(8, FF + 128), like(384, D), like(384, D)],
        scratch_shapes=[pltpu.VMEM(array.shape, array.dtype) for array in arrays]
        + [pltpu.VMEM((128, 128), F32), pltpu.VMEM((8, FF + 128), F32)]
        + [pltpu.SemaphoreType.DMA((9,))],
        compiler_params=pltpu.CompilerParams(vmem_limit_bytes=60 * MIB),
        cost_estimate=SMALL,
    )(core, *arrays)


def pack_body(core_ref, mine_in, got_in, to_ref, sems):
    pairs = []
    for source, core in ((mine_in, core_ref[0]), (got_in, 1 - core_ref[0])):
        for j in range(4):
            rows = pl.ds(j * 96 + core * 48, 48)
            pairs.append((source.at[pl.ds(j * 48, 48), :], to_ref.at[rows, :]))
        pairs.append((source.at[pl.ds(192, 192), :], to_ref.at[pl.ds(384 + core * 192, 192), :]))
    finish(begin(sems, 0, *pairs))


def pack(core, mine, got):
    anywhere = pl.BlockSpec(memory_space=pl.ANY)
    return pl.pallas_call(
        pack_body,
        in_specs=[pl.BlockSpec(memory_space=pltpu.SMEM)] + [anywhere] * 2,
        out_shape=like(D, D),
        scratch_shapes=[pltpu.SemaphoreType.DMA((10,))],
        compiler_params=pltpu.CompilerParams(vmem_limit_bytes=16 * MIB),
        cost_estimate=SMALL,
    )(core, mine, got)


def shift(value, axis, by):
    count = lax.axis_size(axis)
    return lax.ppermute(value, axis, [(i, (i + by) % count) for i in range(count)])


def ordered(mine, other, index):
    first = jnp.where(index == 0, mine, other)
    second = jnp.where(index == 0, other, mine)
    return first, second


FAR = ("x", "yh", "yl")
PEERS = ("c", "z", "yl")


def to_all(rows, names):
    return lax.all_to_all(rows, names, split_axis=0, concat_axis=0, tiled=True)


def spread_x(block):
    return jnp.stack([block] + [shift(block, "x", step) for step in (1, 2, 3)])


def spread_y(along_x):
    near = [along_x] + [shift(along_x, ("yh", "yl"), step) for step in (1, 2, 3)]
    return jnp.stack(near)[:, :, :6].reshape(96, along_x.shape[2])


def natural_rows():
    x, c, z = (lax.axis_index(name) for name in ("x", "c", "z"))
    y = lax.axis_index("yh") * 2 + lax.axis_index("yl")
    row = jnp.arange(768)
    step, other, i = row // 192, (row // 96) % 2, row % 96
    core, deep = (c + other) % 2, (z - step) % 4
    high, long = (y - i // 24) % 4, (x - (i // 6) % 4) % 4
    device = ((long * 2 + high // 2) * 2 + core) * 8 + deep * 2 + high % 2
    return (device * 6 + i % 6).astype(jnp.int32)


def step_of(keep, got, step):
    rows = slice(step * 96, (step + 1) * 96)
    return (keep[rows].astype(F32) + got[rows].astype(F32)).astype(BF)


def along_z(keep, got):
    return [shift(step_of(keep, got, step), "z", -step) for step in (1, 2, 3)]


def take_body(core_ref, *refs):
    sources, (to_ref, *held), sems = refs[1:3], refs[3:6], refs[6]
    rows = held[0].shape[0]

    @pl.when(core_ref[0] == 1)
    def _():
        targets = [to_ref.at[pl.ds(at, rows), :] for at in (0, rows)]
        loads, stores = begin(sems, 0, *zip(sources, held)), []
        for i in range(2):
            finish(loads[i : i + 1])
            stores += begin(sems, 2 + i, (held[i], targets[i]))
        finish(stores)


def take(core, kept, *sent):
    got = [lax.ppermute(part, "c", [(0, 1)]) for part in sent]
    anywhere = pl.BlockSpec(memory_space=pl.ANY)
    return pl.pallas_call(
        take_body,
        in_specs=[pl.BlockSpec(memory_space=pltpu.SMEM)] + [anywhere] * 3,
        out_specs=anywhere,
        out_shape=like(*kept.shape),
        input_output_aliases={1: 0},
        scratch_shapes=[pltpu.VMEM(part.shape, part.dtype) for part in got]
        + [pltpu.SemaphoreType.DMA((4,))],
        compiler_params=pltpu.CompilerParams(vmem_limit_bytes=62 * MIB),
        cost_estimate=SMALL,
    )(core, kept, *got)


def over_y(mine):
    y = lax.axis_index("yh")
    parts = mine.reshape(2, mine.shape[0] // 2, mine.shape[1])
    kept, sent = (lax.dynamic_index_in_dim(parts, at, 0, False) for at in (y, 1 - y))
    return kept.astype(F32) + shift(sent, "yh", 1).astype(F32)


def owned(mine, axis):
    return lax.psum_scatter(mine, axis, scatter_dimension=0, tiled=True)


def shards(
    tokens,
    seq_lengths,
    key_mask,
    routes,
    cotangent,
    qkv_weight,
    out_weight,
    router_weight,
    norm_gains,
    norm_biases,
    up_train,
    down_train,
    up_frozen,
    down_frozen,
):
    core = lax.axis_index("c")

    place = jnp.stack([lax.axis_index(name) for name in ("x", "yh", "yl")]).astype(jnp.int32)

    block, mine, other = prepare(
        core.reshape(1), qkv_weight, out_weight, router_weight, norm_gains, norm_biases, up_train,
        down_train, up_frozen, down_frozen,
    )
    other = shift(other, "c", 1)
    block, routes, other = lax.optimization_barrier((block, routes, other))
    along_x = spread_x(block)

    both = pack(core.reshape(1), mine, other)
    along_x, both = lax.optimization_barrier((along_x, both))
    rows = spread_y(along_x)
    nat = natural_rows().reshape(1, D)
    g_slots, sid, sidt = route(routes, cotangent)
    near = lax.all_gather(both, "x", tiled=True)

    rows, g_slots, both = lax.optimization_barrier((rows, g_slots, both))
    parts = [rows] + [shift(rows, "z", step) for step in (1, 2, 3)]
    both = shift(both, "yh", 1)
    parts, both, g_slots = lax.optimization_barrier((parts, both, g_slots))
    pieces = []
    for part in parts:
        pieces += [part, shift(part, "c", 1)]
    far = lax.all_gather(both, "x", tiled=True)

    g_rows = to_all(g_slots.reshape(16, CAP, D), PEERS)
    w, h1p, qkv, probs, attnp, x_mid, h2, turn, gate, vec, router, sent = forward(
        seq_lengths[0], nat, key_mask.reshape(1, ROW), tokens, sid, sidt, pieces
    )
    sent, g_rows = lax.optimization_barrier((sent, g_rows))

    arrived = to_all(sent, PEERS)
    out, back, x_rows, d_out, act, d_up = experts(
        place, arrived, g_rows, near, far
    )
    d_back = to_all(back, PEERS)
    up_all = take(core.reshape(1), *up_grad(x_rows, d_up))
    down_parts = down_grad(d_out, act)
    d_back, out, up_all, down_parts = lax.optimization_barrier((d_back, out, up_all, down_parts))

    returned = to_all(out, PEERS)
    up_all, down_all = owned(up_all, "x"), take(core.reshape(1), *down_parts)
    d_x_mid, d_attn, first, keep, away = back_one(
        sid, gate, router, vec, d_back, x_mid, cotangent, w, attnp, h2, probs, qkv, h1p, turn
    )
    input_grad, *last = back_two(vec, d_attn, probs, qkv, h1p, first, w, tokens, d_x_mid, turn)
    got = shift(away, "c", 1)
    keep, got, returned, down_all = lax.optimization_barrier((keep, got, returned, down_all))
    down_all = owned(down_all, "x")
    one, two, three = (step_of(keep, got, step) for step in (1, 2, 3))
    one, three = shift(one, "z", -1), shift(three, "z", -3)
    two = [shift(half, "z", -2) for half in (two[:, :1280], two[:, 1280:])]
    one, three, two[0], last, up_all = lax.optimization_barrier((one, three, two[0], last, up_all))
    groups = [(0, keep), (0, got), (0, one), (0, three), (0, two[0]), (1280, two[1])]
    up_all = over_y(up_all)
    keep, got = last[0], shift(last[1], "c", 1)
    groups += [(2432, part) for part in (keep, got, *along_z(keep, got))]
    offsets, parts = zip(*groups)
    parts, down_all, up_all = lax.optimization_barrier((parts, down_all, up_all))
    down_all = owned(down_all, "yh")
    blocks = to_blocks(place, list(zip(offsets, parts)))
    blocks, returned = lax.optimization_barrier((blocks, returned))
    grad_down = down_all.astype(F32)[None]
    blocks, grad_down = lax.optimization_barrier((to_all(blocks, FAR), grad_down))
    own_qkv, own_out, small = from_blocks(blocks)
    grad_up = up_all.astype(F32)[None]
    block_out = merge(sid, returned.reshape(16 * CAP, D), gate, x_mid)
    return (
        block_out,
        input_grad,
        own_qkv,
        own_out,
        small[:, :16],
        small[:, 16:18].T,
        small[:, 18:20].T,
        grad_up,
        grad_down,
    )


def solution(mesh):
    fine = Mesh(mesh.devices.reshape(SIZES), NAMES)
    by_row = P(NAMES, None)
    by_column = P(None, NAMES)
    by_expert = P(NARROW, WIDE, None)
    return jax.shard_map(
        shards,
        mesh=fine,
        in_specs=(by_row, by_row, P(NAMES)) + (by_row,) * 5 + (by_column,) * 2 + (by_expert,) * 4,
        out_specs=(by_row,) * 5 + (by_column,) * 2 + (by_expert,) * 2,
        check_vma=False,
    )
```
